128 devices in a mesh: dp: 16 (over z, y), vocab: 8 (over x, core).
Axes of the slice: x: 4, y: 4, z: 4, core: 2. Of those that a mesh axis runs over, the one named last changes fastest.
Arguments:
- tokens: int32 [16, 256], P('dp'), may hold values from 0 to 51199
- segments: int32 [16, 256], P('dp'), may hold values from 0 to 4, as said below
- valid: int32 [16, 256], P('dp'), may hold values from 0 to 1, as said below
- embedding: bfloat16 [51200, 1024], P('vocab')
- positions_table: bfloat16 [256, 1024], replicated, may hold values from -0.59765625 to 0.59765625
- w_qkv: bfloat16 [1, 1024, 3072], replicated, may hold values from -0.1875 to 0.1875
- w_attn_out: bfloat16 [1, 1024, 1024], replicated, may hold values from -0.5 to 0.5
- w_fc: bfloat16 [1, 1024, 4096], replicated, may hold values from -0.1875 to 0.1875
- w_fc_out: bfloat16 [1, 4096, 1024], replicated, may hold values from -0.09375 to 0.09375
- layer_bias: bfloat16 [1, 9216], replicated, may hold values from -0.59765625 to 0.59765625
- norm_params: float32 [3, 2, 1024], replicated
- prefix: float32 [10, 512], P(None, 'dp'), may hold values from -1.2 to 1.2
- prefix_in: float32 [512, 512], P(None, 'dp'), may hold values from -0.25 to 0.25
- prefix_out: float32 [512, 2048], P(None, 'dp'), may hold values from -0.25 to 0.25
- prefix_bias: float32 [2560], P('dp'), may hold values from -1.2 to 1.2
- moment_prefix: float32 [10, 512], P(None, 'dp')
- moment_in: float32 [512, 512], P(None, 'dp')
- moment_out: float32 [512, 2048], P(None, 'dp')
- moment_bias: float32 [2560], P('dp')
- square_prefix: float32 [10, 512], P(None, 'dp')
- square_in: float32 [512, 512], P(None, 'dp')
- square_out: float32 [512, 2048], P(None, 'dp')
- square_bias: float32 [2560], P('dp')
Outputs:
- loss_sum: float32 [], replicated
- valid_count: float32 [], replicated
- grad_norm: float32 [], replicated
- new_prefix: float32 [10, 512], P(None, 'dp')
- new_in: float32 [512, 512], P(None, 'dp')
- new_out: float32 [512, 2048], P(None, 'dp')
- new_bias: float32 [2560], P('dp')
- first_prefix: float32 [10, 512], P(None, 'dp')
- first_in: float32 [512, 512], P(None, 'dp')
- first_out: float32 [512, 2048], P(None, 'dp')
- first_bias: float32 [2560], P('dp')
- second_prefix: float32 [10, 512], P(None, 'dp')
- second_in: float32 [512, 512], P(None, 'dp')
- second_out: float32 [512, 2048], P(None, 'dp')
- second_bias: float32 [2560], P('dp')
The draws below stay inside these ranges and needn't reach their ends.
Inputs may be any that keep to these rules, and one draw needn't show every extreme that they name: `segments`: along each row the number never falls, starts at 0 at the first two positions and ends at 4. `valid`: the first position of every row is 1.
All inputs are finite; a program needn't handle non-finite values.
Results may differ from the reference program's by a relative error of at most 0.024.
Values may be sent and summed in bfloat16 or wider, within the bound.
No kernel may reach another device: no remote copies, remote signals or barrier semaphores. Data moves between devices by JAX's collectives and lax.ppermute only.
A program may use at most 192 MiB of HBM per device.

```python
import math
import jax
import jax.numpy as jnp
import numpy as np
from jax import lax

D = 1024
HEADS = 16
HEAD_DIM = 64
FF = 4096
VOCAB = 51200
PREFIX = 10
PEMB = 512
PHID = 512
LAYERS = 1
LENGTH = 256
STEP = 10
ROWS = 16
NCUT = 4
KVW = 2048


CLIP = 0.001


def grad_size():
    total = PREFIX * PEMB + PEMB * PHID + PHID * 2 * LAYERS * D + PHID + 2 * LAYERS * D
    return CLIP / math.sqrt(total)


def first_moment(key, shape):
    return 0.111 * grad_size() * jax.random.normal(key, shape, jnp.float32)


def second_moment(key, shape):
    base = 0.001001 * grad_size() * grad_size()
    spread = jax.random.uniform(key, shape, jnp.float32, math.log(0.5), math.log(8.0))
    return base * jnp.exp(spread)


def draw_segments(key, part):
    key = jax.random.fold_in(key, 11)
    row_keys = jax.random.split(key, ROWS)

    def one(row_key):
        cuts = jax.random.permutation(row_key, LENGTH - 2)[:NCUT] + 2
        places = jnp.arange(LENGTH)
        return jnp.sum((cuts[None, :] <= places[:, None]).astype(jnp.int32), 1)
    return jax.vmap(one)(row_keys).astype(jnp.int32)


def draw_valid(key, part):
    key = jax.random.fold_in(key, 12)
    rows = jnp.arange(ROWS)[:, None]
    places = jnp.arange(LENGTH)[None, :]
    ticket = jax.random.randint(key, (ROWS, LENGTH), 0, 3 * ROWS)
    keep = (ticket < ROWS + 2 * rows) | (places == 0)
    return keep.astype(jnp.int32)


def draw_embedding(key, part):
    key = jax.random.fold_in(key, 13)
    rows = jnp.arange(VOCAB, dtype=jnp.float32)[:, None] / VOCAB
    base = jax.random.normal(key, (VOCAB, D), jnp.float32)
    rise = 1.0 + 2.0 * rows
    return (base * rise / math.sqrt(D)).astype(jnp.bfloat16)


def draw_norm_params(key, part):
    key = jax.random.fold_in(key, 14)
    noise = jax.random.normal(key, (2 * LAYERS + 1, 2, D), jnp.float32)
    gains = 1.0 + 0.1 * noise[:, 0]
    shifts = 0.2 * noise[:, 1]
    return jnp.stack([gains, shifts], 1)


def draw_moment_prefix(key, part):
    return first_moment(jax.random.fold_in(key, 21), (PREFIX, PEMB))


def draw_moment_in(key, part):
    return first_moment(jax.random.fold_in(key, 22), (PEMB, PHID))


def draw_moment_out(key, part):
    return first_moment(jax.random.fold_in(key, 23), (PHID, KVW))


def draw_moment_bias(key, part):
    return first_moment(jax.random.fold_in(key, 24), (PHID + KVW,))


def draw_square_prefix(key, part):
    return second_moment(jax.random.fold_in(key, 31), (PREFIX, PEMB))


def draw_square_in(key, part):
    return second_moment(jax.random.fold_in(key, 32), (PEMB, PHID))


def draw_square_out(key, part):
    return second_moment(jax.random.fold_in(key, 33), (PHID, KVW))


def draw_square_bias(key, part):
    return second_moment(jax.random.fold_in(key, 34), (PHID + KVW,))


def plant(values, own_key, smallest, high):
    shape = values.shape
    index_at = [jax.random.randint(jax.random.fold_in(own_key, axis), (), 0, shape[axis]) for axis in range(len(shape))]
    values = values.at[tuple(index_at)].set(smallest)
    longest = shape.index(max(shape))
    index_at[longest] = (index_at[longest] + 1) % shape[longest]
    return values.at[tuple(index_at)].set(high)


def block_scale(rng, shape, shards, smallest, top_value):
    def one(position, shards_of):
        draws = jax.random.uniform(jax.random.fold_in(jax.random.fold_in(rng, 6), position), (shards_of,), jnp.float32, smallest / len(shards), top_value / len(shards))
        return jnp.repeat(jnp.exp(draws), shape[position] // shards_of).reshape((-1,) + (1,) * (len(shape) - position - 1))

    factor_of = one(*shards[0])
    for cut in shards[1:]:
        factor_of = factor_of * one(*cut)
    return factor_of


def cumulative_ranks(count, lean):
    portions = [(1 << 20) // math.isqrt(standing ** lean) + 1 for standing in range(1, count + 1)]
    deviation = 1 + sum(portions) // (1 << 30)
    return np.cumsum(np.array([max(1, weight // deviation) for weight in portions]))


def ranked(stream_key, dims, count, skew):
    listing = cumulative_ranks(count, skew)
    pick = jax.random.randint(jax.random.fold_in(stream_key, 1), dims, 0, int(listing[count - 1]))
    grade = jnp.searchsorted(jnp.asarray(listing, jnp.int32), pick, side="right")
    return jax.random.permutation(jax.random.fold_in(stream_key, 2), count)[grade].astype(jnp.int32)


def scatter_about(rng, dims, scale, bound, pieces=(), held_as=jnp.bfloat16):
    array = scale * jax.random.normal(rng, dims, jnp.float32)
    if pieces:
        array = array * block_scale(rng, dims, pieces, -0.22, 0.18)
    return jnp.clip(array, -bound, bound).astype(held_as)


def setup_inputs(seed: int = 0) -> dict:
    arg_keys = jax.random.split(jax.random.key(seed), 24)
    tokens = plant(ranked(arg_keys[0], (ROWS, LENGTH), VOCAB, 1), jax.random.fold_in(arg_keys[0], 3), 0, VOCAB - 1).astype(jnp.int32)
    segments = draw_segments(jax.random.fold_in(arg_keys[23], 71), 0)
    valid = draw_valid(jax.random.fold_in(arg_keys[23], 71), 0)
    embedding = draw_embedding(jax.random.fold_in(arg_keys[23], 71), 0)
    positions_table = scatter_about(arg_keys[4], (LENGTH, D), 0.1, 0.59765625)
    w_qkv = scatter_about(arg_keys[5], (LAYERS, D, 3 * D), D ** -0.5, 0.1875)
    w_attn_out = scatter_about(arg_keys[6], (LAYERS, D, D), (D // 8) ** -0.5, 0.5)
    w_fc = scatter_about(arg_keys[7], (LAYERS, D, FF), D ** -0.5, 0.1875)
    w_fc_out = scatter_about(arg_keys[8], (LAYERS, FF, D), FF ** -0.5, 0.09375)
    layer_bias = scatter_about(arg_keys[9], (LAYERS, 5 * D + FF), 0.1, 0.59765625)
    norm_params = draw_norm_params(jax.random.fold_in(arg_keys[23], 71), 0)
    prefix = scatter_about(arg_keys[11], (PREFIX, PEMB), 0.2, 1.2, ((1, 16),), jnp.float32)
    prefix_in = scatter_about(arg_keys[12], (PEMB, PHID), PEMB ** -0.5, 0.25, ((1, 16),), jnp.float32)
    prefix_out = scatter_about(arg_keys[13], (PHID, KVW), PHID ** -0.5, 0.25, ((1, 16),), jnp.float32)
    prefix_bias = scatter_about(arg_keys[14], (PHID + KVW,), 0.2, 1.2, ((0, 16),), jnp.float32)
    moment_prefix = draw_moment_prefix(jax.random.fold_in(arg_keys[23], 71), 0)
    moment_in = draw_moment_in(jax.random.fold_in(arg_keys[23], 71), 0)
    moment_out = draw_moment_out(jax.random.fold_in(arg_keys[23], 71), 0)
    moment_bias = draw_moment_bias(jax.random.fold_in(arg_keys[23], 71), 0)
    square_prefix = draw_square_prefix(jax.random.fold_in(arg_keys[23], 71), 0)
    square_in = draw_square_in(jax.random.fold_in(arg_keys[23], 71), 0)
    square_out = draw_square_out(jax.random.fold_in(arg_keys[23], 71), 0)
    square_bias = draw_square_bias(jax.random.fold_in(arg_keys[23], 71), 0)
    return dict(tokens=tokens, segments=segments, valid=valid, embedding=embedding, positions_table=positions_table, w_qkv=w_qkv, w_attn_out=w_attn_out, w_fc=w_fc, w_fc_out=w_fc_out, layer_bias=layer_bias, norm_params=norm_params, prefix=prefix, prefix_in=prefix_in, prefix_out=prefix_out, prefix_bias=prefix_bias, moment_prefix=moment_prefix, moment_in=moment_in, moment_out=moment_out, moment_bias=moment_bias, square_prefix=square_prefix, square_in=square_in, square_out=square_out, square_bias=square_bias)


@jax.custom_vjp
def low(v):
    return lax.optimization_barrier(v.astype(jnp.bfloat16)).astype(jnp.float32)

@jax.custom_vjp
def low_back(v):
    return v

def low_keep(v):
    return (low(v), None)

def low_pass(kept, grad):
    return (grad,)

def back_keep(v):
    return (v, None)

def back_low(kept, grad):
    return (low(grad),)
low.defvjp(low_keep, low_pass)
low_back.defvjp(back_keep, back_low)
HIGH = lax.Precision.HIGHEST
NORM_EPS = 1e-05
BETA_ONE = 0.9
BETA_TWO = 0.999
ADAM_EPS = 1e-08
RATE = 0.1
DECAY = 0.01
CLIP = 0.001
MASKED = -1e+30

def layer_norm(value, gain, shift):
    mean = lax.optimization_barrier(jnp.mean(value, axis=-1, keepdims=True))
    centred = value - mean
    spread = lax.optimization_barrier(jnp.mean(centred * centred, axis=-1, keepdims=True))
    return centred * lax.rsqrt(spread + NORM_EPS) * gain + shift

def gelu(value):
    return jax.nn.gelu(value, approximate=True)

def prefix_states(prefix, prefix_in, prefix_out, prefix_bias):
    hidden = jnp.tanh(jnp.dot(prefix, prefix_in, precision=HIGH) + prefix_bias[:PHID])
    return jnp.dot(hidden, prefix_out, precision=HIGH) + prefix_bias[PHID:]

def counted_of(segments, valid):
    places = jnp.arange(LENGTH)
    next_segments = jnp.concatenate([segments[1:], segments[:1]])
    keep = (valid > 0) & (places < LENGTH - 1) & (next_segments == segments)
    return keep.astype(jnp.float32)

def block(x, layer, states, visible, frozen):
    w_qkv, w_attn_out, w_fc, w_fc_out, layer_bias, norm_params = frozen
    bias = layer_bias[layer]
    rows = x.shape[0]
    normed = low(layer_norm(x, norm_params[2 * layer, 0], norm_params[2 * layer, 1]))
    qkv = low(low_back(jnp.dot(normed, w_qkv[layer], precision=HIGH) + bias[:3 * D]))
    query = qkv[:, :D].reshape(rows, HEADS, HEAD_DIM)
    keys = jnp.concatenate([low(states[:, layer, 0]).reshape(PREFIX, HEADS, HEAD_DIM), qkv[:, D:2 * D].reshape(rows, HEADS, HEAD_DIM)], 0)
    values = jnp.concatenate([low(states[:, layer, 1]).reshape(PREFIX, HEADS, HEAD_DIM), qkv[:, 2 * D:].reshape(rows, HEADS, HEAD_DIM)], 0)
    scores = low_back(HEAD_DIM ** (-0.5) * jnp.einsum('qhd,khd->hqk', query, keys, precision=HIGH))
    scores = jnp.where(visible[None], scores, MASKED)
    top = lax.optimization_barrier(jnp.max(scores, axis=-1, keepdims=True))
    expo = jnp.exp(scores - top)
    probs = low(expo / lax.optimization_barrier(jnp.sum(expo, axis=-1, keepdims=True)))
    mixed = jnp.einsum('hqk,khd->qhd', probs, values, precision=HIGH).reshape(rows, D)
    mixed = low(low_back(mixed))
    attended = x + low_back(jnp.dot(mixed, w_attn_out[layer], precision=HIGH) + bias[3 * D:4 * D])
    normed_two = low(layer_norm(attended, norm_params[2 * layer + 1, 0], norm_params[2 * layer + 1, 1]))
    inner = low_back(jnp.dot(normed_two, w_fc[layer], precision=HIGH) + bias[4 * D:4 * D + FF])
    active = low(gelu(inner))
    return attended + low_back(jnp.dot(active, w_fc_out[layer], precision=HIGH) + bias[4 * D + FF:])

def row_loss(states, tokens, segments, valid, frozen, table, positions):
    norm_params = frozen[5]
    places = jnp.arange(LENGTH)
    same = (segments[None, :] == segments[:, None]) & (places[None, :] <= places[:, None])
    visible = jnp.concatenate([jnp.ones((LENGTH, PREFIX), bool), same], 1)
    x = table[tokens] + positions
    for layer in range(LAYERS):
        x = block(x, layer, states, visible, frozen)
    final = low(layer_norm(x, norm_params[2 * LAYERS, 0], norm_params[2 * LAYERS, 1]))
    logits = low_back(jnp.dot(final, table.T, precision=HIGH))
    top = lax.optimization_barrier(jnp.max(logits, axis=-1, keepdims=True))
    log_total = top[:, 0] + jnp.log(lax.optimization_barrier(jnp.sum(jnp.exp(logits - top), axis=-1)))
    target = jnp.concatenate([tokens[1:], tokens[:1]]).astype(jnp.int32)
    picked = jnp.take_along_axis(logits, target[:, None], axis=1)[:, 0]
    return jnp.sum((log_total - picked) * counted_of(segments, valid))

def adam(weight, grad, first, second):
    first = BETA_ONE * first + (1.0 - BETA_ONE) * grad
    second = BETA_TWO * second + (1.0 - BETA_TWO) * grad * grad
    move = first / (1.0 - BETA_ONE ** STEP) / (jnp.sqrt(second / (1.0 - BETA_TWO ** STEP)) + ADAM_EPS)
    return (weight - RATE * (move + DECAY * weight), first, second)

def reference(tokens, segments, valid, embedding, positions_table, w_qkv, w_attn_out, w_fc, w_fc_out, layer_bias, norm_params, prefix, prefix_in, prefix_out, prefix_bias, moment_prefix, moment_in, moment_out, moment_bias, square_prefix, square_in, square_out, square_bias):
    frozen = (w_qkv.astype(jnp.float32), w_attn_out.astype(jnp.float32), w_fc.astype(jnp.float32), w_fc_out.astype(jnp.float32), layer_bias.astype(jnp.float32), norm_params)
    table = embedding.astype(jnp.float32)
    positions = positions_table.astype(jnp.float32)
    count = jnp.sum(jax.vmap(counted_of)(segments, valid))

    def total(p_emb, p_in, p_out, p_bias):
        states = prefix_states(p_emb, p_in, p_out, p_bias).reshape(PREFIX, LAYERS, 2, D)

        def one(row):
            return row_loss(states, row[0], row[1], row[2], frozen, table, positions)
        sums = lax.map(jax.checkpoint(one), (tokens, segments, valid))
        loss_sum = jnp.sum(sums)
        return (loss_sum / count, loss_sum)
    loss, pullback, loss_sum = jax.vjp(total, prefix, prefix_in, prefix_out, prefix_bias, has_aux=True)
    grads = pullback(jnp.ones_like(loss))
    norm = jnp.sqrt(sum((jnp.sum(g * g) for g in grads)))
    factor = jnp.minimum(1.0, CLIP / (norm + 1e-06))
    weights = (prefix, prefix_in, prefix_out, prefix_bias)
    firsts = (moment_prefix, moment_in, moment_out, moment_bias)
    seconds = (square_prefix, square_in, square_out, square_bias)
    result = [adam(w, g * factor, m, v) for w, g, m, v in zip(weights, grads, firsts, seconds)]
    return (loss_sum, count, norm, result[0][0], result[1][0], result[2][0], result[3][0], result[0][1], result[1][1], result[2][1], result[3][1], result[0][2], result[1][2], result[2][2], result[3][2])
```

```python
import jax
import jax.numpy as jnp
from jax import lax
from jax.experimental import pallas as pl
from jax.experimental.pallas import tpu as pltpu
from jax.sharding import Mesh
from jax.sharding import PartitionSpec as P

D = 1024
HEADS = 16
HEAD_DIM = 64
FF = 4096
VOCAB = 51200
PREFIX = 10
PHID = 512
LENGTH = 256
STEP = 10
KVW = 2048
HALF = 128
PART = 32
SHARD = VOCAB // 8
PRE = 16
EXT = D + 128
FLAT = KVW + 768

NORM_EPS = 1e-05
BETA_ONE = 0.9
BETA_TWO = 0.999
ADAM_EPS = 1e-08
RATE = 0.1
DECAY = 0.01
CLIP = 0.001
MASKED = -1e30
SCALE = HEAD_DIM**-0.5
GELU_K = 0.7978845608028654
GELU_C = 0.044715

HIGH = lax.Precision.HIGHEST
F32 = jnp.float32
BF16 = jnp.bfloat16
MIB = 1 << 20

WHOLE = pl.BlockSpec(memory_space=pltpu.VMEM)
SCALARS = pl.BlockSpec(memory_space=pltpu.SMEM)
REMAIN = pl.BlockSpec(memory_space=pl.ANY)


def nn(a, b, precision=None):
    return lax.dot_general(a, b, (((1,), (0,)), ((), ())), precision=precision, preferred_element_type=F32)


def nt(a, b, precision=None):
    return lax.dot_general(a, b, (((1,), (1,)), ((), ())), precision=precision, preferred_element_type=F32)


def tn(a, b, precision=None):
    return lax.dot_general(a, b, (((0,), (0,)), ((), ())), precision=precision, preferred_element_type=F32)


def lanes(shape):
    return lax.broadcasted_iota(jnp.int32, shape, len(shape) - 1)


def rows(shape):
    return lax.broadcasted_iota(jnp.int32, shape, 0)


def call(body, outs, ins, scratch=(), limit=48, name=None, flops=0, moved=0):
    return pl.pallas_call(
        body,
        out_shape=outs,
        in_specs=ins,
        out_specs=jax.tree.map(lambda _: WHOLE, outs),
        scratch_shapes=scratch,
        compiler_params=pltpu.CompilerParams(vmem_limit_bytes=limit * MIB),
        cost_estimate=pl.CostEstimate(flops=flops, bytes_accessed=moved, transcendentals=0),
        name=name,
    )


def shaped(shape, dtype=F32):
    return jax.ShapeDtypeStruct(shape, dtype)


def normalised(value):
    mean = jnp.mean(value, axis=-1, keepdims=True)
    centred = value - mean
    spread = jnp.mean(centred * centred, axis=-1, keepdims=True)
    inverse = lax.rsqrt(spread + NORM_EPS)
    return centred * inverse, inverse


def norm_back(value, gain, grad):
    unit, inverse = normalised(value)
    scaled = grad * gain
    first = jnp.mean(scaled, axis=-1, keepdims=True)
    second = jnp.mean(scaled * unit, axis=-1, keepdims=True)
    return inverse * (scaled - first - unit * second)


def three_way(value):
    high = value.astype(BF16).astype(F32)
    rest = value - high
    middle = rest.astype(BF16).astype(F32)
    return high, middle, rest - middle


def with_stat(body, stat):
    high, middle, low = three_way(stat)
    lane = lanes((body.shape[0], 128))
    tail = jnp.where(lane == 0, high, jnp.where(lane == 1, middle, jnp.where(lane == 2, low, 0.0)))
    return body.astype(BF16), tail.astype(BF16)


def stat_of(ref):
    tail = ref[:, D:EXT].astype(F32)
    return jnp.sum(jnp.where(lanes(tail.shape) < 3, tail, 0.0), axis=1, keepdims=True)


OWN = 96
SMALL = 16
PACK = OWN + SMALL
TALL = 4 * OWN + SMALL


def two_way(value):
    high = value.astype(BF16)
    return high, (value - high.astype(F32)).astype(BF16)


def pack_body(idx, weight_in, weight_out, weight, bias, segments, valid, out, small):
    core = idx[3]
    place = idx[0] * 4 + idx[1]
    own = (rows((32, PHID)) + place * 32 == lanes((32, PHID))).astype(F32)
    small[...] = jnp.zeros_like(small)
    small[0:PREFIX, :] = nn(weight[...], own, HIGH)
    spread = (rows((160, 5 * PHID)) + place * 160 == lanes((160, 5 * PHID))).astype(F32)
    flat = nn(bias[...], spread, HIGH)
    for r in range(5):
        small[PREFIX + r : PREFIX + r + 1, :] = flat[:, r * PHID : (r + 1) * PHID]
    seg = segments[...]
    after = jnp.concatenate([seg[:, 1:], seg[:, :1]], axis=1)
    kept = (valid[...] > 0) & (lanes(seg.shape) < LENGTH - 1) & (after == seg)
    total = jnp.sum(kept.astype(F32), axis=1, keepdims=True)
    small[15:16, :] = jnp.where(lanes((1, PHID)) == place, total, 0.0)
    high, low = two_way(small[...])

    @pl.when(core == 0)
    def _():
        first, second = two_way(weight_in[...])
        out[0:32, :] = first
        out[32:64, :] = second
        out[64:96, :] = jnp.transpose(weight_out[...])[0:32, :].astype(BF16)
        out[OWN:PACK, :] = high

    @pl.when(core == 1)
    def _():
        out[0:OWN, :] = jnp.transpose(weight_out[...])[32:128, :].astype(BF16)
        out[OWN:PACK, :] = low


def pack(idx, weight_in, weight_out, weight, bias, segments, valid):
    return call(
        pack_body,
        shaped((PACK, PHID), BF16),
        [SCALARS] + [WHOLE] * 6,
        (pltpu.VMEM((SMALL, PHID), F32),),
        limit=8,
        name="pack_prefix_weights",
        moved=500000,
    )(idx, weight_in, weight_out, weight, bias, segments, valid)


def stack_body(a, b, c, d, out):
    for k, ref in enumerate((a, b, c, d)):
        out[k * OWN : (k + 1) * OWN, :] = ref[0:OWN, :]
    small = sum((r[OWN:PACK, :].astype(F32) for r in (b, c, d)), a[OWN:PACK, :].astype(F32))
    out[4 * OWN : TALL, :] = small.astype(BF16)


def stack(pieces):
    return call(
        stack_body, shaped((TALL, PHID), BF16), [WHOLE] * 4, limit=8, name="stack_pieces", moved=800000
    )(*pieces)


def states_body(
    idx, a0, b0, c0, d0, a1, b1, c1, d1,
    in_high, in_low, out_t, weight, hidden, extra, states,
):
    z, y, core = idx[0], idx[1], idx[3]

    def unpack(first, second):
        for dz in range(4):
            for dy in range(4):
                place = lax.rem(z + 4 - dz, 4) * 4 + lax.rem(y + 4 - dy, 4)
                at = pl.ds(pl.multiple_of(place * 32, 32), 32)
                in_high[at, :] = first[dz][dy * OWN : dy * OWN + 32, :]
                in_low[at, :] = first[dz][dy * OWN + 32 : dy * OWN + 64, :]
                out_t[pl.ds(pl.multiple_of(place * 128, 32), 32), :] = first[dz][dy * OWN + 64 : dy * OWN + 96, :]
                out_t[pl.ds(pl.multiple_of(place * 128 + 32, 32), 96), :] = second[dz][dy * OWN : (dy + 1) * OWN, :]

    mine, theirs = (a0, b0, c0, d0), (a1, b1, c1, d1)
    pl.when(core == 0)(lambda: unpack(mine, theirs))
    pl.when(core == 1)(lambda: unpack(theirs, mine))
    rest = sum((r[4 * OWN : TALL, :].astype(F32) for r in (*mine[1:], *theirs)), mine[0][4 * OWN : TALL, :].astype(F32))
    live = rows((PRE, PHID)) < PREFIX
    whole = jnp.where(live, rest, 0.0)
    weight[...] = whole
    high, low = two_way(whole)
    pre = nt(high, in_high[...]) + nt(high, in_low[...]) + nt(low, in_high[...]) + rest[PREFIX : PREFIX + 1, :]
    hid = jnp.where(live, jnp.tanh(pre), 0.0)
    hidden[...] = hid
    flat = jnp.concatenate([rest[r : r + 1, :] for r in range(11, 15)], axis=1)
    count = jnp.sum(rest[15:16, :], axis=1, keepdims=True)
    extra[...] = jnp.broadcast_to(count, extra.shape)
    high, low = two_way(hid)
    out = nt(high, out_t[...]) + nt(low, out_t[...]) + flat
    states[...] = jnp.where(rows((PRE, KVW)) < PREFIX, out, 0.0).astype(BF16)


def prefix_states(idx, mine, theirs):
    return call(
        states_body,
        (
            shaped((PHID, PHID), BF16),
            shaped((PHID, PHID), BF16),
            shaped((KVW, PHID), BF16),
            shaped((PRE, PHID)),
            shaped((PRE, PHID)),
            shaped((1, 128)),
            shaped((PRE, KVW), BF16),
        ),
        [SCALARS] + [WHOLE] * 8,
        limit=12,
        name="prefix_states",
        moved=7000000,
    )(idx, *mine, *theirs)


def rows_body(idx, tokens, table, own, other, block, held, found, sems):
    first = (idx[2] * 2 + idx[3]) * SHARD

    def find(p, n):
        local = tokens[0, p] - first
        found[n] = p
        return n + ((local >= 0) & (local < SHARD)).astype(jnp.int32)

    number = lax.fori_loop(0, LENGTH, find, 0, unroll=16)

    def copy(n, local):
        at = pl.multiple_of((local // 16) * 16, 16)
        return pltpu.make_async_copy(table.at[pl.ds(at, 16), :], block.at[n], sems.at[n])

    def begin(n, carry):
        copy(n, tokens[0, found[n]] - first).start()
        return carry

    lax.fori_loop(0, number, begin, 0)
    held[...] = jnp.zeros_like(held)

    def take(n, carry):
        p = found[n]
        local = tokens[0, p] - first
        copy(n, local).wait()
        got = block[n].astype(F32)
        line = jnp.sum(jnp.where(rows((16, D)) == lax.rem(local, 16), got, 0.0), axis=0, keepdims=True)
        held[pl.ds(p, 1), :] = line
        return carry

    lax.fori_loop(0, number, take, 0)
    core = idx[3]
    own[...] = held[pl.ds(pl.multiple_of(core * HALF, HALF), HALF), :].astype(BF16)
    other[...] = held[pl.ds(pl.multiple_of((1 - core) * HALF, HALF), HALF), :].astype(BF16)


def token_rows(idx, tokens, table):
    return call(
        rows_body,
        (shaped((HALF, D), BF16), shaped((HALF, D), BF16)),
        [SCALARS, SCALARS, pl.BlockSpec(memory_space=pltpu.HBM)],
        (
            pltpu.VMEM((LENGTH, 16, D), BF16),
            pltpu.VMEM((LENGTH, D), F32),
            pltpu.SMEM((LENGTH,), jnp.int32),
            pltpu.SemaphoreType.DMA((LENGTH,)),
        ),
        limit=16,
        name="token_rows",
        moved=2000000,
    )(idx, tokens, table)


def qkv_body(idx, e0, e1, e2, e3, places, norms, bias, weight, x_out, embedded, query, keyval):
    core = idx[3]
    mine = e0[...].astype(F32) + e1[...].astype(F32) + e2[...].astype(F32) + e3[...].astype(F32)
    embedded[...] = mine.astype(BF16)
    x = mine + places[pl.ds(pl.multiple_of(core * HALF, HALF), HALF), :].astype(F32)
    x_out[...] = x
    unit, _ = normalised(x)
    normed = (unit * norms[0, 0:1, :] + norms[0, 1:2, :]).astype(BF16)
    for j in range(6):
        at = slice(j * 512, (j + 1) * 512)
        part = nn(normed, weight[0, :, at]) + bias[:, at].astype(F32)
        if j < 2:
            query[:, at] = (part.astype(BF16).astype(F32) * SCALE).astype(BF16)
        else:
            keyval[0:HALF, (j - 2) * 512 : (j - 1) * 512] = part.astype(BF16)
    keyval[HALF : HALF + 16, 0:D] = mine[0:16, :].astype(BF16)
    keyval[HALF : HALF + 16, D:KVW] = jnp.zeros((16, D), BF16)


def projections(idx, pieces, places, norms, bias, weight):
    return call(
        qkv_body,
        (
            shaped((HALF, D)),
            shaped((HALF, D), BF16),
            shaped((HALF, D), BF16),
            shaped((HALF + 16, KVW), BF16),
        ),
        [SCALARS] + [WHOLE] * 8,
        limit=10,
        name="norm_and_projections",
        flops=2 * HALF * D * 3 * D,
        moved=9000000,
    )(idx, *pieces, places, norms, bias, weight)


FCH = 1024


def layer_body(
    idx, query, kv_own, kv_other, embedded, x_in, prefix_kv, segments, valid, norms, bias,
    w_out, w_fc, w_fc_out,
    final, attended_part, last_part, inner_part, mixed_part, query_part, target_part, stats_part,
    mixed, log_sums, keep, wide,
):
    xx, core = idx[2], idx[3]
    part = pl.ds(pl.multiple_of(xx * PART, PART), PART)

    seg = segments[...]
    mine = jnp.where(core == 0, seg[:, 0:HALF], seg[:, HALF:LENGTH])
    theirs = jnp.where(core == 0, seg[:, HALF:LENGTH], seg[:, 0:HALF])
    square = (HALF, HALF)
    mine_down = jnp.transpose(jnp.broadcast_to(mine, square))
    sees_own = (mine_down == jnp.broadcast_to(mine, square)) & (lanes(square) <= rows(square))
    sees_other = (mine_down == jnp.broadcast_to(theirs, square)) & (core == 1)
    sees_prefix = lanes(square) < PREFIX
    hide = jnp.concatenate([jnp.where(m, 0.0, MASKED) for m in (sees_own, sees_other, sees_prefix)], axis=1)
    hide = jnp.concatenate([hide, hide], axis=0)
    left = lanes(square) < HEAD_DIM
    sums = jnp.zeros(square, F32)
    pad = jnp.zeros((HALF - PRE, HALF), BF16)
    for pair in range(HEADS // 2):
        at = slice(pair * 128, pair * 128 + 128)
        at_v = slice(D + pair * 128, D + pair * 128 + 128)
        q = query[:, at]
        zero = jnp.zeros_like(q)
        both = jnp.concatenate([jnp.where(left, q, zero), jnp.where(left, zero, q)], axis=0)
        keys = jnp.concatenate([kv_own[0:HALF, at], kv_other[0:HALF, at], prefix_kv[:, at], pad], axis=0)
        values = jnp.concatenate([kv_own[0:HALF, at_v], kv_other[0:HALF, at_v], prefix_kv[:, at_v], pad], axis=0)
        scores = nt(both, keys) + hide
        top = jnp.max(scores, axis=1, keepdims=True)
        expo = jnp.exp(scores - top)
        total = jnp.sum(expo, axis=1, keepdims=True)
        out = nn(expo.astype(BF16), values) * (1.0 / total)
        mixed[:, at] = jnp.where(left, out[0:HALF], out[HALF:])
        logs = top + jnp.log(total)
        sums = jnp.where(lanes(square) == 2 * pair, logs[0:HALF], sums)
        sums = jnp.where(lanes(square) == 2 * pair + 1, logs[HALF:], sums)
    log_sums[...] = sums
    mixed_part[...] = mixed[part, :]
    query_part[...] = query[part, :]

    x = x_in[...] + nn(mixed[...].astype(BF16), w_out[0]) + bias[:, 3 * D : 4 * D].astype(F32)
    keep[...] = x
    attended_part[...] = keep[part, :]
    unit, _ = normalised(x)
    normed = (unit * norms[1, 0:1, :] + norms[1, 1:2, :]).astype(BF16)
    x = x + bias[:, 4 * D + FF : 5 * D + FF].astype(F32)
    for j in range(4):
        inner = nn(normed, w_fc[0, :, j * FCH : (j + 1) * FCH]) + bias[:, 4 * D + j * FCH : 4 * D + (j + 1) * FCH].astype(F32)
        wide[...] = inner
        inner_part[:, j * FCH : (j + 1) * FCH] = wide[part, :]
        active = (0.5 * inner * (1.0 + jnp.tanh(GELU_K * (inner + GELU_C * inner * inner * inner)))).astype(BF16)
        x = x + nn(active, w_fc_out[0, j * FCH : (j + 1) * FCH, :])
    keep[...] = x
    last_part[...] = keep[part, :]
    unit, _ = normalised(x)
    result = (unit * norms[2, 0:1, :] + norms[2, 1:2, :]).astype(BF16)
    final[...] = result

    wide[...] = embedded[...].astype(F32)
    keep[...] = result.astype(F32)
    after = jnp.concatenate([wide[1:HALF, :], kv_other[HALF : HALF + 1, 0:D].astype(F32)], axis=0)
    wide[...] = after
    target = wide[part, :]
    target_part[...] = target
    picked = jnp.sum(keep[part, :] * target, axis=1, keepdims=True)
    following = jnp.concatenate([seg[:, 1:], seg[:, :1]], axis=1)
    kept = (valid[...] > 0) & (lanes(seg.shape) < LENGTH - 1) & (following == seg)
    kept = kept.astype(F32)
    counted = jnp.where(core == 0, kept[:, 0:HALF], kept[:, HALF:LENGTH])
    wide[:, 0:HALF] = jnp.transpose(jnp.broadcast_to(counted, square))
    lane = lanes((PART, 128))
    stats_part[:, 0:128] = log_sums[part, :]
    stats_part[:, 128:256] = jnp.where(lane == 0, picked, jnp.where(lane == 1, wide[part, 0:128], 0.0))


def layer(idx, query, kv_own, kv_other, embedded, x, states, segments, valid, norms, bias, w_out, w_fc, w_fc_out):
    return call(
        layer_body,
        (
            shaped((HALF, D), BF16),
            shaped((PART, D)),
            shaped((PART, D)),
            shaped((PART, FF)),
            shaped((PART, D)),
            shaped((PART, D), BF16),
            shaped((PART, D)),
            shaped((PART, 256)),
        ),
        [SCALARS] + [WHOLE] * 13,
        (
            pltpu.VMEM((HALF, D), F32),
            pltpu.VMEM((HALF, 128), F32),
            pltpu.VMEM((HALF, D), F32),
            pltpu.VMEM((HALF, FCH), F32),
        ),
        limit=10,
        name="attention_and_feed_forward",
        flops=2 * HALF * D * 9 * D,
        moved=22000000,
    )(idx, query, kv_own, kv_other, embedded, x, states, segments, valid, norms, bias, w_out, w_fc, w_fc_out)


VCH = 1280


def vocab_body(idx, f_own, f_other, table, o0, o1, o2, o3, final, log_sums, grad):
    final[0:HALF, :] = f_own[...]
    final[HALF:LENGTH, :] = f_other[...]
    for j in range(SHARD // VCH):
        chunk = table[j * VCH : (j + 1) * VCH, :]
        logits = nt(final[...], chunk)
        now = jnp.max(logits, axis=1, keepdims=True)
        if j:
            now = jnp.maximum(top, now)
            shrink = jnp.exp(top - now)
        expo = jnp.exp(logits - now)
        part = jnp.sum(expo, axis=1, keepdims=True)
        total = total * shrink + part if j else part
        part = nn(expo.astype(BF16), chunk)
        grad[...] = grad[...] * shrink + part if j else part
        top = now
    xx = idx[2]
    grad[...] = grad[...] * (1.0 / total)
    log_sums[...] = jnp.broadcast_to(top + jnp.log(total), log_sums.shape)
    for k, out in enumerate((o0, o1, o2, o3)):
        to = lax.rem(xx + k, 4) * PART
        for side in range(2):
            at = pl.ds(pl.multiple_of(side * HALF + to, PART), PART)
            body, tail = with_stat(grad[at, :], log_sums[at, 0:1])
            out[side * PART : (side + 1) * PART, 0:D] = body
            out[side * PART : (side + 1) * PART, D:EXT] = tail


def vocabulary(idx, f_own, f_other, table):
    return call(
        vocab_body,
        (shaped((2 * PART, EXT), BF16),) * 4,
        [SCALARS] + [WHOLE] * 3,
        (
            pltpu.VMEM((LENGTH, D), BF16),
            pltpu.VMEM((LENGTH, 128), F32),
            pltpu.VMEM((LENGTH, D), F32),
        ),
        limit=16,
        name="logits_and_gradient",
        flops=4 * LENGTH * D * SHARD,
        moved=SHARD * D * 2,
    )(idx, f_own, f_other, table)


def merged(refs):
    stats = [stat_of(r) for r in refs]
    top = stats[0]
    for s in stats[1:]:
        top = jnp.maximum(top, s)
    weights = [jnp.exp(s - top) for s in stats]
    total = sum(weights[1:], weights[0])
    mean = sum((w * r[:, 0:D].astype(F32) for w, r in zip(weights[1:], refs[1:])), weights[0] * refs[0][:, 0:D].astype(F32))
    return mean * (1.0 / total), top + jnp.log(total)


def merge_body(a, b, c, d, own, other):
    mean, log_total = merged((a, b, c, d))
    for out, at in ((own, slice(0, PART)), (other, slice(PART, 2 * PART))):
        body, tail = with_stat(mean[at, :], log_total[at, :])
        out[:, 0:D] = body
        out[:, D:EXT] = tail


def merge(pieces):
    one = shaped((PART, EXT), BF16)
    return call(merge_body, (one, one), [WHOLE] * 4, name="merge_partial_gradients", moved=800000)(*pieces)


def backward_body(
    own, other, attended, last, inner, mixed, query, target, stats, prefix_kv, norms, w_out, w_fc, w_fc_out,
    result,
):
    mean, log_total = merged((own, other))
    counted = stats[:, 129:130]
    loss = jnp.sum((log_total - stats[:, 128:129]) * counted, axis=0, keepdims=True)
    grad = (mean - target[...]) * counted
    grad_x = norm_back(last[...], norms[2, 0:1, :], grad)
    low = grad_x.astype(BF16)
    grad_normed = jnp.zeros((PART, D), F32)
    for j in range(4):
        u = inner[:, j * FCH : (j + 1) * FCH]
        bend = jnp.tanh(GELU_K * (u + GELU_C * u * u * u))
        slope = 0.5 * (1.0 + bend) + 0.5 * u * (1.0 - bend * bend) * (GELU_K * (1.0 + 3.0 * GELU_C * u * u))
        grad_u = (nt(low, w_fc_out[0, j * FCH : (j + 1) * FCH, :]) * slope).astype(BF16)
        grad_normed = grad_normed + nt(grad_u, w_fc[0, :, j * FCH : (j + 1) * FCH])
    grad_h = grad_x + norm_back(attended[...], norms[1, 0:1, :], grad_normed)
    grad_mixed = nt(grad_h.astype(BF16), w_out[0]).astype(BF16)

    wide = (HEADS * PRE, D)
    same_head = (rows(wide) // PRE) == (lanes(wide) // HEAD_DIM)
    keys = prefix_kv[:, 0:D]
    values = prefix_kv[:, D:KVW]
    zero = jnp.zeros(wide, BF16)
    keys = jnp.where(same_head, jnp.concatenate([keys] * HEADS, axis=0), zero)
    values = jnp.where(same_head, jnp.concatenate([values] * HEADS, axis=0), zero)
    of_head = (lanes((128, HEADS * PRE)) // PRE == rows((128, HEADS * PRE))).astype(F32)
    logs = nn(stats[:, 0:128], of_head, HIGH)
    lane = lanes((PART, HEADS * PRE))
    live = lane - (lane // PRE) * PRE < PREFIX
    q = query[...]
    probs = jnp.where(live, jnp.exp(nt(q, keys) - logs), 0.0)
    grad_probs = nt(grad_mixed, values)
    inner_sum = nt(grad_mixed.astype(F32) * mixed[...], same_head.astype(F32), HIGH)
    grad_scores = (probs * (grad_probs - inner_sum)).astype(BF16)
    grad_keys = jnp.where(same_head, tn(grad_scores, q), 0.0)
    grad_values = jnp.where(same_head, tn(probs.astype(BF16), grad_mixed), 0.0)
    for side, value in enumerate((grad_keys, grad_values)):
        folded = value[0:PRE, :]
        for h in range(1, HEADS):
            folded = folded + value[h * PRE : (h + 1) * PRE, :]
        result[:, side * D : (side + 1) * D] = folded[0:8, :]
        for r in range(2):
            for k in range(2):
                result[4 * r + 2 * side + k : 4 * r + 2 * side + k + 1, KVW : KVW + 512] = folded[
                    8 + r : 9 + r, k * 512 : (k + 1) * 512
                ]
    lane = lanes((8, 256))
    result[:, KVW + 512 : FLAT] = jnp.where((lane == 0) & (rows((8, 256)) == 0), loss, 0.0)


def backward(own, other, kept, prefix_kv, norms, w_out, w_fc, w_fc_out):
    return call(
        backward_body,
        shaped((8, FLAT)),
        [WHOLE] * 14,
        limit=10,
        name="backward_to_prefix",
        flops=2 * PART * D * 9 * D,
        moved=20000000,
    )(own, other, *kept, prefix_kv, norms, w_out, w_fc, w_fc_out)


def send_body(a, b, out):
    total = a[...] + b[...]
    low = total.astype(BF16)
    tail = total[0:1, KVW + 512 : FLAT]
    high, middle, rest = three_way(tail[:, 0:1])
    lane = lanes((8, 256))
    loss = jnp.where(lane == 0, high, jnp.where(lane == 1, middle, jnp.where(lane == 2, rest, 0.0)))
    low = jnp.concatenate([low[:, : KVW + 512], loss.astype(BF16)], axis=1)
    both = jnp.concatenate([low[:, : FLAT // 2], low[:, FLAT // 2 :]], axis=0)
    out[...] = jnp.broadcast_to(both[None], out.shape)


def copies_to_send(a, b):
    return call(
        send_body, shaped((16, 16, FLAT // 2), BF16), [WHOLE] * 2, limit=8, name="sum_to_send", moved=900000
    )(a, b)


def adam(weight, grad, first, second):
    first = BETA_ONE * first + (1.0 - BETA_ONE) * grad
    second = BETA_TWO * second + (1.0 - BETA_TWO) * grad * grad
    move = first / (1.0 - BETA_ONE**STEP) / (jnp.sqrt(second / (1.0 - BETA_TWO**STEP)) + ADAM_EPS)
    return weight - RATE * (move + DECAY * weight), first, second


def total_of(value):
    return jnp.sum(jnp.sum(value, axis=1, keepdims=True), axis=0, keepdims=True)


def update_body(
    idx, pieces, in_high, in_low, out_t, prefix, hidden, extra,
    w0, w1, w2, w3, m0, m1, m2, m3, v0, v1, v2, v3,
    loss, count, norm, nw0, nw1, nw2, nw3, nm0, nm1, nm2, nm3, nv0, nv1, nv2, nv3, columns,
):
    place = idx[0] * 4 + idx[1]
    counted = extra[0:1, 0:1]
    scale = 1.0 / counted
    both = pieces[0].astype(F32)
    for k in range(1, 16):
        both = both + pieces[k].astype(F32)
    flat = jnp.concatenate([both[0:8, :], both[8:16, :]], axis=1)
    loss[...] = jnp.sum(flat[0:1, KVW + 512 : FLAT], axis=1, keepdims=True)
    last = flat[:, KVW : KVW + 512]
    ends = [jnp.concatenate([last[4 * r + k : 4 * r + k + 1, :] for k in range(4)], axis=1) for r in range(2)]
    states = jnp.concatenate([flat[:, 0:KVW], *ends, jnp.zeros((6, KVW), F32)], axis=0) * scale
    columns[...] = states
    live = rows((PRE, PHID)) < PREFIX
    hid = hidden[...]
    pre_weight = prefix[...]
    high, low = two_way(states)
    got = nn(high, out_t[...]) + nn(low, out_t[...])
    grad_pre = jnp.where(live, got * (1.0 - hid * hid), 0.0)
    high, low = two_way(grad_pre)
    grad_prefix = nn(high, in_high[...]) + nn(high, in_low[...]) + nn(low, in_high[...])
    biases = jnp.concatenate(
        [jnp.sum(grad_pre, axis=0, keepdims=True), jnp.sum(states, axis=0, keepdims=True)], axis=1
    )
    squares = (
        total_of(grad_prefix * grad_prefix)
        + total_of(nt(pre_weight, pre_weight, HIGH) * nt(grad_pre, grad_pre, HIGH))
        + total_of(nt(hid, hid, HIGH) * nt(states, states, HIGH))
        + total_of(biases * biases)
    )
    size = jnp.sqrt(squares)
    factor = jnp.minimum(1.0, CLIP / (size + 1e-06))
    count[...] = counted
    norm[...] = size

    select = (rows((PHID, 32)) == lanes((PHID, 32)) + place * 32).astype(F32)
    mine = nn(jnp.concatenate([grad_pre, grad_prefix], axis=0), select, HIGH) * factor
    nw0[...], nm0[...], nv0[...] = adam(w0[...], mine[PRE : PRE + PREFIX, :], m0[...], v0[...])
    grad_in = tn(mine[0:PRE, :], pre_weight, HIGH)
    nw1[...], nm1[...], nv1[...] = adam(w1[...], grad_in, m1[...], v1[...])
    own = columns[:, pl.ds(pl.multiple_of(place * 128, 128), 128)]
    grad_out = tn(hid, own * factor, HIGH)
    nw2[...], nm2[...], nv2[...] = adam(w2[...], grad_out, m2[...], v2[...])
    turned = jnp.broadcast_to(biases, (8, 5 * PHID))
    turned = pltpu.roll(turned, lax.rem(5 * PHID - place * 160, 5 * PHID), 1)[0:1, 0:160] * factor
    nw3[...], nm3[...], nv3[...] = adam(w3[...], turned, m3[...], v3[...])


def update(idx, pieces, network, weights, firsts, seconds):
    sizes = [shaped(w.shape) for w in weights]
    one = shaped((1, 1))
    return call(
        update_body,
        (one, one, one, *sizes, *sizes, *sizes),
        [SCALARS] + [WHOLE] * 19,
        (pltpu.VMEM((PRE, KVW), F32),),
        limit=16,
        name="clip_and_update",
        moved=6000000,
    )(idx, pieces, *network, *weights, *firsts, *seconds)


def from_behind(value, axis, k):
    return lax.ppermute(value, axis, [(i, (i + k) % 4) for i in range(4)])


def around(value, axis):
    return (value, *(from_behind(value, axis, k) for k in (1, 2, 3)))


def scattered(values, axis):
    return (values[0], *(from_behind(values[k], axis, k) for k in (1, 2, 3)))


def with_neighbour(value, axis, bit):
    return lax.ppermute(value, axis, [(i, i ^ bit) for i in range(4)])


def swapped(value):
    return lax.ppermute(value, "core", [(0, 1), (1, 0)])


def on_device(
    tokens,
    segments,
    valid,
    embedding,
    positions_table,
    w_qkv,
    w_attn_out,
    w_fc,
    w_fc_out,
    layer_bias,
    norm_params,
    prefix,
    prefix_in,
    prefix_out,
    prefix_bias,
    moment_prefix,
    moment_in,
    moment_out,
    moment_bias,
    square_prefix,
    square_in,
    square_out,
    square_bias,
):
    idx = jnp.stack([lax.axis_index(a) for a in ("z", "y", "x", "core")]).astype(jnp.int32)
    bias_row = prefix_bias.reshape(1, -1)

    packed = pack(idx, prefix_in.T, prefix_out, prefix, bias_row, segments, valid)
    packed, tokens = lax.optimization_barrier((packed, tokens))
    packed = around(packed, "y")
    own, other = token_rows(idx, tokens, embedding)
    embedded = own + swapped(other)
    embedded = around(embedded, "x")
    packed = around(stack(packed), "z")
    *network, extra, states = prefix_states(idx, packed, [swapped(p) for p in packed])

    x, embedded, query, keyval = projections(idx, embedded, positions_table, norm_params, layer_bias, w_qkv)
    final, *kept = layer(
        idx, query, keyval, swapped(keyval), embedded, x, states, segments, valid, norm_params, layer_bias,
        w_attn_out, w_fc, w_fc_out,
    )
    pieces = scattered(vocabulary(idx, final, swapped(final), embedding), "x")
    mine, theirs = merge(pieces)
    grad = backward(mine, swapped(theirs), kept, states, norm_params, w_attn_out, w_fc, w_fc_out)
    grad = grad + swapped(grad)
    grad = grad + with_neighbour(grad, "x", 1)
    grad = copies_to_send(grad, with_neighbour(grad, "x", 3))
    grad = lax.all_to_all(grad, ("z", "y"), 0, 0, tiled=True)
    outs = update(
        idx, grad, (*network, extra),
        (prefix, prefix_in.T, prefix_out, bias_row),
        (moment_prefix, moment_in.T, moment_out, moment_bias.reshape(1, -1)),
        (square_prefix, square_in.T, square_out, square_bias.reshape(1, -1)),
    )
    outs = list(outs)
    for k in range(3):
        outs[k] = outs[k].reshape(())
        outs[4 + 4 * k] = outs[4 + 4 * k].T
        outs[6 + 4 * k] = outs[6 + 4 * k].reshape(-1)
    return tuple(outs)


def solution(mesh):
    split = Mesh(mesh.devices.reshape(4, 4, 4, 2), ("z", "y", "x", "core"))
    dp = ("z", "y")
    sharded = (P(None, dp), P(None, dp), P(None, dp), P(dp))
    placed = (
        P(dp, None),
        P(dp, None),
        P(dp, None),
        P(("x", "core"), None),
        *([P()] * 7),
        *sharded,
        *sharded,
        *sharded,
    )
    return jax.shard_map(
        on_device,
        mesh=split,
        in_specs=placed,
        out_specs=(P(), P(), P(), *sharded, *sharded, *sharded),
        check_vma=False,
    )
```

```python
import jax
import jax.numpy as jnp
from jax import lax
from jax.experimental import pallas as pl
from jax.experimental.pallas import tpu as pltpu
from jax.sharding import Mesh
from jax.sharding import PartitionSpec as P

D = 1024
HEADS = 16
HEAD_DIM = 64
FF = 4096
VOCAB = 51200
PREFIX = 10
PHID = 512
LENGTH = 256
STEP = 10
KVW = 2048
HALF = 128
PART = 32
SHARD = VOCAB // 8
PRE = 16
EXT = D + 128
FLAT = KVW + 768
SIDE = FLAT // 2

NORM_EPS = 1e-05
BETA_ONE = 0.9
BETA_TWO = 0.999
ADAM_EPS = 1e-08
RATE = 0.1
DECAY = 0.01
CLIP = 0.001
MASKED = -1e30
SCALE = HEAD_DIM**-0.5
GELU_K = 0.7978845608028654
GELU_C = 0.044715

HIGH = lax.Precision.HIGHEST
F32 = jnp.float32
BF16 = jnp.bfloat16
MIB = 1 << 20

WHOLE = pl.BlockSpec(memory_space=pltpu.VMEM)
SCALARS = pl.BlockSpec(memory_space=pltpu.SMEM)
REMAIN = pl.BlockSpec(memory_space=pl.ANY)


def nn(a, b, precision=None):
    return lax.dot_general(a, b, (((1,), (0,)), ((), ())), precision=precision, preferred_element_type=F32)


def nt(a, b, precision=None):
    return lax.dot_general(a, b, (((1,), (1,)), ((), ())), precision=precision, preferred_element_type=F32)


def tn(a, b, precision=None):
    return lax.dot_general(a, b, (((0,), (0,)), ((), ())), precision=precision, preferred_element_type=F32)


def lanes(shape):
    return lax.broadcasted_iota(jnp.int32, shape, len(shape) - 1)


def rows(shape):
    return lax.broadcasted_iota(jnp.int32, shape, 0)


def call(body, outs, ins, scratch=(), limit=48, name=None, flops=0, moved=0):
    return pl.pallas_call(
        body,
        out_shape=outs,
        in_specs=ins,
        out_specs=jax.tree.map(lambda _: WHOLE, outs),
        scratch_shapes=scratch,
        compiler_params=pltpu.CompilerParams(vmem_limit_bytes=limit * MIB),
        cost_estimate=pl.CostEstimate(flops=flops, bytes_accessed=moved, transcendentals=0),
        name=name,
    )


def shaped(shape, dtype=F32):
    return jax.ShapeDtypeStruct(shape, dtype)


def normalised(value):
    mean = jnp.mean(value, axis=-1, keepdims=True)
    centred = value - mean
    spread = jnp.mean(centred * centred, axis=-1, keepdims=True)
    inverse = lax.rsqrt(spread + NORM_EPS)
    return centred * inverse, inverse


def norm_back(value, gain, grad):
    unit, inverse = normalised(value)
    scaled = grad * gain
    first = jnp.mean(scaled, axis=-1, keepdims=True)
    second = jnp.mean(scaled * unit, axis=-1, keepdims=True)
    return inverse * (scaled - first - unit * second)


def three_way(value):
    high = value.astype(BF16).astype(F32)
    rest = value - high
    middle = rest.astype(BF16).astype(F32)
    return high, middle, rest - middle


def with_stat(body, stat):
    high, middle, low = three_way(stat)
    lane = lanes((body.shape[0], 128))
    tail = jnp.where(lane == 0, high, jnp.where(lane == 1, middle, jnp.where(lane == 2, low, 0.0)))
    return body.astype(BF16), tail.astype(BF16)


def stat_of(ref):
    tail = ref[:, D:EXT].astype(F32)
    return jnp.sum(jnp.where(lanes(tail.shape) < 3, tail, 0.0), axis=1, keepdims=True)


UNITS = 16
HALF_HID = PHID // 2
COLS = 64
OWN = UNITS + COLS
SMALL = 32
PACK = OWN + SMALL
TALL = 4 * OWN + SMALL


def two_way(value):
    high = value.astype(BF16)
    return high, (value - high.astype(F32)).astype(BF16)


def placed(value, width, start):
    wide = jnp.concatenate([value, jnp.zeros((value.shape[0], width - value.shape[1]), F32)], axis=1)
    return pltpu.roll(wide, start, 1)


def pack_body(idx, weight_in_at, weight_out_at, weight_at, bias_at, segments_at, valid_at, out, *scratch):
    *held, small, sems = scratch
    sources = (weight_in_at, weight_out_at, weight_at, bias_at, segments_at, valid_at)
    copies = [pltpu.make_async_copy(a, b, sems.at[k]) for k, (a, b) in enumerate(zip(sources, held))]
    for c in copies:
        c.start()
    weight_in, weight_out, weight, bias, segments, valid = held
    core = idx[3]
    place = idx[0] * 4 + idx[1]
    for c in copies:
        c.wait()
    out[0:UNITS, :] = weight_in[pl.ds(pl.multiple_of(core * UNITS, UNITS), UNITS), :]
    own = [
        jnp.where(core == 0, weight_out[32 * d : 32 * d + UNITS, :], weight_out[32 * d + UNITS : 32 * d + 32, :])
        for d in range(16)
    ]
    turned = jnp.transpose(jnp.concatenate(own, axis=0))
    out[UNITS:OWN, 0:HALF_HID] = turned[0:COLS, :]
    out[UNITS:OWN, HALF_HID:PHID] = turned[COLS:128, :]
    whole = jnp.concatenate([weight[...], jnp.zeros((16 - PREFIX, 32), F32)], axis=0)
    small[...] = placed(whole, PHID, place * 32)
    flat = placed(jnp.broadcast_to(bias[...], (8, 160)), 5 * PHID, place * 160)
    for r in range(5):
        small[PREFIX + r : PREFIX + r + 1, :] = flat[0:1, r * PHID : (r + 1) * PHID]
    seg = segments[...]
    after = jnp.concatenate([seg[:, 1:], seg[:, :1]], axis=1)
    kept = (valid[...] > 0) & (lanes(seg.shape) < LENGTH - 1) & (after == seg)
    total = jnp.sum(kept.astype(F32), axis=1, keepdims=True)
    small[15:16, :] = jnp.where(lanes((1, PHID)) == place, total, 0.0)
    high = small[...].astype(BF16).astype(F32)
    out[OWN : OWN + 16, :] = high
    out[OWN + 16 : PACK, :] = small[...] - high


def in_hbm(value):
    return pltpu.with_memory_space_constraint(value, pltpu.HBM)


def pack(idx, *inputs):
    return call(
        pack_body,
        shaped((PACK, PHID)),
        [SCALARS] + [REMAIN] * 6,
        (*(pltpu.VMEM(v.shape, v.dtype) for v in inputs), pltpu.VMEM((16, PHID), F32), pltpu.SemaphoreType.DMA((6,))),
        limit=8,
        name="pack_prefix_weights",
        moved=500000,
    )(idx, *(in_hbm(v) for v in inputs))


def stack(pieces):
    small = (pieces[0][OWN:] + pieces[1][OWN:]) + (pieces[2][OWN:] + pieces[3][OWN:])
    return jnp.concatenate([*(p[:OWN] for p in pieces), small], axis=0)


NET_IN = 2 * KVW
NET_HID = NET_IN + 4 * HALF_HID
NET = NET_HID + 2 * PRE


def by_units(first, second):
    parts = []
    for d in range(16):
        at = slice(d * UNITS, (d + 1) * UNITS)
        parts += [first[:, at], second[:, at]]
    return jnp.concatenate(parts, axis=1)


def three_products(product, left, right_high, right_low):
    high, low = two_way(left)
    return product(high, right_high) + (product(high, right_low) + product(low, right_high))


def states_body(idx, a, b, c, d, net, weight, extra, part, in_t, out_t):
    z, y, core = idx[0], idx[1], idx[3]
    pieces = (a, b, c, d)
    for late in range(4):
        for early in range(4):
            dz = jnp.where(core == 0, late, early)
            dy = jnp.where(core == 0, early, late)
            place = lax.rem(z + 4 - dz, 4) * 4 + lax.rem(y + 4 - dy, 4)
            at = early * OWN
            in_t[pl.ds(pl.multiple_of(place * UNITS, UNITS), UNITS), :] = pieces[late][at : at + UNITS, :]
            for side in range(2):
                to = pl.ds(pl.multiple_of(place * 128 + side * COLS, COLS), COLS)
                out_t[to, :] = pieces[late][at + UNITS : at + OWN, side * HALF_HID : (side + 1) * HALF_HID]
    rest = sum((r[4 * OWN : TALL, :] for r in pieces[1:]), a[4 * OWN : TALL, :])
    rest = rest[0:16, :] + rest[16:32, :]
    extra[...] = rest
    whole = jnp.where(rows((PRE, PHID)) < PREFIX, rest, 0.0)
    weight[...] = whole
    bias = rest[PREFIX : PREFIX + 1, :]
    bias = jnp.where(core == 0, bias, pltpu.roll(bias, PHID - UNITS, 1))
    bias = jnp.concatenate([bias[:, 32 * k : 32 * k + UNITS] for k in range(16)], axis=1)
    high, low = two_way(in_t[...])
    pre = three_products(nt, whole, high, low) + bias
    hid = jnp.where(rows(pre.shape) < PREFIX, jnp.tanh(pre), 0.0)
    for k, piece in enumerate((high, low)):
        at = NET_IN + 2 * k * HALF_HID
        net[at : at + HALF_HID, :] = piece[:, 0:HALF_HID]
        net[at + HALF_HID : at + 2 * HALF_HID, :] = piece[:, HALF_HID:PHID]
    net[NET_HID : NET_HID + PRE, :], net[NET_HID + PRE : NET, :] = two_way(hid)
    high, low = two_way(out_t[...])
    net[0:KVW, :] = high
    net[KVW : 2 * KVW, :] = low
    part[...] = three_products(nt, hid, high, low)


def prefix_states(idx, pieces):
    return call(
        states_body,
        (shaped((NET, HALF_HID), BF16), shaped((PRE, PHID)), shaped((PRE, PHID)), shaped((PRE, KVW))),
        [SCALARS] + [WHOLE] * 4,
        (pltpu.VMEM((HALF_HID, PHID), F32), pltpu.VMEM((KVW, HALF_HID), F32)),
        limit=12,
        name="prefix_states",
        moved=7000000,
    )(idx, *pieces)


AHEAD = 64


def rows_body(idx, tokens_at, table, own, other, block, held, tokens, found, sems):
    first = (idx[2] * 2 + idx[3]) * SHARD
    fetch = pltpu.make_async_copy(tokens_at, tokens, sems.at[AHEAD])
    fetch.start()
    held[...] = jnp.zeros_like(held)
    fetch.wait()

    def find(p, n):
        local = tokens[0, p] - first
        found[n] = p
        return n + ((local >= 0) & (local < SHARD)).astype(jnp.int32)

    number = lax.fori_loop(0, LENGTH, find, 0, unroll=16)

    def copy(n, local):
        at = pl.multiple_of((local // 16) * 16, 16)
        slot = lax.rem(n, AHEAD)
        return pltpu.make_async_copy(table.at[pl.ds(at, 16), :], block.at[slot], sems.at[slot])

    def begin(n, carry):
        copy(n, tokens[0, found[n]] - first).start()
        return carry

    def take(n, carry):
        p = found[n]
        local = tokens[0, p] - first
        copy(n, local).wait()
        got = block[lax.rem(n, AHEAD)].astype(F32)
        line = jnp.sum(jnp.where(rows((16, D)) == lax.rem(local, 16), got, 0.0), axis=0, keepdims=True)
        held[pl.ds(p, 1), :] = line
        return carry

    for batch in range(LENGTH // AHEAD):
        low = jnp.minimum(number, batch * AHEAD)
        high = jnp.minimum(number, (batch + 1) * AHEAD)
        lax.fori_loop(low, high, begin, 0)
        lax.fori_loop(low, high, take, 0)
    core = idx[3]
    own[...] = held[pl.ds(pl.multiple_of(core * HALF, HALF), HALF), :].astype(BF16)
    other[...] = held[pl.ds(pl.multiple_of((1 - core) * HALF, HALF), HALF), :].astype(BF16)


def token_rows(idx, tokens, table):
    return call(
        rows_body,
        (shaped((HALF, D), BF16), shaped((HALF, D), BF16)),
        [SCALARS, REMAIN, REMAIN],
        (
            pltpu.VMEM((AHEAD, 16, D), BF16),
            pltpu.VMEM((LENGTH, D), F32),
            pltpu.SMEM((1, LENGTH), jnp.int32),
            pltpu.SMEM((LENGTH,), jnp.int32),
            pltpu.SemaphoreType.DMA((AHEAD + 1,)),
        ),
        limit=8,
        name="token_rows",
        moved=2000000,
    )(idx, in_hbm(tokens), in_hbm(table))


def bring_body(*refs):
    half = len(refs) // 2
    sems = refs[-1]
    copies = [pltpu.make_async_copy(refs[k], refs[half + k], sems.at[k]) for k in range(half)]
    for c in copies:
        c.start()
    for c in copies:
        c.wait()


def bring(*inputs):
    return pl.pallas_call(
        bring_body,
        out_shape=tuple(pltpu.VMEM(v.shape, v.dtype) for v in inputs),
        in_specs=[REMAIN] * len(inputs),
        out_specs=tuple(REMAIN for _ in inputs),
        scratch_shapes=(pltpu.SemaphoreType.DMA((len(inputs),)),),
        compiler_params=pltpu.CompilerParams(vmem_limit_bytes=MIB),
        cost_estimate=pl.CostEstimate(flops=0, bytes_accessed=2 * sum(v.size * v.dtype.itemsize for v in inputs), transcendentals=0),
        name="bring_into_vmem",
    )(*(in_hbm(v) for v in inputs))


def qkv_body(idx, embedded, places, norms, bias, weight, x_out, query, keyval):
    core = idx[3]
    mine = embedded[...]
    x = mine.astype(F32) + places[pl.ds(pl.multiple_of(core * HALF, HALF), HALF), :].astype(F32)
    x_out[...] = x
    unit, _ = normalised(x)
    normed = (unit * norms[0, 0:1, :] + norms[0, 1:2, :]).astype(BF16)
    for j in range(6):
        at = slice(j * 512, (j + 1) * 512)
        part = nn(normed, weight[0, :, at]) + bias[:, at].astype(F32)
        if j < 2:
            query[:, at] = (part.astype(BF16).astype(F32) * SCALE).astype(BF16)
        else:
            keyval[0:HALF, (j - 2) * 512 : (j - 1) * 512] = part.astype(BF16)
    keyval[HALF : HALF + 16, 0:D] = mine[0:16, :]
    keyval[HALF : HALF + 16, D:KVW] = jnp.zeros((16, D), BF16)


def projections(idx, embedded, places, norms, bias, weight):
    return call(
        qkv_body,
        (shaped((HALF, D)), shaped((HALF, D), BF16), shaped((HALF + 16, KVW), BF16)),
        [SCALARS] + [WHOLE] * 5,
        limit=10,
        name="norm_and_projections",
        flops=2 * HALF * D * 3 * D,
        moved=9000000,
    )(idx, embedded, places, norms, bias, weight)


FCH = 1024


def layer_body(
    idx, query, kv_own, kv_other, embedded, x_in, states_own, states_other, extra, segments, valid, norms, bias,
    w_out, w_fc, w_fc_out,
    final, attended_part, last_part, inner_part, mixed_part, query_part, target_part, stats_part, prefix_kv,
    mixed, log_sums, keep, wide,
):
    xx, core = idx[2], idx[3]
    part = pl.ds(pl.multiple_of(xx * PART, PART), PART)
    shift = jnp.concatenate([extra[r : r + 1, :] for r in range(PREFIX + 1, PREFIX + 5)], axis=1)
    states = states_own[...] + states_other[...] + shift
    prefix_kv[...] = jnp.where(rows(states.shape) < PREFIX, states, 0.0).astype(BF16)

    seg = segments[...]
    mine = jnp.where(core == 0, seg[:, 0:HALF], seg[:, HALF:LENGTH])
    theirs = jnp.where(core == 0, seg[:, HALF:LENGTH], seg[:, 0:HALF])
    square = (HALF, HALF)
    mine_down = jnp.transpose(jnp.broadcast_to(mine, square))
    sees_own = (mine_down == jnp.broadcast_to(mine, square)) & (lanes(square) <= rows(square))
    sees_other = (mine_down == jnp.broadcast_to(theirs, square)) & (core == 1)
    sees_prefix = lanes(square) < PREFIX
    hide = jnp.concatenate([jnp.where(m, 0.0, MASKED) for m in (sees_own, sees_other, sees_prefix)], axis=1)
    hide = jnp.concatenate([hide, hide], axis=0)
    left = lanes(square) < HEAD_DIM
    sums = jnp.zeros(square, F32)
    pad = jnp.zeros((HALF - PRE, HALF), BF16)
    for pair in range(HEADS // 2):
        at = slice(pair * 128, pair * 128 + 128)
        at_v = slice(D + pair * 128, D + pair * 128 + 128)
        q = query[:, at]
        zero = jnp.zeros_like(q)
        both = jnp.concatenate([jnp.where(left, q, zero), jnp.where(left, zero, q)], axis=0)
        keys = jnp.concatenate([kv_own[0:HALF, at], kv_other[0:HALF, at], prefix_kv[:, at], pad], axis=0)
        values = jnp.concatenate([kv_own[0:HALF, at_v], kv_other[0:HALF, at_v], prefix_kv[:, at_v], pad], axis=0)
        scores = nt(both, keys) + hide
        top = jnp.max(scores, axis=1, keepdims=True)
        expo = jnp.exp(scores - top)
        total = jnp.sum(expo, axis=1, keepdims=True)
        out = nn(expo.astype(BF16), values) * (1.0 / total)
        mixed[:, at] = jnp.where(left, out[0:HALF], out[HALF:])
        logs = top + jnp.log(total)
        sums = jnp.where(lanes(square) == 2 * pair, logs[0:HALF], sums)
        sums = jnp.where(lanes(square) == 2 * pair + 1, logs[HALF:], sums)
    log_sums[...] = sums
    mixed_part[...] = mixed[part, :]
    query_part[...] = query[part, :]

    x = x_in[...] + nn(mixed[...].astype(BF16), w_out[0]) + bias[:, 3 * D : 4 * D].astype(F32)
    keep[...] = x
    attended_part[...] = keep[part, :]
    unit, _ = normalised(x)
    normed = (unit * norms[1, 0:1, :] + norms[1, 1:2, :]).astype(BF16)
    x = x + bias[:, 4 * D + FF : 5 * D + FF].astype(F32)
    for j in range(4):
        inner = nn(normed, w_fc[0, :, j * FCH : (j + 1) * FCH]) + bias[:, 4 * D + j * FCH : 4 * D + (j + 1) * FCH].astype(F32)
        wide[...] = inner
        inner_part[:, j * FCH : (j + 1) * FCH] = wide[part, :]
        active = (0.5 * inner * (1.0 + jnp.tanh(GELU_K * (inner + GELU_C * inner * inner * inner)))).astype(BF16)
        x = x + nn(active, w_fc_out[0, j * FCH : (j + 1) * FCH, :])
    keep[...] = x
    last_part[...] = keep[part, :]
    unit, _ = normalised(x)
    result = (unit * norms[2, 0:1, :] + norms[2, 1:2, :]).astype(BF16)
    final[...] = result

    wide[...] = embedded[...].astype(F32)
    keep[...] = result.astype(F32)
    after = jnp.concatenate([wide[1:HALF, :], kv_other[HALF : HALF + 1, 0:D].astype(F32)], axis=0)
    wide[...] = after
    target = wide[part, :]
    target_part[...] = target
    picked = jnp.sum(keep[part, :] * target, axis=1, keepdims=True)
    following = jnp.concatenate([seg[:, 1:], seg[:, :1]], axis=1)
    kept = (valid[...] > 0) & (lanes(seg.shape) < LENGTH - 1) & (following == seg)
    kept = kept.astype(F32)
    counted = jnp.where(core == 0, kept[:, 0:HALF], kept[:, HALF:LENGTH])
    wide[:, 0:HALF] = jnp.transpose(jnp.broadcast_to(counted, square))
    lane = lanes((PART, 128))
    stats_part[:, 0:128] = log_sums[part, :]
    stats_part[:, 128:256] = jnp.where(lane == 0, picked, jnp.where(lane == 1, wide[part, 0:128], 0.0))


def layer(idx, *inputs):
    return call(
        layer_body,
        (
            shaped((HALF, D), BF16),
            shaped((PART, D)),
            shaped((PART, D)),
            shaped((PART, FF)),
            shaped((PART, D)),
            shaped((PART, D), BF16),
            shaped((PART, D)),
            shaped((PART, 256)),
            shaped((PRE, KVW), BF16),
        ),
        [SCALARS] + [WHOLE] * len(inputs),
        (
            pltpu.VMEM((HALF, D), F32),
            pltpu.VMEM((HALF, 128), F32),
            pltpu.VMEM((HALF, D), F32),
            pltpu.VMEM((HALF, FCH), F32),
        ),
        limit=10,
        name="attention_and_feed_forward",
        flops=2 * HALF * D * 9 * D,
        moved=22000000,
    )(idx, *inputs)


VCH = 1280


def vocab_body(f_own, f_other, table, own, other, final, grad):
    final[0:HALF, :] = f_own[...]
    final[HALF:LENGTH, :] = f_other[...]
    for j in range(SHARD // VCH):
        chunk = table[j * VCH : (j + 1) * VCH, :]
        logits = nt(final[...], chunk)
        now = jnp.max(logits, axis=1, keepdims=True)
        if j:
            now = jnp.maximum(top, now)
            shrink = jnp.exp(top - now)
        expo = jnp.exp(logits - now)
        part = jnp.sum(expo, axis=1, keepdims=True)
        total = total * shrink + part if j else part
        part = nn(expo.astype(BF16), chunk)
        grad[...] = grad[...] * shrink + part if j else part
        top = now
    mean = grad[...] * (1.0 / total)
    log_sum = top + jnp.log(total)
    for out, at in ((own, slice(0, HALF)), (other, slice(HALF, LENGTH))):
        body, tail = with_stat(mean[at, :], log_sum[at, :])
        out[:, 0:D] = body
        out[:, D:EXT] = tail


def vocabulary(f_own, f_other, table):
    return call(
        vocab_body,
        (shaped((HALF, EXT), BF16),) * 2,
        [WHOLE] * 3,
        (pltpu.VMEM((LENGTH, D), BF16), pltpu.VMEM((LENGTH, D), F32)),
        limit=16,
        name="logits_and_gradient",
        flops=4 * LENGTH * D * SHARD,
        moved=SHARD * D * 2,
    )(f_own, f_other, table)


def merged(refs):
    stats = [stat_of(r) for r in refs]
    top = stats[0]
    for s in stats[1:]:
        top = jnp.maximum(top, s)
    weights = [jnp.exp(s - top) for s in stats]
    total = sum(weights[1:], weights[0])
    mean = sum((w * r[:, 0:D].astype(F32) for w, r in zip(weights[1:], refs[1:])), weights[0] * refs[0][:, 0:D].astype(F32))
    return mean * (1.0 / total), top + jnp.log(total)


def merge_body(idx, own, other, o0, o1, o2, o3, held):
    mean, log_total = merged((own, other))
    body, tail = with_stat(mean, log_total)
    held[:, 0:D] = body
    held[:, D:EXT] = tail
    for k, out in enumerate((o0, o1, o2, o3)):
        out[...] = held[pl.ds(pl.multiple_of(lax.rem(idx[2] + k, 4) * PART, PART), PART), :]


def merge(idx, own, other):
    return call(
        merge_body,
        (shaped((PART, EXT), BF16),) * 4,
        [SCALARS] + [WHOLE] * 2,
        (pltpu.VMEM((HALF, EXT), BF16),),
        limit=8,
        name="merge_two_cores",
        moved=900000,
    )(idx, own, other)


def backward_body(
    idx, extra, p0, p1, p2, p3, attended, last, inner, mixed, query, target, stats, prefix_kv, norms, w_out, w_fc, w_fc_out,
    own, other, result,
):
    mean, log_total = merged((p0, p1, p2, p3))
    counted = stats[:, 129:130]
    loss = jnp.sum((log_total - stats[:, 128:129]) * counted, axis=0, keepdims=True)
    scale = counted * (1.0 / jnp.sum(extra[15:16, :], axis=1, keepdims=True))
    exact = (jnp.exp(stats[:, 128:129] - log_total) - 1.0) * scale
    grad = mean * scale - target[...] * (scale + exact - exact.astype(BF16).astype(F32))
    grad_x = norm_back(last[...], norms[2, 0:1, :], grad)
    low = grad_x.astype(BF16)
    grad_normed = jnp.zeros((PART, D), F32)
    for j in range(4):
        u = inner[:, j * FCH : (j + 1) * FCH]
        bend = jnp.tanh(GELU_K * (u + GELU_C * u * u * u))
        slope = 0.5 * (1.0 + bend) + 0.5 * u * (1.0 - bend * bend) * (GELU_K * (1.0 + 3.0 * GELU_C * u * u))
        grad_u = (nt(low, w_fc_out[0, j * FCH : (j + 1) * FCH, :]) * slope).astype(BF16)
        grad_normed = grad_normed + nt(grad_u, w_fc[0, :, j * FCH : (j + 1) * FCH])
    grad_h = grad_x + norm_back(attended[...], norms[1, 0:1, :], grad_normed)
    grad_mixed = nt(grad_h.astype(BF16), w_out[0]).astype(BF16)

    wide = (HEADS * PRE, D)
    same_head = (rows(wide) // PRE) == (lanes(wide) // HEAD_DIM)
    keys = prefix_kv[:, 0:D]
    values = prefix_kv[:, D:KVW]
    zero = jnp.zeros(wide, BF16)
    keys = jnp.where(same_head, jnp.concatenate([keys] * HEADS, axis=0), zero)
    values = jnp.where(same_head, jnp.concatenate([values] * HEADS, axis=0), zero)
    of_head = (lanes((128, HEADS * PRE)) // PRE == rows((128, HEADS * PRE))).astype(F32)
    logs = nn(stats[:, 0:128], of_head, HIGH)
    lane = lanes((PART, HEADS * PRE))
    live = lane - (lane // PRE) * PRE < PREFIX
    q = query[...]
    probs = jnp.where(live, jnp.exp(nt(q, keys) - logs), 0.0)
    grad_probs = nt(grad_mixed, values)
    inner_sum = nt(grad_mixed.astype(F32) * mixed[...], same_head.astype(F32), HIGH)
    grad_scores = (probs * (grad_probs - inner_sum)).astype(BF16)
    grad_keys = jnp.where(same_head, tn(grad_scores, q), 0.0)
    grad_values = jnp.where(same_head, tn(probs.astype(BF16), grad_mixed), 0.0)
    for side, value in enumerate((grad_keys, grad_values)):
        folded = value[0:PRE, :]
        for h in range(1, HEADS):
            folded = folded + value[h * PRE : (h + 1) * PRE, :]
        result[:, side * D : (side + 1) * D] = folded[0:8, :]
        for r in range(2):
            for k in range(2):
                result[4 * r + 2 * side + k : 4 * r + 2 * side + k + 1, KVW : KVW + 512] = folded[
                    8 + r : 9 + r, k * 512 : (k + 1) * 512
                ]
    lane = lanes((8, 256))
    result[:, KVW + 512 : FLAT] = jnp.where((lane == 0) & (rows((8, 256)) == 0), loss, 0.0)
    left, right = result[:, 0:SIDE], result[:, SIDE:FLAT]
    own[...] = jnp.where(idx[3] == 0, left, right)
    other[...] = jnp.where(idx[3] == 0, right, left)


def backward(idx, *inputs):
    return call(
        backward_body,
        (shaped((8, SIDE)), shaped((8, SIDE))),
        [SCALARS] + [WHOLE] * len(inputs),
        (pltpu.VMEM((8, FLAT), F32),),
        limit=10,
        name="backward_to_prefix",
        flops=2 * PART * D * 9 * D,
        moved=20000000,
    )(idx, *inputs)


def send_body(idx, a, b, c, d, out):
    total = (a[...] + b[...]) + (c[...] + d[...])
    tail = total[:, SIDE - 256 : SIDE]
    high, middle, low = three_way(tail[:, 0:1])
    lane = lanes((8, 256))
    pieces = jnp.where(lane == 0, high, jnp.where(lane == 1, middle, jnp.where(lane == 2, low, 0.0)))
    tail = jnp.where(idx[3] == 1, pieces, tail)
    total = jnp.concatenate([total[:, 0 : SIDE - 256], tail], axis=1).astype(BF16)
    out[...] = jnp.broadcast_to(total[None], out.shape)


def copies_to_send(idx, pieces):
    return call(
        send_body,
        shaped((16, 8, SIDE), BF16),
        [SCALARS] + [WHOLE] * 4,
        limit=8,
        name="sum_to_send",
        moved=600000,
    )(idx, *pieces)


def adam(weight, grad, first, second):
    first = BETA_ONE * first + (1.0 - BETA_ONE) * grad
    second = BETA_TWO * second + (1.0 - BETA_TWO) * grad * grad
    move = first / (1.0 - BETA_ONE**STEP) / (jnp.sqrt(second / (1.0 - BETA_TWO**STEP)) + ADAM_EPS)
    return weight - RATE * (move + DECAY * weight), first, second


def total_of(value):
    return jnp.sum(jnp.sum(value, axis=1, keepdims=True), axis=0, keepdims=True)


def received_body(pieces, out):
    total = pieces[0].astype(F32)
    for k in range(1, 16):
        total = total + pieces[k].astype(F32)
    out[...] = total


def received(pieces):
    return call(received_body, shaped((8, SIDE)), [WHOLE], limit=8, name="sum_received", moved=400000)(pieces)


def update_body(idx, side_own, side_other, net_own, net_other, prefix, extra, *refs):
    away, refs = refs[:12], refs[12:]
    (loss, count, norm), outs, refs = refs[:3], refs[3:15], refs[15:]
    held, (columns, sems) = refs[:12], refs[12:]
    copies = [pltpu.make_async_copy(a, b, sems.at[k]) for k, (a, b) in enumerate(zip(away, held))]
    for c in copies:
        c.start()
    place = idx[0] * 4 + idx[1]
    core = idx[3]

    def in_order(mine, theirs):
        return jnp.where(core == 0, mine, theirs), jnp.where(core == 0, theirs, mine)

    flat = jnp.concatenate(in_order(side_own[...], side_other[...]), axis=1)
    loss[...] = jnp.sum(flat[0:1, KVW + 512 : FLAT], axis=1, keepdims=True)
    last = flat[:, KVW : KVW + 512]
    ends = [jnp.concatenate([last[4 * r + k : 4 * r + k + 1, :] for k in range(4)], axis=1) for r in range(2)]
    states = jnp.concatenate([flat[:, 0:KVW], *ends, jnp.zeros((6, KVW), F32)], axis=0)
    columns[...] = states
    pre_weight = prefix[...]
    states_high, states_low = two_way(states)

    def back(net):
        hid = net[NET_HID : NET_HID + PRE, :].astype(F32) + net[NET_HID + PRE : NET, :].astype(F32)
        weight = net[0:KVW, :]
        grad = nn(states_high, weight) + (nn(states_low, weight) + nn(states_high, net[KVW : 2 * KVW, :]))
        grad = grad * (1.0 - hid * hid)
        high, low = two_way(grad)
        sides = []
        for side in range(2):
            at = NET_IN + side * HALF_HID
            weight = net[at : at + HALF_HID, :]
            rest = net[at + 2 * HALF_HID : at + 3 * HALF_HID, :]
            sides.append(nn(high, weight) + (nn(low, weight) + nn(high, rest)))
        return hid, grad, jnp.concatenate(sides, axis=1)

    hid_own, grad_own, first = back(net_own)
    hid_other, grad_other, second = back(net_other)
    grad_prefix = first + second
    grad_pre = jnp.concatenate(in_order(grad_own, grad_other), axis=1)
    hid = jnp.concatenate(in_order(hid_own, hid_other), axis=1)
    biases = jnp.sum(grad_pre, axis=0, keepdims=True)
    biases = jnp.concatenate(
        [by_units(biases[:, 0:HALF_HID], biases[:, HALF_HID:PHID]), jnp.sum(states, axis=0, keepdims=True)], axis=1
    )
    squares = (
        total_of(grad_prefix * grad_prefix)
        + total_of(nt(pre_weight, pre_weight, HIGH) * nt(grad_pre, grad_pre, HIGH))
        + total_of(nt(hid, hid, HIGH) * nt(states, states, HIGH))
        + total_of(biases * biases)
    )
    size = jnp.sqrt(squares)
    factor = jnp.minimum(1.0, CLIP / (size + 1e-06))
    count[...] = jnp.sum(extra[15:16, :], axis=1, keepdims=True)
    norm[...] = size

    own = pltpu.roll(grad_prefix, lax.rem(PHID - place * 32, PHID), 1)[0:PREFIX, 0:32] * factor
    back_by = lax.rem(HALF_HID - place * UNITS, HALF_HID)
    sides = [pltpu.roll(grad_pre[:, at : at + HALF_HID], back_by, 1)[:, 0:UNITS] for at in (0, HALF_HID)]
    grad_in = tn(jnp.concatenate(sides, axis=1) * factor, pre_weight, HIGH)
    grad_out = tn(hid, columns[:, pl.ds(pl.multiple_of(place * 128, 128), 128)] * factor, HIGH)
    parts = []
    for d in range(16):
        parts += [grad_out[at + d * UNITS : at + (d + 1) * UNITS, :] for at in (0, HALF_HID)]
    grad_out = jnp.concatenate(parts, axis=0)
    turned = jnp.broadcast_to(biases, (8, 5 * PHID))
    turned = pltpu.roll(turned, lax.rem(5 * PHID - place * 160, 5 * PHID), 1)[0:1, 0:160] * factor
    for c in copies:
        c.wait()
    for k, grad in enumerate((own, grad_in, grad_out, turned)):
        new = adam(held[k][...], grad, held[4 + k][...], held[8 + k][...])
        for j in range(3):
            outs[4 * j + k][...] = new[j]


def update(idx, network, weights, firsts, seconds):
    sizes = [shaped(w.shape) for w in weights]
    one = shaped((1, 1))
    away = (*weights, *firsts, *seconds)
    return call(
        update_body,
        (one, one, one, *sizes, *sizes, *sizes),
        [SCALARS] + [WHOLE] * len(network) + [REMAIN] * 12,
        (*(pltpu.VMEM(w.shape, F32) for w in away), pltpu.VMEM((PRE, KVW), F32), pltpu.SemaphoreType.DMA((12,))),
        limit=16,
        name="clip_and_update",
        moved=6000000,
    )(idx, *network, *(in_hbm(w) for w in away))


def from_behind(value, axis, k):
    return lax.ppermute(value, axis, [(i, (i + k) % 4) for i in range(4)])


def around(value, axis):
    return (value, *(from_behind(value, axis, k) for k in (1, 2, 3)))


def scattered(values, axis):
    return (values[0], *(from_behind(values[k], axis, k) for k in (1, 2, 3)))


def crossed(value, late):
    got = [value]
    for k in (1, 2, 3):
        pairs = []
        for z in range(4):
            for y in range(4):
                for core in range(2):
                    to = (z, (y + k) % 4) if (core == 0) != late else ((z + k) % 4, y)
                    pairs.append(((z * 4 + y) * 2 + core, (to[0] * 4 + to[1]) * 2 + core))
        got.append(lax.ppermute(value, ("z", "y", "core"), pairs))
    return got


def summed_over(value, axis):
    for bit in (1, 3):
        value = value + lax.ppermute(value, axis, [(i, i ^ bit) for i in range(4)])
    return value


def swapped(value):
    return lax.ppermute(value, "core", [(0, 1), (1, 0)])


def on_device(
    tokens,
    segments,
    valid,
    embedding,
    positions_table,
    w_qkv,
    w_attn_out,
    w_fc,
    w_fc_out,
    layer_bias,
    norm_params,
    prefix,
    prefix_in,
    prefix_out,
    prefix_bias,
    moment_prefix,
    moment_in,
    moment_out,
    moment_bias,
    square_prefix,
    square_in,
    square_out,
    square_bias,
):
    idx = jnp.stack([lax.axis_index(a) for a in ("z", "y", "x", "core")]).astype(jnp.int32)
    bias_row = prefix_bias.reshape(1, -1)

    packed = pack(idx, prefix_in.T, prefix_out, prefix, bias_row, segments, valid)
    packed, tokens = lax.optimization_barrier((packed, tokens))
    packed = crossed(packed.astype(jnp.float16), False)
    own, other = token_rows(idx, tokens, embedding)
    other, packed = lax.optimization_barrier((other, packed))
    embedded, packed = lax.optimization_barrier((own + swapped(other), packed))
    embedded = summed_over(embedded, "x")
    packed = crossed(stack(packed), True)
    x, query, keyval = projections(idx, embedded, *bring(positions_table, norm_params, layer_bias, w_qkv))
    keyval, packed = lax.optimization_barrier((keyval, packed))
    packed = [p.astype(F32) for p in packed]
    net, prefix_all, extra, states = prefix_states(idx, packed)
    final, *kept = layer(
        idx, query, keyval, swapped(keyval), embedded, x, states, swapped(states), extra, segments, valid,
        norm_params, layer_bias, w_attn_out, w_fc, w_fc_out,
    )
    final_other, net = lax.optimization_barrier((swapped(final), net))
    own, other = vocabulary(final, final_other, embedding)
    own, net_other = lax.optimization_barrier((own, swapped(net)))
    pieces = scattered(merge(idx, own, swapped(other)), "x")
    own, other = backward(idx, extra, *pieces, *kept, norm_params, w_attn_out, w_fc, w_fc_out)
    grad = copies_to_send(idx, around(own + swapped(other), "x"))
    grad = lax.all_to_all(grad, ("z", "y"), 0, 0, tiled=True)
    grad = received(grad)
    outs = update(
        idx, (grad, swapped(grad), net, net_other, prefix_all, extra),
        (prefix, prefix_in.T, prefix_out, bias_row),
        (moment_prefix, moment_in.T, moment_out, moment_bias.reshape(1, -1)),
        (square_prefix, square_in.T, square_out, square_bias.reshape(1, -1)),
    )
    outs = list(outs)
    for k in range(3):
        outs[k] = outs[k].reshape(())
        outs[4 + 4 * k] = outs[4 + 4 * k].T
        outs[6 + 4 * k] = outs[6 + 4 * k].reshape(-1)
    return tuple(outs)


def solution(mesh):
    split = Mesh(mesh.devices.reshape(4, 4, 4, 2), ("z", "y", "x", "core"))
    dp = ("z", "y")
    sharded = (P(None, dp), P(None, dp), P(None, dp), P(dp))
    placed = (
        P(dp, None),
        P(dp, None),
        P(dp, None),
        P(("x", "core"), None),
        *([P()] * 7),
        *sharded,
        *sharded,
        *sharded,
    )
    return jax.shard_map(
        on_device,
        mesh=split,
        in_specs=placed,
        out_specs=(P(), P(), P(), *sharded, *sharded, *sharded),
        check_vma=False,
    )
```

```python
import jax
import jax.numpy as jnp
from jax import lax
from jax.experimental import pallas as pl
from jax.experimental.pallas import tpu as pltpu
from jax.sharding import Mesh
from jax.sharding import PartitionSpec as P

D = 1024
HEADS = 16
HEAD_DIM = 64
FF = 4096
VOCAB = 51200
PREFIX = 10
PHID = 512
LENGTH = 256
STEP = 10
KVW = 2048
HALF = 128
PART = 32
SHARD = VOCAB // 8
PRE = 16
EXT = D + 128
FLAT = KVW + 768
SIDE = FLAT // 2

NORM_EPS = 1e-05
BETA_ONE = 0.9
BETA_TWO = 0.999
ADAM_EPS = 1e-08
RATE = 0.1
DECAY = 0.01
CLIP = 0.001
MASKED = -1e30
SCALE = HEAD_DIM**-0.5
GELU_K = 0.7978845608028654
GELU_C = 0.044715

HIGH = lax.Precision.HIGHEST
F32 = jnp.float32
BF16 = jnp.bfloat16
MIB = 1 << 20

WHOLE = pl.BlockSpec(memory_space=pltpu.VMEM)
SCALARS = pl.BlockSpec(memory_space=pltpu.SMEM)
REMAIN = pl.BlockSpec(memory_space=pl.ANY)


def nn(a, b, precision=None):
    return lax.dot_general(a, b, (((1,), (0,)), ((), ())), precision=precision, preferred_element_type=F32)


def nt(a, b, precision=None):
    return lax.dot_general(a, b, (((1,), (1,)), ((), ())), precision=precision, preferred_element_type=F32)


def tn(a, b, precision=None):
    return lax.dot_general(a, b, (((0,), (0,)), ((), ())), precision=precision, preferred_element_type=F32)


def lanes(shape):
    return lax.broadcasted_iota(jnp.int32, shape, len(shape) - 1)


def rows(shape):
    return lax.broadcasted_iota(jnp.int32, shape, 0)


def call(body, outs, ins, scratch=(), limit=48, name=None, flops=0, moved=0):
    return pl.pallas_call(
        body,
        out_shape=outs,
        in_specs=ins,
        out_specs=jax.tree.map(lambda _: WHOLE, outs),
        scratch_shapes=scratch,
        compiler_params=pltpu.CompilerParams(vmem_limit_bytes=limit * MIB),
        cost_estimate=pl.CostEstimate(flops=flops, bytes_accessed=moved, transcendentals=0),
        name=name,
    )


def shaped(shape, dtype=F32):
    return jax.ShapeDtypeStruct(shape, dtype)


def normalised(value):
    mean = jnp.mean(value, axis=-1, keepdims=True)
    centred = value - mean
    spread = jnp.mean(centred * centred, axis=-1, keepdims=True)
    inverse = lax.rsqrt(spread + NORM_EPS)
    return centred * inverse, inverse


def norm_back(value, gain, grad):
    unit, inverse = normalised(value)
    scaled = grad * gain
    first = jnp.mean(scaled, axis=-1, keepdims=True)
    second = jnp.mean(scaled * unit, axis=-1, keepdims=True)
    return inverse * (scaled - first - unit * second)


def three_way(value):
    high = value.astype(BF16).astype(F32)
    rest = value - high
    middle = rest.astype(BF16).astype(F32)
    return high, middle, rest - middle


def with_stat(body, stat):
    high, middle, low = three_way(stat)
    lane = lanes((body.shape[0], 128))
    tail = jnp.where(lane == 0, high, jnp.where(lane == 1, middle, jnp.where(lane == 2, low, 0.0)))
    return body.astype(BF16), tail.astype(BF16)


def stat_of(ref):
    tail = ref[:, D:EXT].astype(F32)
    return jnp.sum(jnp.where(lanes(tail.shape) < 3, tail, 0.0), axis=1, keepdims=True)


UNITS = 16
HALF_HID = PHID // 2
COLS = 64
OWN = UNITS + COLS
SMALL = 32
PACK = OWN + SMALL
TALL = 4 * OWN + SMALL


def two_way(value):
    high = value.astype(BF16)
    return high, (value - high.astype(F32)).astype(BF16)


def placed(value, width, start):
    wide = jnp.concatenate([value, jnp.zeros((value.shape[0], width - value.shape[1]), F32)], axis=1)
    return pltpu.roll(wide, start, 1)


def pack_body(idx, weight_in_at, weight_out_at, weight_at, bias_at, segments_at, valid_at, out, *scratch):
    *held, small, sems = scratch
    sources = (weight_in_at, weight_out_at, weight_at, bias_at, segments_at, valid_at)
    copies = [pltpu.make_async_copy(a, b, sems.at[k]) for k, (a, b) in enumerate(zip(sources, held))]
    for c in copies:
        c.start()
    weight_in, weight_out, weight, bias, segments, valid = held
    core = idx[3]
    place = idx[0] * 4 + idx[1]
    for c in copies:
        c.wait()
    out[0:UNITS, :] = weight_in[pl.ds(pl.multiple_of(core * UNITS, UNITS), UNITS), :]
    own = [
        jnp.where(core == 0, weight_out[32 * d : 32 * d + UNITS, :], weight_out[32 * d + UNITS : 32 * d + 32, :])
        for d in range(16)
    ]
    turned = jnp.transpose(jnp.concatenate(own, axis=0))
    out[UNITS:OWN, 0:HALF_HID] = turned[0:COLS, :]
    out[UNITS:OWN, HALF_HID:PHID] = turned[COLS:128, :]
    whole = jnp.concatenate([weight[...], jnp.zeros((16 - PREFIX, 32), F32)], axis=0)
    small[...] = placed(whole, PHID, place * 32)
    flat = placed(jnp.broadcast_to(bias[...], (8, 160)), 5 * PHID, place * 160)
    for r in range(5):
        small[PREFIX + r : PREFIX + r + 1, :] = flat[0:1, r * PHID : (r + 1) * PHID]
    seg = segments[...]
    after = jnp.concatenate([seg[:, 1:], seg[:, :1]], axis=1)
    kept = (valid[...] > 0) & (lanes(seg.shape) < LENGTH - 1) & (after == seg)
    total = jnp.sum(kept.astype(F32), axis=1, keepdims=True)
    small[15:16, :] = jnp.where(lanes((1, PHID)) == place, total, 0.0)
    high = small[...].astype(BF16).astype(F32)
    out[OWN : OWN + 16, :] = high
    out[OWN + 16 : PACK, :] = small[...] - high


def in_hbm(value):
    return pltpu.with_memory_space_constraint(value, pltpu.HBM)


def pack(idx, *inputs):
    return call(
        pack_body,
        shaped((PACK, PHID)),
        [SCALARS] + [REMAIN] * 6,
        (*(pltpu.VMEM(v.shape, v.dtype) for v in inputs), pltpu.VMEM((16, PHID), F32), pltpu.SemaphoreType.DMA((6,))),
        limit=8,
        name="pack_prefix_weights",
        moved=500000,
    )(idx, *(in_hbm(v) for v in inputs))


def stack(pieces):
    small = (pieces[0][OWN:] + pieces[1][OWN:]) + (pieces[2][OWN:] + pieces[3][OWN:])
    return jnp.concatenate([*(p[:OWN] for p in pieces), small], axis=0)


NET_IN = 2 * KVW
NET_HID = NET_IN + 4 * HALF_HID
NET = NET_HID + 2 * PRE


def by_units(first, second):
    parts = []
    for d in range(16):
        at = slice(d * UNITS, (d + 1) * UNITS)
        parts += [first[:, at], second[:, at]]
    return jnp.concatenate(parts, axis=1)


def three_products(product, left, right_high, right_low):
    high, low = two_way(left)
    size = left.shape[0]
    both = product(jnp.concatenate([high, low], axis=0), right_high)
    return both[0:size] + (both[size : 2 * size] + product(high, right_low))


def gram(value):
    high, low = two_way(value)
    size = value.shape[0]
    both = jnp.concatenate([high, low], axis=0)
    both = nt(both, both)
    return both[0:size, 0:size] + (both[0:size, size:] + both[size:, 0:size])


def outer(left, right):
    left_high, left_low = two_way(left)
    high, low = two_way(right)
    return tn(jnp.concatenate([left_high, left_low, left_high], axis=0), jnp.concatenate([high, high, low], axis=0))


def states_body(idx, a, b, c, d, net, weight, extra, part, in_t, out_t):
    z, y, core = idx[0], idx[1], idx[3]
    pieces = (a, b, c, d)
    for late in range(4):
        for early in range(4):
            dz = jnp.where(core == 0, late, early)
            dy = jnp.where(core == 0, early, late)
            place = lax.rem(z + 4 - dz, 4) * 4 + lax.rem(y + 4 - dy, 4)
            at = early * OWN
            in_t[pl.ds(pl.multiple_of(place * UNITS, UNITS), UNITS), :] = pieces[late][at : at + UNITS, :]
            for side in range(2):
                to = pl.ds(pl.multiple_of(place * 128 + side * COLS, COLS), COLS)
                out_t[to, :] = pieces[late][at + UNITS : at + OWN, side * HALF_HID : (side + 1) * HALF_HID]
    rest = sum((r[4 * OWN : TALL, :] for r in pieces[1:]), a[4 * OWN : TALL, :])
    rest = rest[0:16, :] + rest[16:32, :]
    extra[...] = rest
    whole = jnp.where(rows((PRE, PHID)) < PREFIX, rest, 0.0)
    weight[...] = whole
    bias = rest[PREFIX : PREFIX + 1, :]
    bias = jnp.where(core == 0, bias, pltpu.roll(bias, PHID - UNITS, 1))
    bias = jnp.concatenate([bias[:, 32 * k : 32 * k + UNITS] for k in range(16)], axis=1)
    high, low = two_way(in_t[...])
    pre = three_products(nt, whole, high, low) + bias
    hid = jnp.where(rows(pre.shape) < PREFIX, jnp.tanh(pre), 0.0)
    for k, piece in enumerate((high, low)):
        at = NET_IN + 2 * k * HALF_HID
        net[at : at + HALF_HID, :] = piece[:, 0:HALF_HID]
        net[at + HALF_HID : at + 2 * HALF_HID, :] = piece[:, HALF_HID:PHID]
    net[NET_HID : NET_HID + PRE, :], net[NET_HID + PRE : NET, :] = two_way(hid)
    high, low = two_way(out_t[...])
    net[0:KVW, :] = high
    net[KVW : 2 * KVW, :] = low
    part[...] = three_products(nt, hid, high, low)


def prefix_states(idx, pieces):
    return call(
        states_body,
        (shaped((NET, HALF_HID), BF16), shaped((PRE, PHID)), shaped((PRE, PHID)), shaped((PRE, KVW))),
        [SCALARS] + [WHOLE] * 4,
        (pltpu.VMEM((HALF_HID, PHID), F32), pltpu.VMEM((KVW, HALF_HID), F32)),
        limit=12,
        name="prefix_states",
        moved=7000000,
    )(idx, *pieces)


AHEAD = 64


def rows_body(idx, tokens_at, table, *refs):
    number = (len(refs) - 8) // 2
    away, (own, other), brought = refs[:number], refs[number : number + 2], refs[number + 2 : 2 * number + 2]
    block, held, tokens, found, locals_, sems = refs[2 * number + 2 :]
    brings = [pltpu.make_async_copy(a, b, sems.at[AHEAD + 1 + k]) for k, (a, b) in enumerate(zip(away, brought))]
    for c in brings:
        c.start()
    first = (idx[2] * 2 + idx[3]) * SHARD
    fetch = pltpu.make_async_copy(tokens_at, tokens, sems.at[AHEAD])
    fetch.start()
    held[...] = jnp.zeros_like(held)
    fetch.wait()

    def find(p, n):
        local = tokens[0, p] - first
        found[n] = p
        locals_[n] = local
        return n + ((local >= 0) & (local < SHARD)).astype(jnp.int32)

    number = lax.fori_loop(0, LENGTH, find, 0, unroll=16)
    for k in range(4):
        found[number + k] = LENGTH
        locals_[number + k] = 0
    number = (number + 3) // 4

    def copy(n):
        at = pl.multiple_of((locals_[n] // 16) * 16, 16)
        slot = lax.rem(n, AHEAD)
        return pltpu.make_async_copy(table.at[pl.ds(at, 16), :], block.at[slot], sems.at[slot])

    def begin(i, carry):
        for k in range(4):
            copy(4 * i + k).start()
        return carry

    def take(i, carry):
        for k in range(4):
            copy(4 * i + k).wait()
        lines = []
        for k in range(4):
            n = 4 * i + k
            got = block[lax.rem(n, AHEAD)].astype(F32)
            row = lax.rem(locals_[n], 16)
            lines.append(jnp.sum(jnp.where(rows((16, D)) == row, got, 0.0), axis=0, keepdims=True))
        for k in range(4):
            held[pl.ds(found[4 * i + k], 1), :] = lines[k]
        return carry

    for batch in range(LENGTH // AHEAD):
        low = jnp.minimum(number, batch * (AHEAD // 4))
        high = jnp.minimum(number, (batch + 1) * (AHEAD // 4))
        lax.fori_loop(low, high, begin, 0)
        lax.fori_loop(low, high, take, 0)
    core = idx[3]
    own[...] = held[pl.ds(pl.multiple_of(core * HALF, HALF), HALF), :].astype(BF16)
    other[...] = held[pl.ds(pl.multiple_of((1 - core) * HALF, HALF), HALF), :].astype(BF16)
    for c in brings:
        c.wait()


def token_rows(idx, tokens, table, *away):
    return pl.pallas_call(
        rows_body,
        out_shape=(
            shaped((HALF, D), BF16),
            shaped((HALF, D), BF16),
            *(pltpu.VMEM(v.shape, v.dtype) for v in away),
        ),
        in_specs=[SCALARS] + [REMAIN] * (2 + len(away)),
        out_specs=(WHOLE, WHOLE, *([REMAIN] * len(away))),
        scratch_shapes=(
            pltpu.VMEM((AHEAD, 16, D), BF16),
            pltpu.VMEM((LENGTH + 8, D), F32),
            pltpu.SMEM((1, LENGTH), jnp.int32),
            pltpu.SMEM((LENGTH + 4,), jnp.int32),
            pltpu.SMEM((LENGTH + 4,), jnp.int32),
            pltpu.SemaphoreType.DMA((AHEAD + 1 + len(away),)),
        ),
        compiler_params=pltpu.CompilerParams(vmem_limit_bytes=8 * MIB),
        cost_estimate=pl.CostEstimate(flops=0, bytes_accessed=9000000, transcendentals=0),
        name="token_rows",
    )(idx, *(in_hbm(v) for v in (tokens, table, *away)))


def bring_body(*refs):
    half = len(refs) // 2
    sems = refs[-1]
    copies = [pltpu.make_async_copy(refs[k], refs[half + k], sems.at[k]) for k in range(half)]
    for c in copies:
        c.start()
    for c in copies:
        c.wait()


def bring(*inputs):
    return pl.pallas_call(
        bring_body,
        out_shape=tuple(pltpu.VMEM(v.shape, v.dtype) for v in inputs),
        in_specs=[REMAIN] * len(inputs),
        out_specs=tuple(REMAIN for _ in inputs),
        scratch_shapes=(pltpu.SemaphoreType.DMA((len(inputs),)),),
        compiler_params=pltpu.CompilerParams(vmem_limit_bytes=MIB),
        cost_estimate=pl.CostEstimate(flops=0, bytes_accessed=2 * sum(v.size * v.dtype.itemsize for v in inputs), transcendentals=0),
        name="bring_into_vmem",
    )(*(in_hbm(v) for v in inputs))


def qkv_body(idx, embedded, places, norms, bias, weight, x_out, query, keyval):
    core = idx[3]
    mine = embedded[...]
    x = mine.astype(F32) + places[pl.ds(pl.multiple_of(core * HALF, HALF), HALF), :].astype(F32)
    x_out[...] = x
    unit, _ = normalised(x)
    normed = (unit * norms[0, 0:1, :] + norms[0, 1:2, :]).astype(BF16)
    for j in range(6):
        at = slice(j * 512, (j + 1) * 512)
        part = nn(normed, weight[0, :, at]) + bias[:, at].astype(F32)
        if j < 2:
            query[:, at] = (part.astype(BF16).astype(F32) * SCALE).astype(BF16)
        else:
            keyval[0:HALF, (j - 2) * 512 : (j - 1) * 512] = part.astype(BF16)
    keyval[HALF : HALF + 16, 0:D] = mine[0:16, :]
    keyval[HALF : HALF + 16, D:KVW] = jnp.zeros((16, D), BF16)


def projections(idx, embedded, places, norms, bias, weight):
    return call(
        qkv_body,
        (shaped((HALF, D)), shaped((HALF, D), BF16), shaped((HALF + 16, KVW), BF16)),
        [SCALARS] + [WHOLE] * 5,
        limit=10,
        name="norm_and_projections",
        flops=2 * HALF * D * 3 * D,
        moved=9000000,
    )(idx, embedded, places, norms, bias, weight)


FCH = 1024


def layer_body(
    idx, query, kv_own, kv_other, embedded, x_in, states_own, states_other, extra, segments, valid, norms, bias,
    w_out, w_fc, w_fc_out,
    final, attended_part, last_part, inner_part, mixed_part, query_part, target_part, stats_part, prefix_kv,
    mixed, log_sums, keep, wide,
):
    xx, core = idx[2], idx[3]
    part = pl.ds(pl.multiple_of(xx * PART, PART), PART)
    shift = jnp.concatenate([extra[r : r + 1, :] for r in range(PREFIX + 1, PREFIX + 5)], axis=1)
    states = states_own[...] + states_other[...] + shift
    prefix_kv[...] = jnp.where(rows(states.shape) < PREFIX, states, 0.0).astype(BF16)

    seg = segments[...]
    mine = jnp.where(core == 0, seg[:, 0:HALF], seg[:, HALF:LENGTH])
    theirs = jnp.where(core == 0, seg[:, HALF:LENGTH], seg[:, 0:HALF])
    square = (HALF, HALF)
    mine_down = jnp.transpose(jnp.broadcast_to(mine, square))
    sees_own = (mine_down == jnp.broadcast_to(mine, square)) & (lanes(square) <= rows(square))
    sees_other = (mine_down == jnp.broadcast_to(theirs, square)) & (core == 1)
    sees_prefix = lanes(square) < PREFIX
    hide = jnp.concatenate([jnp.where(m, 0.0, MASKED) for m in (sees_own, sees_other, sees_prefix)], axis=1)
    hide = jnp.concatenate([hide, hide], axis=0)
    left = lanes(square) < HEAD_DIM
    sums = jnp.zeros(square, F32)
    pad = jnp.zeros((HALF - PRE, HALF), BF16)
    for pair in range(HEADS // 2):
        at = slice(pair * 128, pair * 128 + 128)
        at_v = slice(D + pair * 128, D + pair * 128 + 128)
        q = query[:, at]
        zero = jnp.zeros_like(q)
        both = jnp.concatenate([jnp.where(left, q, zero), jnp.where(left, zero, q)], axis=0)
        keys = jnp.concatenate([kv_own[0:HALF, at], kv_other[0:HALF, at], prefix_kv[:, at], pad], axis=0)
        values = jnp.concatenate([kv_own[0:HALF, at_v], kv_other[0:HALF, at_v], prefix_kv[:, at_v], pad], axis=0)
        scores = nt(both, keys) + hide
        top = jnp.max(scores, axis=1, keepdims=True)
        expo = jnp.exp(scores - top)
        total = jnp.sum(expo, axis=1, keepdims=True)
        out = nn((expo * (1.0 / total)).astype(BF16), values)
        mixed[:, at] = jnp.where(left, out[0:HALF], out[HALF:])
        logs = top + jnp.log(total)
        sums = jnp.where(lanes(square) == 2 * pair, logs[0:HALF], sums)
        sums = jnp.where(lanes(square) == 2 * pair + 1, logs[HALF:], sums)
    log_sums[...] = sums
    mixed_part[...] = mixed[part, :]
    query_part[...] = query[part, :]

    x = x_in[...] + nn(mixed[...].astype(BF16), w_out[0]) + bias[:, 3 * D : 4 * D].astype(F32)
    keep[...] = x
    attended_part[...] = keep[part, :]
    unit, _ = normalised(x)
    normed = (unit * norms[1, 0:1, :] + norms[1, 1:2, :]).astype(BF16)
    x = x + bias[:, 4 * D + FF : 5 * D + FF].astype(F32)
    for j in range(4):
        inner = nn(normed, w_fc[0, :, j * FCH : (j + 1) * FCH]) + bias[:, 4 * D + j * FCH : 4 * D + (j + 1) * FCH].astype(F32)
        wide[...] = inner
        inner_part[:, j * FCH : (j + 1) * FCH] = wide[part, :]
        active = (0.5 * inner * (1.0 + jnp.tanh(GELU_K * (inner + GELU_C * inner * inner * inner)))).astype(BF16)
        x = x + nn(active, w_fc_out[0, j * FCH : (j + 1) * FCH, :])
    keep[...] = x
    last_part[...] = keep[part, :]
    unit, _ = normalised(x)
    result = (unit * norms[2, 0:1, :] + norms[2, 1:2, :]).astype(BF16)
    final[...] = result

    wide[...] = embedded[...].astype(F32)
    keep[...] = result.astype(F32)
    after = jnp.concatenate([wide[1:HALF, :], kv_other[HALF : HALF + 1, 0:D].astype(F32)], axis=0)
    wide[...] = after
    target = wide[part, :]
    target_part[...] = target
    picked = jnp.sum(keep[part, :] * target, axis=1, keepdims=True)
    following = jnp.concatenate([seg[:, 1:], seg[:, :1]], axis=1)
    kept = (valid[...] > 0) & (lanes(seg.shape) < LENGTH - 1) & (following == seg)
    kept = kept.astype(F32)
    counted = jnp.where(core == 0, kept[:, 0:HALF], kept[:, HALF:LENGTH])
    wide[:, 0:HALF] = jnp.transpose(jnp.broadcast_to(counted, square))
    lane = lanes((PART, 128))
    stats_part[:, 0:128] = log_sums[part, :]
    stats_part[:, 128:256] = jnp.where(lane == 0, picked, jnp.where(lane == 1, wide[part, 0:128], 0.0))


def layer(idx, *inputs):
    return call(
        layer_body,
        (
            shaped((HALF, D), BF16),
            shaped((PART, D)),
            shaped((PART, D)),
            shaped((PART, FF)),
            shaped((PART, D)),
            shaped((PART, D), BF16),
            shaped((PART, D)),
            shaped((PART, 256)),
            shaped((PRE, KVW), BF16),
        ),
        [SCALARS] + [WHOLE] * len(inputs),
        (
            pltpu.VMEM((HALF, D), F32),
            pltpu.VMEM((HALF, 128), F32),
            pltpu.VMEM((HALF, D), F32),
            pltpu.VMEM((HALF, FCH), F32),
        ),
        limit=10,
        name="attention_and_feed_forward",
        flops=2 * HALF * D * 9 * D,
        moved=22000000,
    )(idx, *inputs)


VCH = 1280


def vocab_body(f_own, f_other, table, own, other, final, grad):
    final[0:HALF, :] = f_own[...]
    final[HALF:LENGTH, :] = f_other[...]
    chunks = SHARD // VCH
    logits = nt(final[...], table[0:VCH, :])
    for j in range(chunks):
        if j + 1 < chunks:
            following = nt(final[...], table[(j + 1) * VCH : (j + 2) * VCH, :])
        now = jnp.max(logits, axis=1, keepdims=True)
        if j:
            now = jnp.maximum(top, now)
            shrink = jnp.exp(top - now)
        expo = jnp.exp(logits - now)
        part = jnp.sum(expo, axis=1, keepdims=True)
        total = total * shrink + part if j else part
        part = nn(expo.astype(BF16), table[j * VCH : (j + 1) * VCH, :])
        grad[...] = grad[...] * shrink + part if j else part
        top, logits = now, following
    mean = grad[...] * (1.0 / total)
    log_sum = top + jnp.log(total)
    for out, at in ((own, slice(0, HALF)), (other, slice(HALF, LENGTH))):
        body, tail = with_stat(mean[at, :], log_sum[at, :])
        out[:, 0:D] = body
        out[:, D:EXT] = tail


def vocabulary(f_own, f_other, table):
    return call(
        vocab_body,
        (shaped((HALF, EXT), BF16),) * 2,
        [WHOLE] * 3,
        (pltpu.VMEM((LENGTH, D), BF16), pltpu.VMEM((LENGTH, D), F32)),
        limit=16,
        name="logits_and_gradient",
        flops=4 * LENGTH * D * SHARD,
        moved=SHARD * D * 2,
    )(f_own, f_other, table)


def merged(refs):
    stats = [stat_of(r) for r in refs]
    top = stats[0]
    for s in stats[1:]:
        top = jnp.maximum(top, s)
    weights = [jnp.exp(s - top) for s in stats]
    total = sum(weights[1:], weights[0])
    mean = sum((w * r[:, 0:D].astype(F32) for w, r in zip(weights[1:], refs[1:])), weights[0] * refs[0][:, 0:D].astype(F32))
    return mean * (1.0 / total), top + jnp.log(total)


def merge_body(idx, own, other, o0, o1, o2, o3, held):
    mean, log_total = merged((own, other))
    body, tail = with_stat(mean, log_total)
    held[:, 0:D] = body
    held[:, D:EXT] = tail
    for k, out in enumerate((o0, o1, o2, o3)):
        out[...] = held[pl.ds(pl.multiple_of(lax.rem(idx[2] + k, 4) * PART, PART), PART), :]


def merge(idx, own, other):
    return call(
        merge_body,
        (shaped((PART, EXT), BF16),) * 4,
        [SCALARS] + [WHOLE] * 2,
        (pltpu.VMEM((HALF, EXT), BF16),),
        limit=8,
        name="merge_two_cores",
        moved=900000,
    )(idx, own, other)


def prepare_body(query, stats, prefix_kv, probs, value_rows, ones_rows, key_rows):
    left = lanes((PRE, 128)) < HEAD_DIM
    zero = jnp.zeros((PRE, 128), BF16)
    for ref in (key_rows, value_rows, ones_rows):
        ref[...] = jnp.zeros_like(ref)
    one = jnp.ones((PRE, 128), BF16)
    for pair in range(HEADS // 2):
        at = slice(pair * 128, (pair + 1) * 128)
        up = slice(2 * pair * PRE, (2 * pair + 1) * PRE)
        down = slice((2 * pair + 1) * PRE, (2 * pair + 2) * PRE)
        for ref, value in (
            (key_rows, prefix_kv[:, at]),
            (value_rows, prefix_kv[:, D + pair * 128 : D + (pair + 1) * 128]),
            (ones_rows, one),
        ):
            ref[up, at] = jnp.where(left, value, zero)
            ref[down, at] = jnp.where(left, zero, value)
    of_head = (lanes((128, HEADS * PRE)) // PRE == rows((128, HEADS * PRE))).astype(BF16)
    high, middle, low = three_way(stats[:, 0:128])
    logs = nn(jnp.concatenate([high, middle, low], axis=0).astype(BF16), of_head)
    logs = logs[0:PART] + (logs[PART : 2 * PART] + logs[2 * PART : 3 * PART])
    lane = lanes((PART, HEADS * PRE))
    live = lane - (lane // PRE) * PRE < PREFIX
    q = query[...]
    probs[...] = jnp.where(live, jnp.exp(nt(q, key_rows[...]) - logs), 0.0)


def prepare(query, stats, prefix_kv):
    wide = shaped((HEADS * PRE, D), BF16)
    return call(
        prepare_body,
        (shaped((PART, HEADS * PRE)), wide, wide),
        [WHOLE] * 3,
        (pltpu.VMEM((HEADS * PRE, D), BF16),),
        limit=8,
        name="prepare_backward",
        moved=3000000,
    )(query, stats, prefix_kv)


def finely(left, right):
    size = left.shape[0]
    both = nt(jnp.concatenate(two_way(left), axis=0), right)
    return both[0:size] + both[size : 2 * size]


def backward_body(
    idx, extra, p0, p1, p2, p3, attended, last, inner, mixed, query, target, stats, probs_in, value_rows, ones_rows, norms, w_out, w_fc, w_fc_out,
    own, other, result,
):
    mean, log_total = merged((p0, p1, p2, p3))
    counted = stats[:, 129:130]
    loss = jnp.sum((log_total - stats[:, 128:129]) * counted, axis=0, keepdims=True)
    scale = counted * (1.0 / jnp.sum(extra[15:16, :], axis=1, keepdims=True))
    exact = (jnp.exp(stats[:, 128:129] - log_total) - 1.0) * scale
    grad = mean * scale - target[...] * (scale + exact - exact.astype(BF16).astype(F32))
    grad_x = norm_back(last[...], norms[2, 0:1, :], grad)
    grad_normed = jnp.zeros((PART, D), F32)
    for j in range(4):
        u = inner[:, j * FCH : (j + 1) * FCH]
        bend = jnp.tanh(GELU_K * (u + GELU_C * u * u * u))
        slope = 0.5 * (1.0 + bend) + 0.5 * u * (1.0 - bend * bend) * (GELU_K * (1.0 + 3.0 * GELU_C * u * u))
        grad_u = finely(grad_x, w_fc_out[0, j * FCH : (j + 1) * FCH, :]) * slope
        grad_normed = grad_normed + finely(grad_u, w_fc[0, :, j * FCH : (j + 1) * FCH])
    grad_h = grad_x + norm_back(attended[...], norms[1, 0:1, :], grad_normed)
    grad_mixed = finely(grad_h, w_out[0])

    q = query[...]
    probs = probs_in[...]
    grad_probs = finely(grad_mixed, value_rows[...])
    inner_sum = finely(grad_mixed * mixed[...], ones_rows[...])
    grad_scores = jnp.concatenate(two_way(probs * (grad_probs - inner_sum)), axis=0)
    left = lanes((PRE, 128)) < HEAD_DIM
    grad_keys = tn(grad_scores, jnp.concatenate([q, q], axis=0))
    probs = probs.astype(BF16)
    grad_values = tn(jnp.concatenate([probs, probs], axis=0), jnp.concatenate(two_way(grad_mixed), axis=0))
    for side, value in enumerate((grad_keys, grad_values)):
        parts = []
        for pair in range(HEADS // 2):
            at = slice(pair * 128, (pair + 1) * 128)
            up = value[2 * pair * PRE : (2 * pair + 1) * PRE, at]
            parts.append(jnp.where(left, up, value[(2 * pair + 1) * PRE : (2 * pair + 2) * PRE, at]))
        folded = jnp.concatenate(parts, axis=1)
        result[:, side * D : (side + 1) * D] = folded[0:8, :]
        for r in range(2):
            for k in range(2):
                result[4 * r + 2 * side + k : 4 * r + 2 * side + k + 1, KVW : KVW + 512] = folded[
                    8 + r : 9 + r, k * 512 : (k + 1) * 512
                ]
    lane = lanes((8, 256))
    result[:, KVW + 512 : FLAT] = jnp.where((lane == 0) & (rows((8, 256)) == 0), loss, 0.0)
    left, right = result[:, 0:SIDE], result[:, SIDE:FLAT]
    own[...] = jnp.where(idx[3] == 0, left, right)
    other[...] = jnp.where(idx[3] == 0, right, left)


def backward(idx, *inputs):
    return call(
        backward_body,
        (shaped((8, SIDE)), shaped((8, SIDE))),
        [SCALARS] + [WHOLE] * len(inputs),
        (pltpu.VMEM((8, FLAT), F32),),
        limit=10,
        name="backward_to_prefix",
        flops=2 * PART * D * 9 * D,
        moved=20000000,
    )(idx, *inputs)


def send_body(idx, a, b, c, d, out):
    total = (a[...] + b[...]) + (c[...] + d[...])
    tail = total[:, SIDE - 256 : SIDE]
    high, middle, low = three_way(tail[:, 0:1])
    lane = lanes((8, 256))
    pieces = jnp.where(lane == 0, high, jnp.where(lane == 1, middle, jnp.where(lane == 2, low, 0.0)))
    tail = jnp.where(idx[3] == 1, pieces, tail)
    total = jnp.concatenate([total[:, 0 : SIDE - 256], tail], axis=1).astype(BF16)
    out[...] = jnp.broadcast_to(total[None], out.shape)


def copies_to_send(idx, pieces):
    return call(
        send_body,
        shaped((16, 8, SIDE), BF16),
        [SCALARS] + [WHOLE] * 4,
        limit=8,
        name="sum_to_send",
        moved=600000,
    )(idx, *pieces)


def adam(weight, grad, first, second):
    first = BETA_ONE * first + (1.0 - BETA_ONE) * grad
    second = BETA_TWO * second + (1.0 - BETA_TWO) * grad * grad
    move = first / (1.0 - BETA_ONE**STEP) / (jnp.sqrt(second / (1.0 - BETA_TWO**STEP)) + ADAM_EPS)
    return weight - RATE * (move + DECAY * weight), first, second


def total_of(value):
    return jnp.sum(jnp.sum(value, axis=1, keepdims=True), axis=0, keepdims=True)


def received_body(pieces, out):
    total = pieces[0].astype(F32)
    for k in range(1, 16):
        total = total + pieces[k].astype(F32)
    out[...] = total


def received(pieces):
    return call(received_body, shaped((8, SIDE)), [WHOLE], limit=8, name="sum_received", moved=400000)(pieces)


def update_body(idx, side_own, side_other, net_own, net_other, prefix, extra, *refs):
    away, refs = refs[:12], refs[12:]
    (loss, count, norm), outs, refs = refs[:3], refs[3:15], refs[15:]
    held, (columns, sems) = refs[:12], refs[12:]
    copies = [pltpu.make_async_copy(a, b, sems.at[k]) for k, (a, b) in enumerate(zip(away, held))]
    for c in copies:
        c.start()
    place = idx[0] * 4 + idx[1]
    core = idx[3]

    def in_order(mine, theirs):
        return jnp.where(core == 0, mine, theirs), jnp.where(core == 0, theirs, mine)

    flat = jnp.concatenate(in_order(side_own[...], side_other[...]), axis=1)
    loss[...] = jnp.sum(flat[0:1, KVW + 512 : FLAT], axis=1, keepdims=True)
    last = flat[:, KVW : KVW + 512]
    ends = [jnp.concatenate([last[4 * r + k : 4 * r + k + 1, :] for k in range(4)], axis=1) for r in range(2)]
    states = jnp.concatenate([flat[:, 0:KVW], *ends, jnp.zeros((6, KVW), F32)], axis=0)
    columns[...] = states
    pre_weight = prefix[...]

    def back(net):
        hid = net[NET_HID : NET_HID + PRE, :].astype(F32) + net[NET_HID + PRE : NET, :].astype(F32)
        grad = three_products(nn, states, net[0:KVW, :], net[KVW : 2 * KVW, :]) * (1.0 - hid * hid)
        sides = []
        for side in range(2):
            at = NET_IN + side * HALF_HID
            sides.append(
                three_products(nn, grad, net[at : at + HALF_HID, :], net[at + 2 * HALF_HID : at + 3 * HALF_HID, :])
            )
        return hid, grad, jnp.concatenate(sides, axis=1)

    hid_own, grad_own, first = back(net_own)
    hid_other, grad_other, second = back(net_other)
    grad_prefix = first + second
    grad_pre = jnp.concatenate(in_order(grad_own, grad_other), axis=1)
    hid = jnp.concatenate(in_order(hid_own, hid_other), axis=1)
    biases = jnp.sum(grad_pre, axis=0, keepdims=True)
    biases = jnp.concatenate(
        [by_units(biases[:, 0:HALF_HID], biases[:, HALF_HID:PHID]), jnp.sum(states, axis=0, keepdims=True)], axis=1
    )
    squares = (
        total_of(grad_prefix * grad_prefix)
        + total_of(gram(pre_weight) * gram(grad_pre))
        + total_of(gram(hid) * gram(states))
        + total_of(biases * biases)
    )
    size = jnp.sqrt(squares)
    factor = jnp.minimum(1.0, CLIP / (size + 1e-06))
    count[...] = jnp.sum(extra[15:16, :], axis=1, keepdims=True)
    norm[...] = size

    own = pltpu.roll(grad_prefix, lax.rem(PHID - place * 32, PHID), 1)[0:PREFIX, 0:32]
    back_by = lax.rem(HALF_HID - place * UNITS, HALF_HID)
    sides = [pltpu.roll(grad_pre[:, at : at + HALF_HID], back_by, 1)[:, 0:UNITS] for at in (0, HALF_HID)]
    grad_in = outer(jnp.concatenate(sides, axis=1), pre_weight)
    grad_out = outer(hid, columns[:, pl.ds(pl.multiple_of(place * 128, 128), 128)])
    parts = []
    for d in range(16):
        parts += [grad_out[at + d * UNITS : at + (d + 1) * UNITS, :] for at in (0, HALF_HID)]
    grad_out = jnp.concatenate(parts, axis=0)
    turned = jnp.broadcast_to(biases, (8, 5 * PHID))
    turned = pltpu.roll(turned, lax.rem(5 * PHID - place * 160, 5 * PHID), 1)[0:1, 0:160]
    for c in copies:
        c.wait()
    for k, grad in enumerate((own, grad_in, grad_out, turned)):
        new = adam(held[k][...], grad * factor, held[4 + k][...], held[8 + k][...])
        for j in range(3):
            outs[4 * j + k][...] = new[j]


def update(idx, network, weights, firsts, seconds):
    sizes = [shaped(w.shape) for w in weights]
    one = shaped((1, 1))
    away = (*weights, *firsts, *seconds)
    return call(
        update_body,
        (one, one, one, *sizes, *sizes, *sizes),
        [SCALARS] + [WHOLE] * len(network) + [REMAIN] * 12,
        (*(pltpu.VMEM(w.shape, F32) for w in away), pltpu.VMEM((PRE, KVW), F32), pltpu.SemaphoreType.DMA((12,))),
        limit=16,
        name="clip_and_update",
        moved=6000000,
    )(idx, *network, *(in_hbm(w) for w in away))


def from_behind(value, axis, k):
    return lax.ppermute(value, axis, [(i, (i + k) % 4) for i in range(4)])


def around(value, axis):
    return (value, *(from_behind(value, axis, k) for k in (1, 2, 3)))


def scattered(values, axis):
    return (values[0], *(from_behind(values[k], axis, k) for k in (1, 2, 3)))


def crossed(value, late):
    got = [value]
    for k in (1, 2, 3):
        pairs = []
        for z in range(4):
            for y in range(4):
                for core in range(2):
                    to = (z, (y + k) % 4) if (core == 0) != late else ((z + k) % 4, y)
                    pairs.append(((z * 4 + y) * 2 + core, (to[0] * 4 + to[1]) * 2 + core))
        got.append(lax.ppermute(value, ("z", "y", "core"), pairs))
    return got


def summed_over_x(value):
    for late in range(2):
        pairs = [(2 * i + core, 2 * (i ^ (3 if core ^ late else 1)) + core) for i in range(4) for core in range(2)]
        value = value + lax.ppermute(value, ("x", "core"), pairs)
    return value


def swapped(value):
    return lax.ppermute(value, "core", [(0, 1), (1, 0)])


def on_device(
    tokens,
    segments,
    valid,
    embedding,
    positions_table,
    w_qkv,
    w_attn_out,
    w_fc,
    w_fc_out,
    layer_bias,
    norm_params,
    prefix,
    prefix_in,
    prefix_out,
    prefix_bias,
    moment_prefix,
    moment_in,
    moment_out,
    moment_bias,
    square_prefix,
    square_in,
    square_out,
    square_bias,
):
    idx = jnp.stack([lax.axis_index(a) for a in ("z", "y", "x", "core")]).astype(jnp.int32)
    bias_row = prefix_bias.reshape(1, -1)

    packed = pack(idx, prefix_in.T, prefix_out, prefix, bias_row, segments, valid)
    packed, tokens = lax.optimization_barrier((packed, tokens))
    packed = crossed(packed.astype(jnp.float16), False)
    own, other = token_rows(idx, tokens, embedding)
    other, packed = lax.optimization_barrier((other, packed))
    embedded, packed = lax.optimization_barrier((own + swapped(other), packed))
    embedded = summed_over_x(embedded)
    packed = crossed(stack(packed), True)
    x, query, keyval = projections(idx, embedded, *bring(positions_table, norm_params, layer_bias, w_qkv))
    keyval, packed = lax.optimization_barrier((keyval, packed))
    packed = [p.astype(F32) for p in packed]
    net, prefix_all, extra, states = prefix_states(idx, packed)
    final, *kept = layer(
        idx, query, keyval, swapped(keyval), embedded, x, states, swapped(states), extra, segments, valid,
        norm_params, layer_bias, w_attn_out, w_fc, w_fc_out,
    )
    final_other, net = lax.optimization_barrier((swapped(final), net))
    own, other = vocabulary(final, final_other, embedding)
    own, net_other = lax.optimization_barrier((own, swapped(net)))
    pieces = scattered(merge(idx, own, swapped(other)), "x")
    *kept, prefix_kv = kept
    own, other = backward(idx, extra, *pieces, *kept, *prepare(kept[4], kept[6], prefix_kv), norm_params, w_attn_out, w_fc, w_fc_out)
    grad = copies_to_send(idx, around(own + swapped(other), "x"))
    grad = lax.all_to_all(grad, ("z", "y"), 0, 0, tiled=True)
    grad = received(grad)
    outs = update(
        idx, (grad, swapped(grad), net, net_other, prefix_all, extra),
        (prefix, prefix_in.T, prefix_out, bias_row),
        (moment_prefix, moment_in.T, moment_out, moment_bias.reshape(1, -1)),
        (square_prefix, square_in.T, square_out, square_bias.reshape(1, -1)),
    )
    outs = list(outs)
    for k in range(3):
        outs[k] = outs[k].reshape(())
        outs[4 + 4 * k] = outs[4 + 4 * k].T
        outs[6 + 4 * k] = outs[6 + 4 * k].reshape(-1)
    return tuple(outs)


def solution(mesh):
    split = Mesh(mesh.devices.reshape(4, 4, 4, 2), ("z", "y", "x", "core"))
    dp = ("z", "y")
    sharded = (P(None, dp), P(None, dp), P(None, dp), P(dp))
    placed = (
        P(dp, None),
        P(dp, None),
        P(dp, None),
        P(("x", "core"), None),
        *([P()] * 7),
        *sharded,
        *sharded,
        *sharded,
    )
    return jax.shard_map(
        on_device,
        mesh=split,
        in_specs=placed,
        out_specs=(P(), P(), P(), *sharded, *sharded, *sharded),
        check_vma=False,
    )
```

```python
import jax
import jax.numpy as jnp
from jax import lax
from jax.experimental import pallas as pl
from jax.experimental.pallas import tpu as pltpu
from jax.sharding import Mesh
from jax.sharding import PartitionSpec as P

D = 1024
HEADS = 16
HEAD_DIM = 64
FF = 4096
VOCAB = 51200
PREFIX = 10
PHID = 512
LENGTH = 256
STEP = 10
KVW = 2048
HALF = 128
PART = 32
SHARD = VOCAB // 8
PRE = 16
EXT = D + 128
FLAT = KVW + 768
SIDE = FLAT // 2

NORM_EPS = 1e-05
BETA_ONE = 0.9
BETA_TWO = 0.999
ADAM_EPS = 1e-08
RATE = 0.1
DECAY = 0.01
CLIP = 0.001
MASKED = -1e30
SCALE = HEAD_DIM**-0.5
GELU_K = 0.7978845608028654
GELU_C = 0.044715

HIGH = lax.Precision.HIGHEST
F32 = jnp.float32
BF16 = jnp.bfloat16
MIB = 1 << 20

WHOLE = pl.BlockSpec(memory_space=pltpu.VMEM)
SCALARS = pl.BlockSpec(memory_space=pltpu.SMEM)
REMAIN = pl.BlockSpec(memory_space=pl.ANY)


def nn(a, b, precision=None):
    return lax.dot_general(a, b, (((1,), (0,)), ((), ())), precision=precision, preferred_element_type=F32)


def nt(a, b, precision=None):
    return lax.dot_general(a, b, (((1,), (1,)), ((), ())), precision=precision, preferred_element_type=F32)


def tn(a, b, precision=None):
    return lax.dot_general(a, b, (((0,), (0,)), ((), ())), precision=precision, preferred_element_type=F32)


def lanes(shape):
    return lax.broadcasted_iota(jnp.int32, shape, len(shape) - 1)


def rows(shape):
    return lax.broadcasted_iota(jnp.int32, shape, 0)


def call(body, outs, ins, scratch=(), limit=48, name=None, flops=0, moved=0):
    return pl.pallas_call(
        body,
        out_shape=outs,
        in_specs=ins,
        out_specs=jax.tree.map(lambda _: WHOLE, outs),
        scratch_shapes=scratch,
        compiler_params=pltpu.CompilerParams(vmem_limit_bytes=limit * MIB),
        cost_estimate=pl.CostEstimate(flops=flops, bytes_accessed=moved, transcendentals=0),
        name=name,
    )


def shaped(shape, dtype=F32):
    return jax.ShapeDtypeStruct(shape, dtype)


def normalised(value):
    mean = jnp.mean(value, axis=-1, keepdims=True)
    centred = value - mean
    spread = jnp.mean(centred * centred, axis=-1, keepdims=True)
    inverse = lax.rsqrt(spread + NORM_EPS)
    return centred * inverse, inverse


def norm_back(value, gain, grad):
    unit, inverse = normalised(value)
    scaled = grad * gain
    first = jnp.mean(scaled, axis=-1, keepdims=True)
    second = jnp.mean(scaled * unit, axis=-1, keepdims=True)
    return inverse * (scaled - first - unit * second)


def three_way(value):
    high = value.astype(BF16).astype(F32)
    rest = value - high
    middle = rest.astype(BF16).astype(F32)
    return high, middle, rest - middle


def with_stat(body, stat):
    high, middle, low = three_way(stat)
    lane = lanes((body.shape[0], 128))
    tail = jnp.where(lane == 0, high, jnp.where(lane == 1, middle, jnp.where(lane == 2, low, 0.0)))
    return body.astype(BF16), tail.astype(BF16)


def stat_of(ref):
    tail = ref[:, D:EXT].astype(F32)
    return jnp.sum(jnp.where(lanes(tail.shape) < 3, tail, 0.0), axis=1, keepdims=True)


UNITS = 16
HALF_HID = PHID // 2
COLS = 64
OWN = UNITS + COLS
SMALL = 32
PACK = OWN + SMALL
TALL = 4 * OWN + SMALL


def two_way(value):
    high = value.astype(BF16)
    return high, (value - high.astype(F32)).astype(BF16)


def placed(value, width, start):
    wide = jnp.concatenate([value, jnp.zeros((value.shape[0], width - value.shape[1]), F32)], axis=1)
    return pltpu.roll(wide, start, 1)


def in_hbm(value):
    return pltpu.with_memory_space_constraint(value, pltpu.HBM)


def stack(pieces):
    small = (pieces[0][OWN:] + pieces[1][OWN:]) + (pieces[2][OWN:] + pieces[3][OWN:])
    return jnp.concatenate([*(p[:OWN] for p in pieces), small], axis=0)


NET_IN = 2 * KVW
NET_HID = NET_IN + 4 * HALF_HID
NET = NET_HID + 2 * PRE


def by_units(first, second):
    parts = []
    for d in range(16):
        at = slice(d * UNITS, (d + 1) * UNITS)
        parts += [first[:, at], second[:, at]]
    return jnp.concatenate(parts, axis=1)


def three_products(product, left, right_high, right_low):
    high, low = two_way(left)
    size = left.shape[0]
    both = product(jnp.concatenate([high, low], axis=0), right_high)
    return both[0:size] + (both[size : 2 * size] + product(high, right_low))


def gram(value):
    high, low = two_way(value)
    size = value.shape[0]
    both = jnp.concatenate([high, low], axis=0)
    both = nt(both, both)
    return both[0:size, 0:size] + (both[0:size, size:] + both[size:, 0:size])


def outer(left, right):
    left_high, left_low = two_way(left)
    high, low = two_way(right)
    return tn(jnp.concatenate([left_high, left_low, left_high], axis=0), jnp.concatenate([high, high, low], axis=0))


def states_body(idx, a, b, c, d, net, weight, extra, part, in_t, out_t):
    z, y, core = idx[0], idx[1], idx[3]
    pieces = (a, b, c, d)
    for late in range(4):
        for early in range(4):
            dz = jnp.where(core == 0, late, early)
            dy = jnp.where(core == 0, early, late)
            place = lax.rem(z + 4 - dz, 4) * 4 + lax.rem(y + 4 - dy, 4)
            at = early * OWN
            in_t[pl.ds(pl.multiple_of(place * UNITS, UNITS), UNITS), :] = pieces[late][at : at + UNITS, :]
            for side in range(2):
                to = pl.ds(pl.multiple_of(place * 128 + side * COLS, COLS), COLS)
                out_t[to, :] = pieces[late][at + UNITS : at + OWN, side * HALF_HID : (side + 1) * HALF_HID]
    rest = sum((r[4 * OWN : TALL, :] for r in pieces[1:]), a[4 * OWN : TALL, :])
    rest = rest[0:16, :] + rest[16:32, :]
    extra[...] = rest
    whole = jnp.where(rows((PRE, PHID)) < PREFIX, rest, 0.0)
    weight[...] = whole
    bias = rest[PREFIX : PREFIX + 1, :]
    bias = jnp.where(core == 0, bias, pltpu.roll(bias, PHID - UNITS, 1))
    bias = jnp.concatenate([bias[:, 32 * k : 32 * k + UNITS] for k in range(16)], axis=1)
    high, low = two_way(in_t[...])
    pre = three_products(nt, whole, high, low) + bias
    hid = jnp.where(rows(pre.shape) < PREFIX, jnp.tanh(pre), 0.0)
    for k, piece in enumerate((high, low)):
        at = NET_IN + 2 * k * HALF_HID
        net[at : at + HALF_HID, :] = piece[:, 0:HALF_HID]
        net[at + HALF_HID : at + 2 * HALF_HID, :] = piece[:, HALF_HID:PHID]
    net[NET_HID : NET_HID + PRE, :], net[NET_HID + PRE : NET, :] = two_way(hid)
    high, low = two_way(out_t[...])
    net[0:KVW, :] = high
    net[KVW : 2 * KVW, :] = low
    part[...] = three_products(nt, hid, high, low)


def prefix_states(idx, pieces):
    return call(
        states_body,
        (shaped((NET, HALF_HID), BF16), shaped((PRE, PHID)), shaped((PRE, PHID)), shaped((PRE, KVW))),
        [SCALARS] + [WHOLE] * 4,
        (pltpu.VMEM((HALF_HID, PHID), F32), pltpu.VMEM((KVW, HALF_HID), F32)),
        limit=12,
        name="prefix_states",
        moved=7000000,
    )(idx, *pieces)


AHEAD = 64


def pack_into(out, small, place, core, weight_in, weight_out, weight, bias, segments, valid):
    out[0:UNITS, :] = weight_in[pl.ds(pl.multiple_of(core * UNITS, UNITS), UNITS), :]
    own = [
        jnp.where(core == 0, weight_out[32 * d : 32 * d + UNITS, :], weight_out[32 * d + UNITS : 32 * d + 32, :])
        for d in range(16)
    ]
    turned = jnp.transpose(jnp.concatenate(own, axis=0))
    out[UNITS:OWN, 0:HALF_HID] = turned[0:COLS, :]
    out[UNITS:OWN, HALF_HID:PHID] = turned[COLS:128, :]
    whole = jnp.concatenate([weight[...], jnp.zeros((16 - PREFIX, 32), F32)], axis=0)
    small[...] = placed(whole, PHID, place * 32)
    flat = placed(jnp.broadcast_to(bias[...], (8, 160)), 5 * PHID, place * 160)
    for r in range(5):
        small[PREFIX + r : PREFIX + r + 1, :] = flat[0:1, r * PHID : (r + 1) * PHID]
    seg = segments[...]
    after = jnp.concatenate([seg[:, 1:], seg[:, :1]], axis=1)
    kept = (valid[...] > 0) & (lanes(seg.shape) < LENGTH - 1) & (after == seg)
    total = jnp.sum(kept.astype(F32), axis=1, keepdims=True)
    small[15:16, :] = jnp.where(lanes((1, PHID)) == place, total, 0.0)
    high = small[...].astype(BF16).astype(F32)
    out[OWN : OWN + 16, :] = high
    out[OWN + 16 : PACK, :] = small[...] - high


def rows_body(idx, tokens_at, table, *refs):
    away, (packed, own, other), refs = refs[:6], refs[6:9], refs[9:]
    taken, refs = refs[:6], refs[6:]
    small, block, held, tokens, found, locals_, sems = refs
    core = idx[3]
    first = (idx[2] * 2 + core) * SHARD
    fetch = pltpu.make_async_copy(tokens_at, tokens, sems.at[AHEAD])
    fetch.start()
    copies = [pltpu.make_async_copy(a, b, sems.at[AHEAD + 1 + k]) for k, (a, b) in enumerate(zip(away, taken))]
    for c in copies:
        c.start()
    held[...] = jnp.zeros_like(held)
    fetch.wait()

    def find(p, n):
        local = tokens[0, p] - first
        found[n] = p
        locals_[n] = local
        return n + ((local >= 0) & (local < SHARD)).astype(jnp.int32)

    number = lax.fori_loop(0, LENGTH, find, 0, unroll=16)
    for k in range(4):
        found[number + k] = LENGTH
        locals_[number + k] = 0
    number = (number + 3) // 4

    def copy(n):
        at = pl.multiple_of((locals_[n] // 16) * 16, 16)
        slot = lax.rem(n, AHEAD)
        return pltpu.make_async_copy(table.at[pl.ds(at, 16), :], block.at[slot], sems.at[slot])

    def begin(i, carry):
        for k in range(4):
            copy(4 * i + k).start()
        return carry

    def take(i, carry):
        for k in range(4):
            copy(4 * i + k).wait()
        lines = []
        for k in range(4):
            n = 4 * i + k
            got = block[lax.rem(n, AHEAD)].astype(F32)
            row = lax.rem(locals_[n], 16)
            lines.append(jnp.sum(jnp.where(rows((16, D)) == row, got, 0.0), axis=0, keepdims=True))
        for k in range(4):
            held[pl.ds(found[4 * i + k], 1), :] = lines[k]
        return carry

    for batch in range(LENGTH // AHEAD):
        low = jnp.minimum(number, batch * (AHEAD // 4))
        high = jnp.minimum(number, (batch + 1) * (AHEAD // 4))
        lax.fori_loop(low, high, begin, 0)
        if batch == 0:
            for c in copies:
                c.wait()
            pack_into(packed, small, idx[0] * 4 + idx[1], core, *taken)
        lax.fori_loop(low, high, take, 0)
    own[...] = held[pl.ds(pl.multiple_of(core * HALF, HALF), HALF), :].astype(BF16)
    other[...] = held[pl.ds(pl.multiple_of((1 - core) * HALF, HALF), HALF), :].astype(BF16)


def token_rows(idx, tokens, table, *network):
    return call(
        rows_body,
        (shaped((PACK, PHID)), shaped((HALF, D), BF16), shaped((HALF, D), BF16)),
        [SCALARS] + [REMAIN] * (2 + len(network)),
        (
            *(pltpu.VMEM(v.shape, v.dtype) for v in network),
            pltpu.VMEM((16, PHID), F32),
            pltpu.VMEM((AHEAD, 16, D), BF16),
            pltpu.VMEM((LENGTH + 8, D), F32),
            pltpu.SMEM((1, LENGTH), jnp.int32),
            pltpu.SMEM((LENGTH + 4,), jnp.int32),
            pltpu.SMEM((LENGTH + 4,), jnp.int32),
            pltpu.SemaphoreType.DMA((AHEAD + 1 + len(network),)),
        ),
        limit=10,
        name="token_rows_and_packed_weights",
        moved=9000000,
    )(idx, *(in_hbm(v) for v in (tokens, table, *network)))


def bring_body(*refs):
    half = len(refs) // 2
    sems = refs[-1]
    copies = [pltpu.make_async_copy(refs[k], refs[half + k], sems.at[k]) for k in range(half)]
    for c in copies:
        c.start()
    for c in copies:
        c.wait()


def bring(*inputs):
    return pl.pallas_call(
        bring_body,
        out_shape=tuple(pltpu.VMEM(v.shape, v.dtype) for v in inputs),
        in_specs=[REMAIN] * len(inputs),
        out_specs=tuple(REMAIN for _ in inputs),
        scratch_shapes=(pltpu.SemaphoreType.DMA((len(inputs),)),),
        compiler_params=pltpu.CompilerParams(vmem_limit_bytes=MIB),
        cost_estimate=pl.CostEstimate(flops=0, bytes_accessed=2 * sum(v.size * v.dtype.itemsize for v in inputs), transcendentals=0),
        name="bring_into_vmem",
    )(*(in_hbm(v) for v in inputs))


def qkv_body(idx, embedded, places, norms, bias, weight, x_out, query, keyval):
    core = idx[3]
    mine = embedded[...]
    x = mine.astype(F32) + places[pl.ds(pl.multiple_of(core * HALF, HALF), HALF), :].astype(F32)
    x_out[...] = x
    unit, _ = normalised(x)
    normed = (unit * norms[0, 0:1, :] + norms[0, 1:2, :]).astype(BF16)
    for j in range(6):
        at = slice(j * 512, (j + 1) * 512)
        part = nn(normed, weight[0, :, at]) + bias[:, at].astype(F32)
        if j < 2:
            query[:, at] = (part.astype(BF16).astype(F32) * SCALE).astype(BF16)
        else:
            keyval[0:HALF, (j - 2) * 512 : (j - 1) * 512] = part.astype(BF16)
    keyval[HALF : HALF + 16, 0:D] = mine[0:16, :]
    keyval[HALF : HALF + 16, D:KVW] = jnp.zeros((16, D), BF16)


def projections(idx, embedded, places, norms, bias, weight):
    return call(
        qkv_body,
        (shaped((HALF, D)), shaped((HALF, D), BF16), shaped((HALF + 16, KVW), BF16)),
        [SCALARS] + [WHOLE] * 5,
        limit=10,
        name="norm_and_projections",
        flops=2 * HALF * D * 3 * D,
        moved=9000000,
    )(idx, embedded, places, norms, bias, weight)


FCH = 1024


def by_heads(out, value, left):
    out[...] = jnp.zeros_like(out)
    zero = jnp.zeros((PRE, 128), BF16)
    for pair in range(HEADS // 2):
        at = slice(pair * 128, (pair + 1) * 128)
        out[2 * pair * PRE : (2 * pair + 1) * PRE, at] = jnp.where(left, value[:, at], zero)
        out[(2 * pair + 1) * PRE : (2 * pair + 2) * PRE, at] = jnp.where(left, zero, value[:, at])


def layer_body(
    idx, query, kv_own, kv_other, embedded, x_in, states_own, states_other, extra, segments, valid, norms, bias,
    w_out, w_fc, w_fc_out,
    final, attended_part, last_part, inner_part, mixed_part, query_part, target_part, stats_part, probs_part, value_rows,
    key_rows, mixed, keep, wide,
):
    xx, core = idx[2], idx[3]
    part = pl.ds(pl.multiple_of(xx * PART, PART), PART)
    shift = jnp.concatenate([extra[r : r + 1, :] for r in range(PREFIX + 1, PREFIX + 5)], axis=1)
    states = states_own[...] + states_other[...] + shift
    states = jnp.where(rows(states.shape) < PREFIX, states, 0.0).astype(BF16)
    left = lanes((PRE, 128)) < HEAD_DIM
    by_heads(key_rows, states[:, 0:D], left)
    by_heads(value_rows, states[:, D:KVW], left)

    seg = segments[...]
    mine = jnp.where(core == 0, seg[:, 0:HALF], seg[:, HALF:LENGTH])
    theirs = jnp.where(core == 0, seg[:, HALF:LENGTH], seg[:, 0:HALF])
    square = (HALF, HALF)
    mine_down = jnp.transpose(jnp.broadcast_to(mine, square))
    sees_own = (mine_down == jnp.broadcast_to(mine, square)) & (lanes(square) <= rows(square))
    sees_other = (mine_down == jnp.broadcast_to(theirs, square)) & (core == 1)
    hide = jnp.concatenate([jnp.where(m, 0.0, MASKED) for m in (sees_own, sees_other)], axis=1)
    hide = jnp.concatenate([hide, hide], axis=0)
    left = lanes(square) < HEAD_DIM
    ahead_scores = nt(query[...], key_rows[...])
    group = lanes(square) // PRE
    live = lanes(square) - group * PRE < PREFIX
    probs = [jnp.zeros(square, F32)] * 2
    for pair in range(HEADS // 2):
        at = slice(pair * 128, pair * 128 + 128)
        at_v = slice(D + pair * 128, D + pair * 128 + 128)
        q = query[:, at]
        zero = jnp.zeros_like(q)
        both = jnp.concatenate([jnp.where(left, q, zero), jnp.where(left, zero, q)], axis=0)
        keys = jnp.concatenate([kv_own[0:HALF, at], kv_other[0:HALF, at]], axis=0)
        values = jnp.concatenate([kv_own[0:HALF, at_v], kv_other[0:HALF, at_v]], axis=0)
        scores = nt(both, keys) + hide
        block = pair // 4
        mine = [live & (group == 2 * (pair % 4) + side) for side in range(2)]
        prefix = ahead_scores[:, block * 128 : (block + 1) * 128]
        prefix = jnp.concatenate([jnp.where(m, prefix, MASKED) for m in mine], axis=0)
        top = jnp.maximum(jnp.maximum(scores[:, 0:HALF], scores[:, HALF:LENGTH]), prefix)
        top = jnp.max(top, axis=1, keepdims=True)
        expo = jnp.exp(scores - top)
        expo_prefix = jnp.exp(prefix - top)
        total = jnp.sum(expo[:, 0:HALF] + expo[:, HALF:LENGTH] + expo_prefix, axis=1, keepdims=True)
        share = 1.0 / total
        out = nn((expo * share).astype(BF16), values)
        mixed[:, at] = jnp.where(left, out[0:HALF], out[HALF:])
        expo_prefix = expo_prefix * share
        probs[block] = probs[block] + (expo_prefix[0:HALF] + expo_prefix[HALF:])
    probs = jnp.concatenate(probs, axis=1)
    mixed[...] = mixed[...] + nn(probs.astype(BF16), value_rows[...])
    mixed_part[...] = mixed[part, :]
    query_part[...] = query[part, :]
    wide[:, 0 : HEADS * PRE] = probs
    probs_part[...] = wide[part, 0 : HEADS * PRE]

    x = x_in[...] + nn(mixed[...].astype(BF16), w_out[0]) + bias[:, 3 * D : 4 * D].astype(F32)
    keep[...] = x
    attended_part[...] = keep[part, :]
    unit, _ = normalised(x)
    normed = (unit * norms[1, 0:1, :] + norms[1, 1:2, :]).astype(BF16)
    x = x + bias[:, 4 * D + FF : 5 * D + FF].astype(F32)
    for j in range(4):
        inner = nn(normed, w_fc[0, :, j * FCH : (j + 1) * FCH]) + bias[:, 4 * D + j * FCH : 4 * D + (j + 1) * FCH].astype(F32)
        wide[...] = inner
        inner_part[:, j * FCH : (j + 1) * FCH] = wide[part, :]
        active = (0.5 * inner * (1.0 + jnp.tanh(GELU_K * (inner + GELU_C * inner * inner * inner)))).astype(BF16)
        x = x + nn(active, w_fc_out[0, j * FCH : (j + 1) * FCH, :])
    keep[...] = x
    last_part[...] = keep[part, :]
    unit, _ = normalised(x)
    result = (unit * norms[2, 0:1, :] + norms[2, 1:2, :]).astype(BF16)
    final[...] = result

    wide[...] = embedded[...].astype(F32)
    keep[...] = result.astype(F32)
    after = jnp.concatenate([wide[1:HALF, :], kv_other[HALF : HALF + 1, 0:D].astype(F32)], axis=0)
    wide[...] = after
    target = wide[part, :]
    target_part[...] = target
    picked = jnp.sum(keep[part, :] * target, axis=1, keepdims=True)
    following = jnp.concatenate([seg[:, 1:], seg[:, :1]], axis=1)
    kept = (valid[...] > 0) & (lanes(seg.shape) < LENGTH - 1) & (following == seg)
    kept = kept.astype(F32)
    counted = jnp.where(core == 0, kept[:, 0:HALF], kept[:, HALF:LENGTH])
    wide[:, 0:HALF] = jnp.transpose(jnp.broadcast_to(counted, square))
    lane = lanes((PART, 128))
    stats_part[...] = jnp.where(lane == 0, picked, jnp.where(lane == 1, wide[part, 0:128], 0.0))


def layer(idx, *inputs):
    return call(
        layer_body,
        (
            shaped((HALF, D), BF16),
            shaped((PART, D)),
            shaped((PART, D)),
            shaped((PART, FF)),
            shaped((PART, D)),
            shaped((PART, D), BF16),
            shaped((PART, D)),
            shaped((PART, 128)),
            shaped((PART, HEADS * PRE)),
            shaped((HEADS * PRE, D), BF16),
        ),
        [SCALARS] + [WHOLE] * len(inputs),
        (
            pltpu.VMEM((HEADS * PRE, D), BF16),
            pltpu.VMEM((HALF, D), F32),
            pltpu.VMEM((HALF, D), F32),
            pltpu.VMEM((HALF, FCH), F32),
        ),
        limit=10,
        name="attention_and_feed_forward",
        flops=2 * HALF * D * 9 * D,
        moved=22000000,
    )(idx, *inputs)


VCH = 1280


def vocab_body(f_own, f_other, table, own, other, final, grad):
    final[0:HALF, :] = f_own[...]
    final[HALF:LENGTH, :] = f_other[...]
    chunks = SHARD // VCH
    logits = nt(final[...], table[0:VCH, :])
    for j in range(chunks):
        if j + 1 < chunks:
            following = nt(final[...], table[(j + 1) * VCH : (j + 2) * VCH, :])
        now = jnp.max(logits, axis=1, keepdims=True)
        if j:
            now = jnp.maximum(top, now)
            shrink = jnp.exp(top - now)
        expo = jnp.exp(logits - now)
        part = jnp.sum(expo, axis=1, keepdims=True)
        total = total * shrink + part if j else part
        part = nn(expo.astype(BF16), table[j * VCH : (j + 1) * VCH, :])
        grad[...] = grad[...] * shrink + part if j else part
        top, logits = now, following
    mean = grad[...] * (1.0 / total)
    log_sum = top + jnp.log(total)
    for out, at in ((own, slice(0, HALF)), (other, slice(HALF, LENGTH))):
        body, tail = with_stat(mean[at, :], log_sum[at, :])
        out[:, 0:D] = body
        out[:, D:EXT] = tail


def vocabulary(f_own, f_other, table):
    return call(
        vocab_body,
        (shaped((HALF, EXT), BF16),) * 2,
        [WHOLE] * 3,
        (pltpu.VMEM((LENGTH, D), BF16), pltpu.VMEM((LENGTH, D), F32)),
        limit=16,
        name="logits_and_gradient",
        flops=4 * LENGTH * D * SHARD,
        moved=SHARD * D * 2,
    )(f_own, f_other, table)


def merged(refs):
    stats = [stat_of(r) for r in refs]
    top = stats[0]
    for s in stats[1:]:
        top = jnp.maximum(top, s)
    weights = [jnp.exp(s - top) for s in stats]
    total = sum(weights[1:], weights[0])
    mean = sum((w * r[:, 0:D].astype(F32) for w, r in zip(weights[1:], refs[1:])), weights[0] * refs[0][:, 0:D].astype(F32))
    return mean * (1.0 / total), top + jnp.log(total)


def merge_body(idx, own, other, o0, o1, o2, o3, held):
    mean, log_total = merged((own, other))
    body, tail = with_stat(mean, log_total)
    held[:, 0:D] = body
    held[:, D:EXT] = tail
    for k, out in enumerate((o0, o1, o2, o3)):
        out[...] = held[pl.ds(pl.multiple_of(lax.rem(idx[2] + k, 4) * PART, PART), PART), :]


def merge(idx, own, other):
    return call(
        merge_body,
        (shaped((PART, EXT), BF16),) * 4,
        [SCALARS] + [WHOLE] * 2,
        (pltpu.VMEM((HALF, EXT), BF16),),
        limit=8,
        name="merge_two_cores",
        moved=900000,
    )(idx, own, other)


def finely(left, right):
    size = left.shape[0]
    both = nt(jnp.concatenate(two_way(left), axis=0), right)
    return both[0:size] + both[size : 2 * size]


def backward_body(
    idx, extra, p0, p1, p2, p3, attended, last, inner, mixed, query, target, stats, probs_in, value_rows, norms, w_out, w_fc, w_fc_out,
    own, other, result, ones_rows,
):
    mean, log_total = merged((p0, p1, p2, p3))
    counted = stats[:, 1:2]
    loss = jnp.sum((log_total - stats[:, 0:1]) * counted, axis=0, keepdims=True)
    scale = counted * (1.0 / jnp.sum(extra[15:16, :], axis=1, keepdims=True))
    exact = (jnp.exp(stats[:, 0:1] - log_total) - 1.0) * scale
    grad = mean * scale - target[...] * (scale + exact - exact.astype(BF16).astype(F32))
    grad_x = norm_back(last[...], norms[2, 0:1, :], grad)
    grad_normed = jnp.zeros((PART, D), F32)
    for j in range(4):
        u = inner[:, j * FCH : (j + 1) * FCH]
        bend = jnp.tanh(GELU_K * (u + GELU_C * u * u * u))
        slope = 0.5 * (1.0 + bend) + 0.5 * u * (1.0 - bend * bend) * (GELU_K * (1.0 + 3.0 * GELU_C * u * u))
        grad_u = finely(grad_x, w_fc_out[0, j * FCH : (j + 1) * FCH, :]) * slope
        grad_normed = grad_normed + finely(grad_u, w_fc[0, :, j * FCH : (j + 1) * FCH])
    grad_h = grad_x + norm_back(attended[...], norms[1, 0:1, :], grad_normed)
    grad_mixed = finely(grad_h, w_out[0])

    left = lanes((PRE, 128)) < HEAD_DIM
    by_heads(ones_rows, jnp.ones((PRE, D), BF16), left)
    q = query[...]
    probs = probs_in[...]
    grad_probs = finely(grad_mixed, value_rows[...])
    inner_sum = finely(grad_mixed * mixed[...], ones_rows[...])
    grad_scores = jnp.concatenate(two_way(probs * (grad_probs - inner_sum)), axis=0)
    grad_keys = tn(grad_scores, jnp.concatenate([q, q], axis=0))
    probs = probs.astype(BF16)
    grad_values = tn(jnp.concatenate([probs, probs], axis=0), jnp.concatenate(two_way(grad_mixed), axis=0))
    for side, value in enumerate((grad_keys, grad_values)):
        parts = []
        for pair in range(HEADS // 2):
            at = slice(pair * 128, (pair + 1) * 128)
            up = value[2 * pair * PRE : (2 * pair + 1) * PRE, at]
            parts.append(jnp.where(left, up, value[(2 * pair + 1) * PRE : (2 * pair + 2) * PRE, at]))
        folded = jnp.concatenate(parts, axis=1)
        result[:, side * D : (side + 1) * D] = folded[0:8, :]
        for r in range(2):
            for k in range(2):
                result[4 * r + 2 * side + k : 4 * r + 2 * side + k + 1, KVW : KVW + 512] = folded[
                    8 + r : 9 + r, k * 512 : (k + 1) * 512
                ]
    lane = lanes((8, 256))
    result[:, KVW + 512 : FLAT] = jnp.where((lane == 0) & (rows((8, 256)) == 0), loss, 0.0)
    left, right = result[:, 0:SIDE], result[:, SIDE:FLAT]
    own[...] = jnp.where(idx[3] == 0, left, right)
    other[...] = jnp.where(idx[3] == 0, right, left)


def backward(idx, *inputs):
    return call(
        backward_body,
        (shaped((8, SIDE)), shaped((8, SIDE))),
        [SCALARS] + [WHOLE] * len(inputs),
        (pltpu.VMEM((8, FLAT), F32), pltpu.VMEM((HEADS * PRE, D), BF16)),
        limit=10,
        name="backward_to_prefix",
        flops=2 * PART * D * 9 * D,
        moved=20000000,
    )(idx, *inputs)


def send_body(idx, a, b, c, d, out):
    total = (a[...] + b[...]) + (c[...] + d[...])
    tail = total[:, SIDE - 256 : SIDE]
    high, middle, low = three_way(tail[:, 0:1])
    lane = lanes((8, 256))
    pieces = jnp.where(lane == 0, high, jnp.where(lane == 1, middle, jnp.where(lane == 2, low, 0.0)))
    tail = jnp.where(idx[3] == 1, pieces, tail)
    total = jnp.concatenate([total[:, 0 : SIDE - 256], tail], axis=1).astype(BF16)
    out[...] = jnp.broadcast_to(total[None], out.shape)


def copies_to_send(idx, pieces):
    return call(
        send_body,
        shaped((16, 8, SIDE), BF16),
        [SCALARS] + [WHOLE] * 4,
        limit=8,
        name="sum_to_send",
        moved=600000,
    )(idx, *pieces)


def adam(weight, grad, first, second):
    first = BETA_ONE * first + (1.0 - BETA_ONE) * grad
    second = BETA_TWO * second + (1.0 - BETA_TWO) * grad * grad
    move = first / (1.0 - BETA_ONE**STEP) / (jnp.sqrt(second / (1.0 - BETA_TWO**STEP)) + ADAM_EPS)
    return weight - RATE * (move + DECAY * weight), first, second


def total_of(value):
    return jnp.sum(jnp.sum(value, axis=1, keepdims=True), axis=0, keepdims=True)


def received_body(pieces, out):
    total = pieces[0].astype(F32)
    for k in range(1, 16):
        total = total + pieces[k].astype(F32)
    out[...] = total


def received(pieces):
    return call(received_body, shaped((8, SIDE)), [WHOLE], limit=8, name="sum_received", moved=400000)(pieces)


def update_body(idx, side_own, side_other, net_own, net_other, prefix, extra, *refs):
    away, refs = refs[:12], refs[12:]
    (loss, count, norm), outs, refs = refs[:3], refs[3:15], refs[15:]
    held, (columns, sems) = refs[:12], refs[12:]
    copies = [pltpu.make_async_copy(a, b, sems.at[k]) for k, (a, b) in enumerate(zip(away, held))]
    for c in copies:
        c.start()
    place = idx[0] * 4 + idx[1]
    core = idx[3]

    def in_order(mine, theirs):
        return jnp.where(core == 0, mine, theirs), jnp.where(core == 0, theirs, mine)

    flat = jnp.concatenate(in_order(side_own[...], side_other[...]), axis=1)
    loss[...] = jnp.sum(flat[0:1, KVW + 512 : FLAT], axis=1, keepdims=True)
    last = flat[:, KVW : KVW + 512]
    ends = [jnp.concatenate([last[4 * r + k : 4 * r + k + 1, :] for k in range(4)], axis=1) for r in range(2)]
    states = jnp.concatenate([flat[:, 0:KVW], *ends, jnp.zeros((6, KVW), F32)], axis=0)
    columns[...] = states
    pre_weight = prefix[...]

    def back(net):
        hid = net[NET_HID : NET_HID + PRE, :].astype(F32) + net[NET_HID + PRE : NET, :].astype(F32)
        grad = three_products(nn, states, net[0:KVW, :], net[KVW : 2 * KVW, :]) * (1.0 - hid * hid)
        sides = []
        for side in range(2):
            at = NET_IN + side * HALF_HID
            sides.append(
                three_products(nn, grad, net[at : at + HALF_HID, :], net[at + 2 * HALF_HID : at + 3 * HALF_HID, :])
            )
        return hid, grad, jnp.concatenate(sides, axis=1)

    hid_own, grad_own, first = back(net_own)
    hid_other, grad_other, second = back(net_other)
    grad_prefix = first + second
    grad_pre = jnp.concatenate(in_order(grad_own, grad_other), axis=1)
    hid = jnp.concatenate(in_order(hid_own, hid_other), axis=1)
    biases = jnp.sum(grad_pre, axis=0, keepdims=True)
    biases = jnp.concatenate(
        [by_units(biases[:, 0:HALF_HID], biases[:, HALF_HID:PHID]), jnp.sum(states, axis=0, keepdims=True)], axis=1
    )
    squares = (
        total_of(grad_prefix * grad_prefix)
        + total_of(gram(pre_weight) * gram(grad_pre))
        + total_of(gram(hid) * gram(states))
        + total_of(biases * biases)
    )
    size = jnp.sqrt(squares)
    factor = jnp.minimum(1.0, CLIP / (size + 1e-06))
    count[...] = jnp.sum(extra[15:16, :], axis=1, keepdims=True)
    norm[...] = size

    own = pltpu.roll(grad_prefix, lax.rem(PHID - place * 32, PHID), 1)[0:PREFIX, 0:32]
    back_by = lax.rem(HALF_HID - place * UNITS, HALF_HID)
    sides = [pltpu.roll(grad_pre[:, at : at + HALF_HID], back_by, 1)[:, 0:UNITS] for at in (0, HALF_HID)]
    grad_in = outer(jnp.concatenate(sides, axis=1), pre_weight)
    grad_out = outer(hid, columns[:, pl.ds(pl.multiple_of(place * 128, 128), 128)])
    parts = []
    for d in range(16):
        parts += [grad_out[at + d * UNITS : at + (d + 1) * UNITS, :] for at in (0, HALF_HID)]
    grad_out = jnp.concatenate(parts, axis=0)
    turned = jnp.broadcast_to(biases, (8, 5 * PHID))
    turned = pltpu.roll(turned, lax.rem(5 * PHID - place * 160, 5 * PHID), 1)[0:1, 0:160]
    for c in copies:
        c.wait()
    for k, grad in enumerate((own, grad_in, grad_out, turned)):
        new = adam(held[k][...], grad * factor, held[4 + k][...], held[8 + k][...])
        for j in range(3):
            outs[4 * j + k][...] = new[j]


def update(idx, network, weights, firsts, seconds):
    sizes = [shaped(w.shape) for w in weights]
    one = shaped((1, 1))
    away = (*weights, *firsts, *seconds)
    return call(
        update_body,
        (one, one, one, *sizes, *sizes, *sizes),
        [SCALARS] + [WHOLE] * len(network) + [REMAIN] * 12,
        (*(pltpu.VMEM(w.shape, F32) for w in away), pltpu.VMEM((PRE, KVW), F32), pltpu.SemaphoreType.DMA((12,))),
        limit=16,
        name="clip_and_update",
        moved=6000000,
    )(idx, *network, *(in_hbm(w) for w in away))


def from_behind(value, axis, k):
    return lax.ppermute(value, axis, [(i, (i + k) % 4) for i in range(4)])


def around(value, axis):
    return (value, *(from_behind(value, axis, k) for k in (1, 2, 3)))


def scattered(values, axis):
    return (values[0], *(from_behind(values[k], axis, k) for k in (1, 2, 3)))


def ahead(value, k, late):
    pairs = []
    for z in range(4):
        for y in range(4):
            for core in range(2):
                to = (z, (y + k) % 4) if (core == 0) != late else ((z + k) % 4, y)
                pairs.append(((z * 4 + y) * 2 + core, (to[0] * 4 + to[1]) * 2 + core))
    return lax.ppermute(value, ("z", "y", "core"), pairs)


def after(value, *others):
    return lax.optimization_barrier((value, *others))[0]


def met_on_x(value, late):
    pairs = [(2 * i + core, 2 * (i ^ (3 if core ^ late else 1)) + core) for i in range(4) for core in range(2)]
    return lax.ppermute(value, ("x", "core"), pairs)


def swapped(value):
    return lax.ppermute(value, "core", [(0, 1), (1, 0)])


def on_device(
    tokens,
    segments,
    valid,
    embedding,
    positions_table,
    w_qkv,
    w_attn_out,
    w_fc,
    w_fc_out,
    layer_bias,
    norm_params,
    prefix,
    prefix_in,
    prefix_out,
    prefix_bias,
    moment_prefix,
    moment_in,
    moment_out,
    moment_bias,
    square_prefix,
    square_in,
    square_out,
    square_bias,
):
    idx = jnp.stack([lax.axis_index(a) for a in ("z", "y", "x", "core")]).astype(jnp.int32)
    bias_row = prefix_bias.reshape(1, -1)

    packed, own, other = token_rows(
        idx, tokens, embedding, prefix_in.T, prefix_out, prefix, bias_row, segments, valid
    )
    packed = packed.astype(jnp.float16)
    pieces = [packed, *(ahead(packed, k, False) for k in (1, 2, 3))]
    embedded = own + swapped(other)
    first = embedded + met_on_x(embedded, 0)
    stacked = stack([after(p, embedded) for p in pieces])
    packed = [stacked, *(ahead(stacked, k, True) for k in (1, 2, 3))]
    embedded = first + met_on_x(first, 1)
    x, query, keyval = projections(idx, embedded, *bring(positions_table, norm_params, layer_bias, w_qkv))
    keyval, packed = lax.optimization_barrier((keyval, packed))
    packed = [p.astype(F32) for p in packed]
    net, prefix_all, extra, states = prefix_states(idx, packed)
    final, *kept = layer(
        idx, query, keyval, swapped(keyval), embedded, x, states, swapped(states), extra, segments, valid,
        norm_params, layer_bias, w_attn_out, w_fc, w_fc_out,
    )
    final_other, net = lax.optimization_barrier((swapped(final), net))
    own, other = vocabulary(final, final_other, embedding)
    own, net_other = lax.optimization_barrier((own, swapped(net)))
    pieces = scattered(merge(idx, own, swapped(other)), "x")
    own, other = backward(idx, extra, *pieces, *kept, norm_params, w_attn_out, w_fc, w_fc_out)
    grad = copies_to_send(idx, around(own + swapped(other), "x"))
    grad = lax.all_to_all(grad, ("z", "y"), 0, 0, tiled=True)
    grad = received(grad)
    outs = update(
        idx, (grad, swapped(grad), net, net_other, prefix_all, extra),
        (prefix, prefix_in.T, prefix_out, bias_row),
        (moment_prefix, moment_in.T, moment_out, moment_bias.reshape(1, -1)),
        (square_prefix, square_in.T, square_out, square_bias.reshape(1, -1)),
    )
    outs = list(outs)
    for k in range(3):
        outs[k] = outs[k].reshape(())
        outs[4 + 4 * k] = outs[4 + 4 * k].T
        outs[6 + 4 * k] = outs[6 + 4 * k].reshape(-1)
    return tuple(outs)


def solution(mesh):
    split = Mesh(mesh.devices.reshape(4, 4, 4, 2), ("z", "y", "x", "core"))
    dp = ("z", "y")
    sharded = (P(None, dp), P(None, dp), P(None, dp), P(dp))
    placed = (
        P(dp, None),
        P(dp, None),
        P(dp, None),
        P(("x", "core"), None),
        *([P()] * 7),
        *sharded,
        *sharded,
        *sharded,
    )
    return jax.shard_map(
        on_device,
        mesh=split,
        in_specs=placed,
        out_specs=(P(), P(), P(), *sharded, *sharded, *sharded),
        check_vma=False,
    )
```

```python
import jax
import jax.numpy as jnp
from jax import lax
from jax.experimental import pallas as pl
from jax.experimental.pallas import tpu as pltpu
from jax.sharding import Mesh
from jax.sharding import PartitionSpec as P

D = 1024
HEADS = 16
HEAD_DIM = 64
FF = 4096
VOCAB = 51200
PREFIX = 10
PHID = 512
LENGTH = 256
STEP = 10
KVW = 2048
HALF = 128
PART = 32
SHARD = VOCAB // 8
PRE = 16
EXT = D + 128
FLAT = KVW + 768
SIDE = FLAT // 2

NORM_EPS = 1e-05
BETA_ONE = 0.9
BETA_TWO = 0.999
ADAM_EPS = 1e-08
RATE = 0.1
DECAY = 0.01
CLIP = 0.001
MASKED = -1e30
SCALE = HEAD_DIM**-0.5
GELU_K = 0.7978845608028654
GELU_C = 0.044715

HIGH = lax.Precision.HIGHEST
F32 = jnp.float32
BF16 = jnp.bfloat16
MIB = 1 << 20

WHOLE = pl.BlockSpec(memory_space=pltpu.VMEM)
SCALARS = pl.BlockSpec(memory_space=pltpu.SMEM)
REMAIN = pl.BlockSpec(memory_space=pl.ANY)


def nn(a, b, precision=None):
    return lax.dot_general(a, b, (((1,), (0,)), ((), ())), precision=precision, preferred_element_type=F32)


def nt(a, b, precision=None):
    return lax.dot_general(a, b, (((1,), (1,)), ((), ())), precision=precision, preferred_element_type=F32)


def tn(a, b, precision=None):
    return lax.dot_general(a, b, (((0,), (0,)), ((), ())), precision=precision, preferred_element_type=F32)


def lanes(shape):
    return lax.broadcasted_iota(jnp.int32, shape, len(shape) - 1)


def rows(shape):
    return lax.broadcasted_iota(jnp.int32, shape, 0)


def call(body, outs, ins, scratch=(), limit=48, name=None, flops=0, moved=0):
    return pl.pallas_call(
        body,
        out_shape=outs,
        in_specs=ins,
        out_specs=jax.tree.map(lambda _: WHOLE, outs),
        scratch_shapes=scratch,
        compiler_params=pltpu.CompilerParams(vmem_limit_bytes=limit * MIB),
        cost_estimate=pl.CostEstimate(flops=flops, bytes_accessed=moved, transcendentals=0),
        name=name,
    )


def shaped(shape, dtype=F32):
    return jax.ShapeDtypeStruct(shape, dtype)


def normalised(value):
    mean = jnp.mean(value, axis=-1, keepdims=True)
    centred = value - mean
    spread = jnp.mean(centred * centred, axis=-1, keepdims=True)
    inverse = lax.rsqrt(spread + NORM_EPS)
    return centred * inverse, inverse


def norm_back(value, gain, grad):
    unit, inverse = normalised(value)
    scaled = grad * gain
    first = jnp.mean(scaled, axis=-1, keepdims=True)
    second = jnp.mean(scaled * unit, axis=-1, keepdims=True)
    return inverse * (scaled - first - unit * second)


def three_way(value):
    high = value.astype(BF16).astype(F32)
    rest = value - high
    middle = rest.astype(BF16).astype(F32)
    return high, middle, rest - middle


def with_stat(body, stat):
    high, middle, low = three_way(stat)
    lane = lanes((body.shape[0], 128))
    tail = jnp.where(lane == 0, high, jnp.where(lane == 1, middle, jnp.where(lane == 2, low, 0.0)))
    return body.astype(BF16), tail.astype(BF16)


def stat_of(ref):
    tail = ref[:, D:EXT].astype(F32)
    return jnp.sum(jnp.where(lanes(tail.shape) < 3, tail, 0.0), axis=1, keepdims=True)


UNITS = 16
HALF_HID = PHID // 2
COLS = 64
OWN = UNITS + COLS
SMALL = 16
PACK = OWN + SMALL
TALL = 4 * OWN + SMALL


def two_way(value):
    high = value.astype(BF16)
    return high, (value - high.astype(F32)).astype(BF16)


def placed(value, width, start):
    wide = jnp.concatenate([value, jnp.zeros((value.shape[0], width - value.shape[1]), F32)], axis=1)
    return pltpu.roll(wide, start, 1)


def in_hbm(value):
    return pltpu.with_memory_space_constraint(value, pltpu.HBM)


def stack(pieces):
    small = (pieces[0][OWN:] + pieces[1][OWN:]) + (pieces[2][OWN:] + pieces[3][OWN:])
    return jnp.concatenate([*(p[:OWN] for p in pieces), small], axis=0)


NET_IN = 2 * KVW
NET_HID = NET_IN + 4 * HALF_HID
NET = NET_HID + 2 * PRE


def by_units(first, second):
    parts = []
    for d in range(16):
        at = slice(d * UNITS, (d + 1) * UNITS)
        parts += [first[:, at], second[:, at]]
    return jnp.concatenate(parts, axis=1)


def three_products(product, left, right_high, right_low):
    high, low = two_way(left)
    size = left.shape[0]
    both = product(jnp.concatenate([high, low], axis=0), right_high)
    return both[0:size] + (both[size : 2 * size] + product(high, right_low))


def gram(value):
    high, low = two_way(value)
    size = value.shape[0]
    both = jnp.concatenate([high, low], axis=0)
    both = nt(both, both)
    return both[0:size, 0:size] + (both[0:size, size:] + both[size:, 0:size])


def outer(left, right):
    left_high, left_low = two_way(left)
    high, low = two_way(right)
    return tn(jnp.concatenate([left_high, left_low, left_high], axis=0), jnp.concatenate([high, high, low], axis=0))


def states_body(idx, a, b, c, d, net, weight, extra, part, in_t, out_t):
    z, y, core = idx[0], idx[1], idx[3]
    pieces = (a, b, c, d)
    for late in range(4):
        for early in range(4):
            dz = jnp.where(core == 0, late, early)
            dy = jnp.where(core == 0, early, late)
            place = lax.rem(z + 4 - dz, 4) * 4 + lax.rem(y + 4 - dy, 4)
            at = early * OWN
            in_t[pl.ds(pl.multiple_of(place * UNITS, UNITS), UNITS), :] = pieces[late][at : at + UNITS, :]
            for side in range(2):
                to = pl.ds(pl.multiple_of(place * 128 + side * COLS, COLS), COLS)
                out_t[to, :] = pieces[late][at + UNITS : at + OWN, side * HALF_HID : (side + 1) * HALF_HID]
    rest = sum((r[4 * OWN : TALL, :] for r in pieces[1:]), a[4 * OWN : TALL, :])
    extra[...] = rest
    whole = jnp.where(rows((PRE, PHID)) < PREFIX, rest, 0.0)
    weight[...] = whole
    bias = rest[PREFIX : PREFIX + 1, :]
    bias = jnp.where(core == 0, bias, pltpu.roll(bias, PHID - UNITS, 1))
    bias = jnp.concatenate([bias[:, 32 * k : 32 * k + UNITS] for k in range(16)], axis=1)
    high, low = two_way(in_t[...])
    pre = three_products(nt, whole, high, low) + bias
    hid = jnp.where(rows(pre.shape) < PREFIX, jnp.tanh(pre), 0.0)
    for k, piece in enumerate((high, low)):
        at = NET_IN + 2 * k * HALF_HID
        net[at : at + HALF_HID, :] = piece[:, 0:HALF_HID]
        net[at + HALF_HID : at + 2 * HALF_HID, :] = piece[:, HALF_HID:PHID]
    net[NET_HID : NET_HID + PRE, :], net[NET_HID + PRE : NET, :] = two_way(hid)
    high, low = two_way(out_t[...])
    net[0:KVW, :] = high
    net[KVW : 2 * KVW, :] = low
    part[...] = three_products(nt, hid, high, low)


def prefix_states(idx, pieces):
    return call(
        states_body,
        (shaped((NET, HALF_HID), BF16), shaped((PRE, PHID)), shaped((PRE, PHID)), shaped((PRE, KVW))),
        [SCALARS] + [WHOLE] * 4,
        (pltpu.VMEM((HALF_HID, PHID), F32), pltpu.VMEM((KVW, HALF_HID), F32)),
        limit=12,
        name="prefix_states",
        moved=7000000,
    )(idx, *pieces)


AHEAD = 64


def pack_into(out, small, place, core, weight_in, weight_out, weight, bias, segments, valid):
    out[0:UNITS, :] = weight_in[pl.ds(pl.multiple_of(core * UNITS, UNITS), UNITS), :]
    own = [
        jnp.where(core == 0, weight_out[32 * d : 32 * d + UNITS, :], weight_out[32 * d + UNITS : 32 * d + 32, :])
        for d in range(16)
    ]
    turned = jnp.transpose(jnp.concatenate(own, axis=0))
    out[UNITS:OWN, 0:HALF_HID] = turned[0:COLS, :]
    out[UNITS:OWN, HALF_HID:PHID] = turned[COLS:128, :]
    whole = jnp.concatenate([weight[...], jnp.zeros((16 - PREFIX, 32), F32)], axis=0)
    small[...] = placed(whole, PHID, place * 32)
    flat = placed(jnp.broadcast_to(bias[...], (8, 160)), 5 * PHID, place * 160)
    for r in range(5):
        small[PREFIX + r : PREFIX + r + 1, :] = flat[0:1, r * PHID : (r + 1) * PHID]
    seg = segments[...]
    after = jnp.concatenate([seg[:, 1:], seg[:, :1]], axis=1)
    kept = (valid[...] > 0) & (lanes(seg.shape) < LENGTH - 1) & (after == seg)
    total = jnp.sum(kept.astype(F32), axis=1, keepdims=True)
    small[15:16, :] = jnp.where(lanes((1, PHID)) == place, total, 0.0)
    out[OWN:PACK, :] = small[...]


def rows_body(idx, tokens_at, table, *refs):
    away, (packed, own, other), refs = refs[:6], refs[6:9], refs[9:]
    taken, refs = refs[:6], refs[6:]
    small, block, held, tokens, found, locals_, sems = refs
    core = idx[3]
    first = (idx[2] * 2 + core) * SHARD
    fetch = pltpu.make_async_copy(tokens_at, tokens, sems.at[AHEAD])
    fetch.start()
    copies = [pltpu.make_async_copy(a, b, sems.at[AHEAD + 1 + k]) for k, (a, b) in enumerate(zip(away, taken))]
    for c in copies:
        c.start()
    held[...] = jnp.zeros_like(held)
    fetch.wait()

    def find(p, n):
        local = tokens[0, p] - first
        found[n] = p
        locals_[n] = local
        return n + ((local >= 0) & (local < SHARD)).astype(jnp.int32)

    number = lax.fori_loop(0, LENGTH, find, 0, unroll=16)
    for k in range(4):
        found[number + k] = LENGTH
        locals_[number + k] = 0
    number = (number + 3) // 4

    def copy(n):
        at = pl.multiple_of((locals_[n] // 16) * 16, 16)
        slot = lax.rem(n, AHEAD)
        return pltpu.make_async_copy(table.at[pl.ds(at, 16), :], block.at[slot], sems.at[slot])

    def begin(i, carry):
        for k in range(4):
            copy(4 * i + k).start()
        return carry

    def take(i, carry):
        for k in range(4):
            copy(4 * i + k).wait()
        lines = []
        for k in range(4):
            n = 4 * i + k
            got = block[lax.rem(n, AHEAD)].astype(F32)
            row = lax.rem(locals_[n], 16)
            lines.append(jnp.sum(jnp.where(rows((16, D)) == row, got, 0.0), axis=0, keepdims=True))
        for k in range(4):
            held[pl.ds(found[4 * i + k], 1), :] = lines[k]
        return carry

    for batch in range(LENGTH // AHEAD):
        low = jnp.minimum(number, batch * (AHEAD // 4))
        high = jnp.minimum(number, (batch + 1) * (AHEAD // 4))
        lax.fori_loop(low, high, begin, 0)
        if batch == 0:
            for c in copies:
                c.wait()
            pack_into(packed, small, idx[0] * 4 + idx[1], core, *taken)
        lax.fori_loop(low, high, take, 0)
    own[...] = held[pl.ds(pl.multiple_of(core * HALF, HALF), HALF), :].astype(BF16)
    other[...] = held[pl.ds(pl.multiple_of((1 - core) * HALF, HALF), HALF), :].astype(BF16)


def token_rows(idx, tokens, table, *network):
    return call(
        rows_body,
        (shaped((PACK, PHID)), shaped((HALF, D), BF16), shaped((HALF, D), BF16)),
        [SCALARS] + [REMAIN] * (2 + len(network)),
        (
            *(pltpu.VMEM(v.shape, v.dtype) for v in network),
            pltpu.VMEM((16, PHID), F32),
            pltpu.VMEM((AHEAD, 16, D), BF16),
            pltpu.VMEM((LENGTH + 8, D), F32),
            pltpu.SMEM((1, LENGTH), jnp.int32),
            pltpu.SMEM((LENGTH + 4,), jnp.int32),
            pltpu.SMEM((LENGTH + 4,), jnp.int32),
            pltpu.SemaphoreType.DMA((AHEAD + 1 + len(network),)),
        ),
        limit=10,
        name="token_rows_and_packed_weights",
        moved=9000000,
    )(idx, *(in_hbm(v) for v in (tokens, table, *network)))


def bring_body(*refs):
    half = len(refs) // 2
    sems = refs[-1]
    copies = [pltpu.make_async_copy(refs[k], refs[half + k], sems.at[k]) for k in range(half)]
    for c in copies:
        c.start()
    for c in copies:
        c.wait()


def bring(*inputs):
    return pl.pallas_call(
        bring_body,
        out_shape=tuple(pltpu.VMEM(v.shape, v.dtype) for v in inputs),
        in_specs=[REMAIN] * len(inputs),
        out_specs=tuple(REMAIN for _ in inputs),
        scratch_shapes=(pltpu.SemaphoreType.DMA((len(inputs),)),),
        compiler_params=pltpu.CompilerParams(vmem_limit_bytes=MIB),
        cost_estimate=pl.CostEstimate(flops=0, bytes_accessed=2 * sum(v.size * v.dtype.itemsize for v in inputs), transcendentals=0),
        name="bring_into_vmem",
    )(*(in_hbm(v) for v in inputs))


def qkv_body(idx, embedded, places, norms, bias, weight, x_out, query, keyval):
    core = idx[3]
    mine = embedded[...]
    x = mine.astype(F32) + places[pl.ds(pl.multiple_of(core * HALF, HALF), HALF), :].astype(F32)
    x_out[...] = x
    unit, _ = normalised(x)
    normed = (unit * norms[0, 0:1, :] + norms[0, 1:2, :]).astype(BF16)
    for j in range(6):
        at = slice(j * 512, (j + 1) * 512)
        part = nn(normed, weight[0, :, at]) + bias[:, at].astype(F32)
        if j < 2:
            query[:, at] = (part.astype(BF16).astype(F32) * SCALE).astype(BF16)
        else:
            keyval[0:HALF, (j - 2) * 512 : (j - 1) * 512] = part.astype(BF16)
    keyval[HALF : HALF + 16, 0:D] = mine[0:16, :]
    keyval[HALF : HALF + 16, D:KVW] = jnp.zeros((16, D), BF16)


def projections(idx, embedded, places, norms, bias, weight):
    return call(
        qkv_body,
        (shaped((HALF, D)), shaped((HALF, D), BF16), shaped((HALF + 16, KVW), BF16)),
        [SCALARS] + [WHOLE] * 5,
        limit=10,
        name="norm_and_projections",
        flops=2 * HALF * D * 3 * D,
        moved=9000000,
    )(idx, embedded, places, norms, bias, weight)


FCH = 1024


def by_heads(out, value, left):
    out[...] = jnp.zeros_like(out)
    zero = jnp.zeros((PRE, 128), BF16)
    for pair in range(HEADS // 2):
        at = slice(pair * 128, (pair + 1) * 128)
        out[2 * pair * PRE : (2 * pair + 1) * PRE, at] = jnp.where(left, value[:, at], zero)
        out[(2 * pair + 1) * PRE : (2 * pair + 2) * PRE, at] = jnp.where(left, zero, value[:, at])


def layer_body(
    idx, query, kv_own, kv_other, embedded, x_in, states_own, states_other, extra, segments, valid, norms, bias,
    w_out, w_fc, w_fc_out,
    final, attended_part, last_part, inner_part, mixed_part, query_part, target_part, stats_part, probs_part, value_rows,
    key_rows, mixed, keep, wide,
):
    xx, core = idx[2], idx[3]
    part = pl.ds(pl.multiple_of(xx * PART, PART), PART)
    shift = jnp.concatenate([extra[r : r + 1, :] for r in range(PREFIX + 1, PREFIX + 5)], axis=1)
    states = states_own[...] + states_other[...] + shift
    states = jnp.where(rows(states.shape) < PREFIX, states, 0.0).astype(BF16)
    left = lanes((PRE, 128)) < HEAD_DIM
    by_heads(key_rows, states[:, 0:D], left)
    by_heads(value_rows, states[:, D:KVW], left)

    seg = segments[...]
    mine = jnp.where(core == 0, seg[:, 0:HALF], seg[:, HALF:LENGTH])
    theirs = jnp.where(core == 0, seg[:, HALF:LENGTH], seg[:, 0:HALF])
    square = (HALF, HALF)
    mine_down = jnp.transpose(jnp.broadcast_to(mine, square))
    sees_own = (mine_down == jnp.broadcast_to(mine, square)) & (lanes(square) <= rows(square))
    sees_other = (mine_down == jnp.broadcast_to(theirs, square)) & (core == 1)
    hide = jnp.concatenate([jnp.where(m, 0.0, MASKED) for m in (sees_own, sees_other)], axis=1)
    hide = jnp.concatenate([hide, hide], axis=0)
    left = lanes(square) < HEAD_DIM
    ahead_scores = nt(query[...], key_rows[...])
    group = lanes(square) // PRE
    live = lanes(square) - group * PRE < PREFIX
    probs = [jnp.zeros(square, F32)] * 2
    for pair in range(HEADS // 2):
        at = slice(pair * 128, pair * 128 + 128)
        at_v = slice(D + pair * 128, D + pair * 128 + 128)
        q = query[:, at]
        zero = jnp.zeros_like(q)
        both = jnp.concatenate([jnp.where(left, q, zero), jnp.where(left, zero, q)], axis=0)
        keys = jnp.concatenate([kv_own[0:HALF, at], kv_other[0:HALF, at]], axis=0)
        values = jnp.concatenate([kv_own[0:HALF, at_v], kv_other[0:HALF, at_v]], axis=0)
        scores = nt(both, keys) + hide
        block = pair // 4
        mine = [live & (group == 2 * (pair % 4) + side) for side in range(2)]
        prefix = ahead_scores[:, block * 128 : (block + 1) * 128]
        prefix = jnp.concatenate([jnp.where(m, prefix, MASKED) for m in mine], axis=0)
        top = jnp.maximum(jnp.maximum(scores[:, 0:HALF], scores[:, HALF:LENGTH]), prefix)
        top = jnp.max(top, axis=1, keepdims=True)
        expo = jnp.exp(scores - top)
        expo_prefix = jnp.exp(prefix - top)
        total = jnp.sum(expo[:, 0:HALF] + expo[:, HALF:LENGTH] + expo_prefix, axis=1, keepdims=True)
        share = 1.0 / total
        out = nn((expo * share).astype(BF16), values)
        mixed[:, at] = jnp.where(left, out[0:HALF], out[HALF:])
        expo_prefix = expo_prefix * share
        probs[block] = probs[block] + (expo_prefix[0:HALF] + expo_prefix[HALF:])
    probs = jnp.concatenate(probs, axis=1)
    mixed[...] = mixed[...] + nn(probs.astype(BF16), value_rows[...])
    mixed_part[...] = mixed[part, :]
    query_part[...] = query[part, :]
    wide[:, 0 : HEADS * PRE] = probs
    probs_part[...] = wide[part, 0 : HEADS * PRE]

    x = x_in[...] + nn(mixed[...].astype(BF16), w_out[0]) + bias[:, 3 * D : 4 * D].astype(F32)
    keep[...] = x
    attended_part[...] = keep[part, :]
    unit, _ = normalised(x)
    normed = (unit * norms[1, 0:1, :] + norms[1, 1:2, :]).astype(BF16)
    x = x + bias[:, 4 * D + FF : 5 * D + FF].astype(F32)
    for j in range(4):
        inner = nn(normed, w_fc[0, :, j * FCH : (j + 1) * FCH]) + bias[:, 4 * D + j * FCH : 4 * D + (j + 1) * FCH].astype(F32)
        wide[...] = inner
        inner_part[:, j * FCH : (j + 1) * FCH] = wide[part, :]
        active = (0.5 * inner * (1.0 + jnp.tanh(GELU_K * (inner + GELU_C * inner * inner * inner)))).astype(BF16)
        x = x + nn(active, w_fc_out[0, j * FCH : (j + 1) * FCH, :])
    keep[...] = x
    last_part[...] = keep[part, :]
    unit, _ = normalised(x)
    result = (unit * norms[2, 0:1, :] + norms[2, 1:2, :]).astype(BF16)
    final[...] = result

    wide[...] = embedded[...].astype(F32)
    keep[...] = result.astype(F32)
    after = jnp.concatenate([wide[1:HALF, :], kv_other[HALF : HALF + 1, 0:D].astype(F32)], axis=0)
    wide[...] = after
    target = wide[part, :]
    target_part[...] = target
    picked = jnp.sum(keep[part, :] * target, axis=1, keepdims=True)
    following = jnp.concatenate([seg[:, 1:], seg[:, :1]], axis=1)
    kept = (valid[...] > 0) & (lanes(seg.shape) < LENGTH - 1) & (following == seg)
    kept = kept.astype(F32)
    counted = jnp.where(core == 0, kept[:, 0:HALF], kept[:, HALF:LENGTH])
    wide[:, 0:HALF] = jnp.transpose(jnp.broadcast_to(counted, square))
    lane = lanes((PART, 128))
    stats_part[...] = jnp.where(lane == 0, picked, jnp.where(lane == 1, wide[part, 0:128], 0.0))


def layer(idx, *inputs):
    return call(
        layer_body,
        (
            shaped((HALF, D), BF16),
            shaped((PART, D)),
            shaped((PART, D)),
            shaped((PART, FF)),
            shaped((PART, D)),
            shaped((PART, D), BF16),
            shaped((PART, D)),
            shaped((PART, 128)),
            shaped((PART, HEADS * PRE)),
            shaped((HEADS * PRE, D), BF16),
        ),
        [SCALARS] + [WHOLE] * len(inputs),
        (
            pltpu.VMEM((HEADS * PRE, D), BF16),
            pltpu.VMEM((HALF, D), F32),
            pltpu.VMEM((HALF, D), F32),
            pltpu.VMEM((HALF, FCH), F32),
        ),
        limit=10,
        name="attention_and_feed_forward",
        flops=2 * HALF * D * 9 * D,
        moved=22000000,
    )(idx, *inputs)


VCH = 1280


def vocab_body(f_own, f_other, table, own, other, final, grad):
    final[0:HALF, :] = f_own[...]
    final[HALF:LENGTH, :] = f_other[...]
    chunks = SHARD // VCH
    logits = nt(final[...], table[0:VCH, :])
    for j in range(chunks):
        if j + 1 < chunks:
            following = nt(final[...], table[(j + 1) * VCH : (j + 2) * VCH, :])
        now = jnp.max(logits, axis=1, keepdims=True)
        if j:
            now = jnp.maximum(top, now)
            shrink = jnp.exp(top - now)
        expo = jnp.exp(logits - now)
        part = jnp.sum(expo, axis=1, keepdims=True)
        total = total * shrink + part if j else part
        part = nn(expo.astype(BF16), table[j * VCH : (j + 1) * VCH, :])
        grad[...] = grad[...] * shrink + part if j else part
        top, logits = now, following
    mean = grad[...] * (1.0 / total)
    log_sum = top + jnp.log(total)
    for out, at in ((own, slice(0, HALF)), (other, slice(HALF, LENGTH))):
        body, tail = with_stat(mean[at, :], log_sum[at, :])
        out[:, 0:D] = body
        out[:, D:EXT] = tail


def vocabulary(f_own, f_other, table):
    return call(
        vocab_body,
        (shaped((HALF, EXT), BF16),) * 2,
        [WHOLE] * 3,
        (pltpu.VMEM((LENGTH, D), BF16), pltpu.VMEM((LENGTH, D), F32)),
        limit=16,
        name="logits_and_gradient",
        flops=4 * LENGTH * D * SHARD,
        moved=SHARD * D * 2,
    )(f_own, f_other, table)


def merged(refs):
    stats = [stat_of(r) for r in refs]
    top = stats[0]
    for s in stats[1:]:
        top = jnp.maximum(top, s)
    weights = [jnp.exp(s - top) for s in stats]
    total = sum(weights[1:], weights[0])
    mean = sum((w * r[:, 0:D].astype(F32) for w, r in zip(weights[1:], refs[1:])), weights[0] * refs[0][:, 0:D].astype(F32))
    return mean * (1.0 / total), top + jnp.log(total)


def merge_body(idx, own, other, o0, o1, o2, o3, held):
    mean, log_total = merged((own, other))
    body, tail = with_stat(mean, log_total)
    held[:, 0:D] = body
    held[:, D:EXT] = tail
    for k, out in enumerate((o0, o1, o2, o3)):
        out[...] = held[pl.ds(pl.multiple_of(lax.rem(idx[2] + k, 4) * PART, PART), PART), :]


def merge(idx, own, other):
    return call(
        merge_body,
        (shaped((PART, EXT), BF16),) * 4,
        [SCALARS] + [WHOLE] * 2,
        (pltpu.VMEM((HALF, EXT), BF16),),
        limit=8,
        name="merge_two_cores",
        moved=900000,
    )(idx, own, other)


def finely(left, right):
    size = left.shape[0]
    both = nt(jnp.concatenate(two_way(left), axis=0), right)
    return both[0:size] + both[size : 2 * size]


def backward_body(
    idx, extra, p0, p1, p2, p3, attended, last, inner, mixed, query, target, stats, probs_in, value_rows, norms, w_out, w_fc, w_fc_out,
    own, other, result, ones_rows,
):
    mean, log_total = merged((p0, p1, p2, p3))
    counted = stats[:, 1:2]
    loss = jnp.sum((log_total - stats[:, 0:1]) * counted, axis=0, keepdims=True)
    scale = counted * (1.0 / jnp.sum(extra[15:16, :], axis=1, keepdims=True))
    exact = (jnp.exp(stats[:, 0:1] - log_total) - 1.0) * scale
    grad = mean * scale - target[...] * (scale + exact - exact.astype(BF16).astype(F32))
    grad_x = norm_back(last[...], norms[2, 0:1, :], grad)
    grad_normed = jnp.zeros((PART, D), F32)
    for j in range(4):
        u = inner[:, j * FCH : (j + 1) * FCH]
        bend = jnp.tanh(GELU_K * (u + GELU_C * u * u * u))
        slope = 0.5 * (1.0 + bend) + 0.5 * u * (1.0 - bend * bend) * (GELU_K * (1.0 + 3.0 * GELU_C * u * u))
        grad_u = finely(grad_x, w_fc_out[0, j * FCH : (j + 1) * FCH, :]) * slope
        grad_normed = grad_normed + finely(grad_u, w_fc[0, :, j * FCH : (j + 1) * FCH])
    grad_h = grad_x + norm_back(attended[...], norms[1, 0:1, :], grad_normed)
    grad_mixed = finely(grad_h, w_out[0])

    left = lanes((PRE, 128)) < HEAD_DIM
    by_heads(ones_rows, jnp.ones((PRE, D), BF16), left)
    q = query[...]
    probs = probs_in[...]
    grad_probs = finely(grad_mixed, value_rows[...])
    inner_sum = finely(grad_mixed * mixed[...], ones_rows[...])
    grad_scores = jnp.concatenate(two_way(probs * (grad_probs - inner_sum)), axis=0)
    grad_keys = tn(grad_scores, jnp.concatenate([q, q], axis=0))
    probs = probs.astype(BF16)
    grad_values = tn(jnp.concatenate([probs, probs], axis=0), jnp.concatenate(two_way(grad_mixed), axis=0))
    for side, value in enumerate((grad_keys, grad_values)):
        parts = []
        for pair in range(HEADS // 2):
            at = slice(pair * 128, (pair + 1) * 128)
            up = value[2 * pair * PRE : (2 * pair + 1) * PRE, at]
            parts.append(jnp.where(left, up, value[(2 * pair + 1) * PRE : (2 * pair + 2) * PRE, at]))
        folded = jnp.concatenate(parts, axis=1)
        result[:, side * D : (side + 1) * D] = folded[0:8, :]
        for r in range(2):
            for k in range(2):
                result[4 * r + 2 * side + k : 4 * r + 2 * side + k + 1, KVW : KVW + 512] = folded[
                    8 + r : 9 + r, k * 512 : (k + 1) * 512
                ]
    lane = lanes((8, 256))
    result[:, KVW + 512 : FLAT] = jnp.where((lane == 0) & (rows((8, 256)) == 0), loss, 0.0)
    left, right = result[:, 0:SIDE], result[:, SIDE:FLAT]
    own[...] = jnp.where(idx[3] == 0, left, right)
    other[...] = jnp.where(idx[3] == 0, right, left)


def backward(idx, *inputs):
    return call(
        backward_body,
        (shaped((8, SIDE)), shaped((8, SIDE))),
        [SCALARS] + [WHOLE] * len(inputs),
        (pltpu.VMEM((8, FLAT), F32), pltpu.VMEM((HEADS * PRE, D), BF16)),
        limit=10,
        name="backward_to_prefix",
        flops=2 * PART * D * 9 * D,
        moved=20000000,
    )(idx, *inputs)


def send_body(idx, a, b, c, d, out):
    total = (a[...] + b[...]) + (c[...] + d[...])
    tail = total[:, SIDE - 256 : SIDE]
    high, middle, low = three_way(tail[:, 0:1])
    lane = lanes((8, 256))
    pieces = jnp.where(lane == 0, high, jnp.where(lane == 1, middle, jnp.where(lane == 2, low, 0.0)))
    tail = jnp.where(idx[3] == 1, pieces, tail)
    total = jnp.concatenate([total[:, 0 : SIDE - 256], tail], axis=1).astype(BF16)
    out[...] = jnp.broadcast_to(total[None], out.shape)


def copies_to_send(idx, pieces):
    return call(
        send_body,
        shaped((16, 8, SIDE), BF16),
        [SCALARS] + [WHOLE] * 4,
        limit=8,
        name="sum_to_send",
        moved=600000,
    )(idx, *pieces)


def adam(weight, grad, first, second):
    first = BETA_ONE * first + (1.0 - BETA_ONE) * grad
    second = BETA_TWO * second + (1.0 - BETA_TWO) * grad * grad
    move = first / (1.0 - BETA_ONE**STEP) / (jnp.sqrt(second / (1.0 - BETA_TWO**STEP)) + ADAM_EPS)
    return weight - RATE * (move + DECAY * weight), first, second


def total_of(value):
    return jnp.sum(jnp.sum(value, axis=1, keepdims=True), axis=0, keepdims=True)


def received_body(pieces, out):
    total = pieces[0].astype(F32)
    for k in range(1, 16):
        total = total + pieces[k].astype(F32)
    out[...] = total


def received(pieces):
    return call(received_body, shaped((8, SIDE)), [WHOLE], limit=8, name="sum_received", moved=400000)(pieces)


def update_body(idx, side_own, side_other, net_own, net_other, prefix, extra, *refs):
    away, refs = refs[:12], refs[12:]
    (loss, count, norm), outs, refs = refs[:3], refs[3:15], refs[15:]
    held, (columns, sems) = refs[:12], refs[12:]
    copies = [pltpu.make_async_copy(a, b, sems.at[k]) for k, (a, b) in enumerate(zip(away, held))]
    for c in copies:
        c.start()
    place = idx[0] * 4 + idx[1]
    core = idx[3]

    def in_order(mine, theirs):
        return jnp.where(core == 0, mine, theirs), jnp.where(core == 0, theirs, mine)

    flat = jnp.concatenate(in_order(side_own[...], side_other[...]), axis=1)
    loss[...] = jnp.sum(flat[0:1, KVW + 512 : FLAT], axis=1, keepdims=True)
    last = flat[:, KVW : KVW + 512]
    ends = [jnp.concatenate([last[4 * r + k : 4 * r + k + 1, :] for k in range(4)], axis=1) for r in range(2)]
    states = jnp.concatenate([flat[:, 0:KVW], *ends, jnp.zeros((6, KVW), F32)], axis=0)
    columns[...] = states
    pre_weight = prefix[...]

    def back(net):
        hid = net[NET_HID : NET_HID + PRE, :].astype(F32) + net[NET_HID + PRE : NET, :].astype(F32)
        grad = three_products(nn, states, net[0:KVW, :], net[KVW : 2 * KVW, :]) * (1.0 - hid * hid)
        sides = []
        for side in range(2):
            at = NET_IN + side * HALF_HID
            sides.append(
                three_products(nn, grad, net[at : at + HALF_HID, :], net[at + 2 * HALF_HID : at + 3 * HALF_HID, :])
            )
        return hid, grad, jnp.concatenate(sides, axis=1)

    hid_own, grad_own, first = back(net_own)
    hid_other, grad_other, second = back(net_other)
    grad_prefix = first + second
    grad_pre = jnp.concatenate(in_order(grad_own, grad_other), axis=1)
    hid = jnp.concatenate(in_order(hid_own, hid_other), axis=1)
    biases = jnp.sum(grad_pre, axis=0, keepdims=True)
    biases = jnp.concatenate(
        [by_units(biases[:, 0:HALF_HID], biases[:, HALF_HID:PHID]), jnp.sum(states, axis=0, keepdims=True)], axis=1
    )
    squares = (
        total_of(grad_prefix * grad_prefix)
        + total_of(gram(pre_weight) * gram(grad_pre))
        + total_of(gram(hid) * gram(states))
        + total_of(biases * biases)
    )
    size = jnp.sqrt(squares)
    factor = jnp.minimum(1.0, CLIP / (size + 1e-06))
    count[...] = jnp.sum(extra[15:16, :], axis=1, keepdims=True)
    norm[...] = size

    own = pltpu.roll(grad_prefix, lax.rem(PHID - place * 32, PHID), 1)[0:PREFIX, 0:32]
    back_by = lax.rem(HALF_HID - place * UNITS, HALF_HID)
    sides = [pltpu.roll(grad_pre[:, at : at + HALF_HID], back_by, 1)[:, 0:UNITS] for at in (0, HALF_HID)]
    grad_in = outer(jnp.concatenate(sides, axis=1), pre_weight)
    grad_out = outer(hid, columns[:, pl.ds(pl.multiple_of(place * 128, 128), 128)])
    parts = []
    for d in range(16):
        parts += [grad_out[at + d * UNITS : at + (d + 1) * UNITS, :] for at in (0, HALF_HID)]
    grad_out = jnp.concatenate(parts, axis=0)
    turned = jnp.broadcast_to(biases, (8, 5 * PHID))
    turned = pltpu.roll(turned, lax.rem(5 * PHID - place * 160, 5 * PHID), 1)[0:1, 0:160]
    for c in copies:
        c.wait()
    for k, grad in enumerate((own, grad_in, grad_out, turned)):
        new = adam(held[k][...], grad * factor, held[4 + k][...], held[8 + k][...])
        for j in range(3):
            outs[4 * j + k][...] = new[j]


def update(idx, network, weights, firsts, seconds):
    sizes = [shaped(w.shape) for w in weights]
    one = shaped((1, 1))
    away = (*weights, *firsts, *seconds)
    return call(
        update_body,
        (one, one, one, *sizes, *sizes, *sizes),
        [SCALARS] + [WHOLE] * len(network) + [REMAIN] * 12,
        (*(pltpu.VMEM(w.shape, F32) for w in away), pltpu.VMEM((PRE, KVW), F32), pltpu.SemaphoreType.DMA((12,))),
        limit=16,
        name="clip_and_update",
        moved=6000000,
    )(idx, *network, *(in_hbm(w) for w in away))


def from_behind(value, axis, k):
    return lax.ppermute(value, axis, [(i, (i + k) % 4) for i in range(4)])


def around(value, axis):
    return (value, *(from_behind(value, axis, k) for k in (1, 2, 3)))


def scattered(values, axis):
    return (values[0], *(from_behind(values[k], axis, k) for k in (1, 2, 3)))


def ahead(value, k, late):
    pairs = []
    for z in range(4):
        for y in range(4):
            for core in range(2):
                to = (z, (y + k) % 4) if (core == 0) != late else ((z + k) % 4, y)
                pairs.append(((z * 4 + y) * 2 + core, (to[0] * 4 + to[1]) * 2 + core))
    return lax.ppermute(value, ("z", "y", "core"), pairs)


def after(value, *others):
    return lax.optimization_barrier((value, *others))[0]


def met_on_x(value, late):
    pairs = [(2 * i + core, 2 * (i ^ (3 if core ^ late else 1)) + core) for i in range(4) for core in range(2)]
    return lax.ppermute(value, ("x", "core"), pairs)


def swapped(value):
    return lax.ppermute(value, "core", [(0, 1), (1, 0)])


def on_device(
    tokens,
    segments,
    valid,
    embedding,
    positions_table,
    w_qkv,
    w_attn_out,
    w_fc,
    w_fc_out,
    layer_bias,
    norm_params,
    prefix,
    prefix_in,
    prefix_out,
    prefix_bias,
    moment_prefix,
    moment_in,
    moment_out,
    moment_bias,
    square_prefix,
    square_in,
    square_out,
    square_bias,
):
    idx = jnp.stack([lax.axis_index(a) for a in ("z", "y", "x", "core")]).astype(jnp.int32)
    bias_row = prefix_bias.reshape(1, -1)

    packed, own, other = token_rows(
        idx, tokens, embedding, prefix_in.T, prefix_out, prefix, bias_row, segments, valid
    )
    packed = packed.astype(jnp.float16)
    pieces = [packed, *(ahead(packed, k, False) for k in (1, 2, 3))]
    embedded = own + swapped(other)
    first = embedded + met_on_x(embedded, 0)
    stacked = stack([after(p, embedded) for p in pieces])
    packed = [stacked, *(ahead(stacked, k, True) for k in (1, 2, 3))]
    embedded = first + met_on_x(first, 1)
    x, query, keyval = projections(idx, embedded, *bring(positions_table, norm_params, layer_bias, w_qkv))
    keyval, packed = lax.optimization_barrier((keyval, packed))
    packed = [p.astype(F32) for p in packed]
    net, prefix_all, extra, states = prefix_states(idx, packed)
    final, *kept = layer(
        idx, query, keyval, swapped(keyval), embedded, x, states, swapped(states), extra, segments, valid,
        norm_params, layer_bias, w_attn_out, w_fc, w_fc_out,
    )
    final_other, net = lax.optimization_barrier((swapped(final), net))
    own, other = vocabulary(final, final_other, embedding)
    own, net_other = lax.optimization_barrier((own, swapped(net)))
    pieces = scattered(merge(idx, own, swapped(other)), "x")
    own, other = backward(idx, extra, *pieces, *kept, norm_params, w_attn_out, w_fc, w_fc_out)
    grad = copies_to_send(idx, around(own + swapped(other), "x"))
    grad = lax.all_to_all(grad, ("z", "y"), 0, 0, tiled=True)
    grad = received(grad)
    outs = update(
        idx, (grad, swapped(grad), net, net_other, prefix_all, extra),
        (prefix, prefix_in.T, prefix_out, bias_row),
        (moment_prefix, moment_in.T, moment_out, moment_bias.reshape(1, -1)),
        (square_prefix, square_in.T, square_out, square_bias.reshape(1, -1)),
    )
    outs = list(outs)
    for k in range(3):
        outs[k] = outs[k].reshape(())
        outs[4 + 4 * k] = outs[4 + 4 * k].T
        outs[6 + 4 * k] = outs[6 + 4 * k].reshape(-1)
    return tuple(outs)


def solution(mesh):
    split = Mesh(mesh.devices.reshape(4, 4, 4, 2), ("z", "y", "x", "core"))
    dp = ("z", "y")
    sharded = (P(None, dp), P(None, dp), P(None, dp), P(dp))
    placed = (
        P(dp, None),
        P(dp, None),
        P(dp, None),
        P(("x", "core"), None),
        *([P()] * 7),
        *sharded,
        *sharded,
        *sharded,
    )
    return jax.shard_map(
        on_device,
        mesh=split,
        in_specs=placed,
        out_specs=(P(), P(), P(), *sharded, *sharded, *sharded),
        check_vma=False,
    )
```

```python
import jax
import jax.numpy as jnp
from jax import lax
from jax.experimental import pallas as pl
from jax.experimental.pallas import tpu as pltpu
from jax.sharding import Mesh
from jax.sharding import PartitionSpec as P

D = 1024
HEADS = 16
HEAD_DIM = 64
FF = 4096
VOCAB = 51200
PREFIX = 10
PHID = 512
LENGTH = 256
STEP = 10
KVW = 2048
HALF = 128
PART = 32
SHARD = VOCAB // 8
PRE = 16
EXT = D + 128
FLAT = KVW + 768
SIDE = FLAT // 2

NORM_EPS = 1e-05
BETA_ONE = 0.9
BETA_TWO = 0.999
ADAM_EPS = 1e-08
RATE = 0.1
DECAY = 0.01
CLIP = 0.001
MASKED = -1e30
SCALE = HEAD_DIM**-0.5
GELU_K = 0.7978845608028654
GELU_C = 0.044715

HIGH = lax.Precision.HIGHEST
F32 = jnp.float32
BF16 = jnp.bfloat16
MIB = 1 << 20

WHOLE = pl.BlockSpec(memory_space=pltpu.VMEM)
SCALARS = pl.BlockSpec(memory_space=pltpu.SMEM)
REMAIN = pl.BlockSpec(memory_space=pl.ANY)


def nn(a, b, precision=None):
    return lax.dot_general(a, b, (((1,), (0,)), ((), ())), precision=precision, preferred_element_type=F32)


def nt(a, b, precision=None):
    return lax.dot_general(a, b, (((1,), (1,)), ((), ())), precision=precision, preferred_element_type=F32)


def tn(a, b, precision=None):
    return lax.dot_general(a, b, (((0,), (0,)), ((), ())), precision=precision, preferred_element_type=F32)


def lanes(shape):
    return lax.broadcasted_iota(jnp.int32, shape, len(shape) - 1)


def rows(shape):
    return lax.broadcasted_iota(jnp.int32, shape, 0)


def call(body, outs, ins, scratch=(), limit=48, name=None, flops=0, moved=0):
    return pl.pallas_call(
        body,
        out_shape=outs,
        in_specs=ins,
        out_specs=jax.tree.map(lambda _: WHOLE, outs),
        scratch_shapes=scratch,
        compiler_params=pltpu.CompilerParams(vmem_limit_bytes=limit * MIB),
        cost_estimate=pl.CostEstimate(flops=flops, bytes_accessed=moved, transcendentals=0),
        name=name,
    )


def shaped(shape, dtype=F32):
    return jax.ShapeDtypeStruct(shape, dtype)


def normalised(value):
    mean = jnp.mean(value, axis=-1, keepdims=True)
    centred = value - mean
    spread = jnp.mean(centred * centred, axis=-1, keepdims=True)
    inverse = lax.rsqrt(spread + NORM_EPS)
    return centred * inverse, inverse


def norm_back(value, gain, grad):
    unit, inverse = normalised(value)
    scaled = grad * gain
    first = jnp.mean(scaled, axis=-1, keepdims=True)
    second = jnp.mean(scaled * unit, axis=-1, keepdims=True)
    return inverse * (scaled - first - unit * second)


def three_way(value):
    high = value.astype(BF16).astype(F32)
    rest = value - high
    middle = rest.astype(BF16).astype(F32)
    return high, middle, rest - middle


def with_stat(body, stat):
    high, middle, low = three_way(stat)
    lane = lanes((body.shape[0], 128))
    tail = jnp.where(lane == 0, high, jnp.where(lane == 1, middle, jnp.where(lane == 2, low, 0.0)))
    return body.astype(BF16), tail.astype(BF16)


def stat_of(ref):
    tail = ref[:, D:EXT].astype(F32)
    return jnp.sum(jnp.where(lanes(tail.shape) < 3, tail, 0.0), axis=1, keepdims=True)


UNITS = 16
HALF_HID = PHID // 2
COLS = 64
OWN = UNITS + COLS
SMALL = 16
PACK = OWN + SMALL
TALL = 4 * OWN + SMALL


def two_way(value):
    high = value.astype(BF16)
    return high, (value - high.astype(F32)).astype(BF16)


def placed(value, width, start):
    wide = jnp.concatenate([value, jnp.zeros((value.shape[0], width - value.shape[1]), F32)], axis=1)
    return pltpu.roll(wide, start, 1)


def in_hbm(value):
    return pltpu.with_memory_space_constraint(value, pltpu.HBM)


def stack(pieces):
    small = (pieces[0][OWN:] + pieces[1][OWN:]) + (pieces[2][OWN:] + pieces[3][OWN:])
    return jnp.concatenate([*(p[:OWN] for p in pieces), small], axis=0)


NET_IN = 2 * KVW
NET_HID = NET_IN + 4 * HALF_HID
NET = NET_HID + 2 * PRE


def by_units(first, second):
    parts = []
    for d in range(16):
        at = slice(d * UNITS, (d + 1) * UNITS)
        parts += [first[:, at], second[:, at]]
    return jnp.concatenate(parts, axis=1)


def three_products(product, left, right_high, right_low):
    high, low = two_way(left)
    size = left.shape[0]
    both = product(jnp.concatenate([high, low], axis=0), right_high)
    return both[0:size] + (both[size : 2 * size] + product(high, right_low))


def gram(value):
    high, low = two_way(value)
    size = value.shape[0]
    both = jnp.concatenate([high, low], axis=0)
    both = nt(both, both)
    return both[0:size, 0:size] + (both[0:size, size:] + both[size:, 0:size])


def outer(left, right):
    left_high, left_low = two_way(left)
    high, low = two_way(right)
    return tn(jnp.concatenate([left_high, left_low, left_high], axis=0), jnp.concatenate([high, high, low], axis=0))


def states_body(idx, a, b, c, d, net, weight, extra, part, in_t, out_t):
    z, y, core = idx[0], idx[1], idx[3]
    pieces = (a, b, c, d)
    for late in range(4):
        for early in range(4):
            dz = jnp.where(core == 0, late, early)
            dy = jnp.where(core == 0, early, late)
            place = lax.rem(z + 4 - dz, 4) * 4 + lax.rem(y + 4 - dy, 4)
            at = early * OWN
            in_t[pl.ds(pl.multiple_of(place * UNITS, UNITS), UNITS), :] = pieces[late][at : at + UNITS, :]
            for side in range(2):
                to = pl.ds(pl.multiple_of(place * 128 + side * COLS, COLS), COLS)
                out_t[to, :] = pieces[late][at + UNITS : at + OWN, side * HALF_HID : (side + 1) * HALF_HID]
    rest = sum((r[4 * OWN : TALL, :] for r in pieces[1:]), a[4 * OWN : TALL, :])
    extra[...] = rest
    whole = jnp.where(rows((PRE, PHID)) < PREFIX, rest, 0.0)
    weight[...] = whole
    bias = rest[PREFIX : PREFIX + 1, :]
    bias = jnp.where(core == 0, bias, pltpu.roll(bias, PHID - UNITS, 1))
    bias = jnp.concatenate([bias[:, 32 * k : 32 * k + UNITS] for k in range(16)], axis=1)
    high, low = two_way(in_t[...])
    pre = three_products(nt, whole, high, low) + bias
    hid = jnp.where(rows(pre.shape) < PREFIX, jnp.tanh(pre), 0.0)
    for k, piece in enumerate((high, low)):
        at = NET_IN + 2 * k * HALF_HID
        net[at : at + HALF_HID, :] = piece[:, 0:HALF_HID]
        net[at + HALF_HID : at + 2 * HALF_HID, :] = piece[:, HALF_HID:PHID]
    net[NET_HID : NET_HID + PRE, :], net[NET_HID + PRE : NET, :] = two_way(hid)
    high, low = two_way(out_t[...])
    net[0:KVW, :] = high
    net[KVW : 2 * KVW, :] = low
    part[...] = three_products(nt, hid, high, low)


def prefix_states(idx, pieces):
    return call(
        states_body,
        (shaped((NET, HALF_HID), BF16), shaped((PRE, PHID)), shaped((PRE, PHID)), shaped((PRE, KVW))),
        [SCALARS] + [WHOLE] * 4,
        (pltpu.VMEM((HALF_HID, PHID), F32), pltpu.VMEM((KVW, HALF_HID), F32)),
        limit=12,
        name="prefix_states",
        moved=7000000,
    )(idx, *pieces)


AHEAD = 64


def pack_into(out, small, place, core, weight_in, weight_out, weight, bias, segments, valid):
    out[0:UNITS, :] = weight_in[pl.ds(pl.multiple_of(core * UNITS, UNITS), UNITS), :]
    own = [
        jnp.where(core == 0, weight_out[32 * d : 32 * d + UNITS, :], weight_out[32 * d + UNITS : 32 * d + 32, :])
        for d in range(16)
    ]
    turned = jnp.transpose(jnp.concatenate(own, axis=0))
    out[UNITS:OWN, 0:HALF_HID] = turned[0:COLS, :]
    out[UNITS:OWN, HALF_HID:PHID] = turned[COLS:128, :]
    whole = jnp.concatenate([weight[...], jnp.zeros((16 - PREFIX, 32), F32)], axis=0)
    small[...] = placed(whole, PHID, place * 32)
    flat = placed(jnp.broadcast_to(bias[...], (8, 160)), 5 * PHID, place * 160)
    for r in range(5):
        small[PREFIX + r : PREFIX + r + 1, :] = flat[0:1, r * PHID : (r + 1) * PHID]
    seg = segments[...]
    after = jnp.concatenate([seg[:, 1:], seg[:, :1]], axis=1)
    kept = (valid[...] > 0) & (lanes(seg.shape) < LENGTH - 1) & (after == seg)
    total = jnp.sum(kept.astype(F32), axis=1, keepdims=True)
    small[15:16, :] = jnp.where(lanes((1, PHID)) == place, total, 0.0)
    out[OWN:PACK, :] = small[...]


def rows_body(idx, tokens_at, table, *refs):
    away, (packed, own, other), refs = refs[:6], refs[6:9], refs[9:]
    taken, refs = refs[:6], refs[6:]
    small, block, held, tokens, found, locals_, sems = refs
    core = idx[3]
    first = (idx[2] * 2 + core) * SHARD
    fetch = pltpu.make_async_copy(tokens_at, tokens, sems.at[AHEAD])
    fetch.start()
    copies = [pltpu.make_async_copy(a, b, sems.at[AHEAD + 1 + k]) for k, (a, b) in enumerate(zip(away, taken))]
    for c in copies:
        c.start()
    held[...] = jnp.zeros_like(held)
    fetch.wait()

    def find(p, n):
        local = tokens[0, p] - first
        found[n] = p
        locals_[n] = local
        return n + ((local >= 0) & (local < SHARD)).astype(jnp.int32)

    number = lax.fori_loop(0, LENGTH, find, 0, unroll=16)
    for k in range(4):
        found[number + k] = LENGTH
        locals_[number + k] = 0
    number = (number + 3) // 4

    def copy(n):
        at = pl.multiple_of((locals_[n] // 16) * 16, 16)
        slot = lax.rem(n, AHEAD)
        return pltpu.make_async_copy(table.at[pl.ds(at, 16), :], block.at[slot], sems.at[slot])

    def begin(i, carry):
        for k in range(4):
            copy(4 * i + k).start()
        return carry

    def take(i, carry):
        for k in range(4):
            copy(4 * i + k).wait()
        lines = []
        for k in range(4):
            n = 4 * i + k
            got = block[lax.rem(n, AHEAD)].astype(F32)
            row = lax.rem(locals_[n], 16)
            lines.append(jnp.sum(jnp.where(rows((16, D)) == row, got, 0.0), axis=0, keepdims=True))
        for k in range(4):
            held[pl.ds(found[4 * i + k], 1), :] = lines[k]
        return carry

    for batch in range(LENGTH // AHEAD):
        low = jnp.minimum(number, batch * (AHEAD // 4))
        high = jnp.minimum(number, (batch + 1) * (AHEAD // 4))
        lax.fori_loop(low, high, begin, 0)
        if batch == 0:
            for c in copies:
                c.wait()
            pack_into(packed, small, idx[0] * 4 + idx[1], core, *taken)
        lax.fori_loop(low, high, take, 0)
    own[...] = held[pl.ds(pl.multiple_of(core * HALF, HALF), HALF), :].astype(BF16)
    other[...] = held[pl.ds(pl.multiple_of((1 - core) * HALF, HALF), HALF), :].astype(BF16)


def token_rows(idx, tokens, table, *network):
    return call(
        rows_body,
        (shaped((PACK, PHID)), shaped((HALF, D), BF16), shaped((HALF, D), BF16)),
        [SCALARS] + [REMAIN] * (2 + len(network)),
        (
            *(pltpu.VMEM(v.shape, v.dtype) for v in network),
            pltpu.VMEM((16, PHID), F32),
            pltpu.VMEM((AHEAD, 16, D), BF16),
            pltpu.VMEM((LENGTH + 8, D), F32),
            pltpu.SMEM((1, LENGTH), jnp.int32),
            pltpu.SMEM((LENGTH + 4,), jnp.int32),
            pltpu.SMEM((LENGTH + 4,), jnp.int32),
            pltpu.SemaphoreType.DMA((AHEAD + 1 + len(network),)),
        ),
        limit=10,
        name="token_rows_and_packed_weights",
        moved=9000000,
    )(idx, *(in_hbm(v) for v in (tokens, table, *network)))


def bring_body(*refs):
    half = len(refs) // 2
    sems = refs[-1]
    copies = [pltpu.make_async_copy(refs[k], refs[half + k], sems.at[k]) for k in range(half)]
    for c in copies:
        c.start()
    for c in copies:
        c.wait()


def bring(*inputs):
    return pl.pallas_call(
        bring_body,
        out_shape=tuple(pltpu.VMEM(v.shape, v.dtype) for v in inputs),
        in_specs=[REMAIN] * len(inputs),
        out_specs=tuple(REMAIN for _ in inputs),
        scratch_shapes=(pltpu.SemaphoreType.DMA((len(inputs),)),),
        compiler_params=pltpu.CompilerParams(vmem_limit_bytes=MIB),
        cost_estimate=pl.CostEstimate(flops=0, bytes_accessed=2 * sum(v.size * v.dtype.itemsize for v in inputs), transcendentals=0),
        name="bring_into_vmem",
    )(*(in_hbm(v) for v in inputs))


def qkv_body(idx, embedded, places, norms, bias, weight, x_out, query, keyval):
    core = idx[3]
    mine = embedded[...]
    x = mine.astype(F32) + places[pl.ds(pl.multiple_of(core * HALF, HALF), HALF), :].astype(F32)
    x_out[...] = x
    unit, _ = normalised(x)
    normed = (unit * norms[0, 0:1, :] + norms[0, 1:2, :]).astype(BF16)
    for j in range(6):
        at = slice(j * 512, (j + 1) * 512)
        part = nn(normed, weight[0, :, at]) + bias[:, at].astype(F32)
        if j < 2:
            query[:, at] = (part.astype(BF16).astype(F32) * SCALE).astype(BF16)
        else:
            keyval[0:HALF, (j - 2) * 512 : (j - 1) * 512] = part.astype(BF16)
    keyval[HALF : HALF + 16, 0:D] = mine[0:16, :]
    keyval[HALF : HALF + 16, D:KVW] = jnp.zeros((16, D), BF16)


def projections(idx, embedded, places, norms, bias, weight):
    return call(
        qkv_body,
        (shaped((HALF, D)), shaped((HALF, D), BF16), shaped((HALF + 16, KVW), BF16)),
        [SCALARS] + [WHOLE] * 5,
        limit=10,
        name="norm_and_projections",
        flops=2 * HALF * D * 3 * D,
        moved=9000000,
    )(idx, embedded, places, norms, bias, weight)


FCH = 1024


def by_heads(out, value, left):
    out[...] = jnp.zeros_like(out)
    zero = jnp.zeros((PRE, 128), BF16)
    for pair in range(HEADS // 2):
        at = slice(pair * 128, (pair + 1) * 128)
        out[2 * pair * PRE : (2 * pair + 1) * PRE, at] = jnp.where(left, value[:, at], zero)
        out[(2 * pair + 1) * PRE : (2 * pair + 2) * PRE, at] = jnp.where(left, zero, value[:, at])


def layer_body(
    idx, query, kv_own, kv_other, embedded, x_in, states_own, states_other, extra, segments, valid, norms, bias,
    w_out, w_fc, w_fc_out,
    final, attended_part, last_part, inner_part, mixed_part, query_part, target_part, stats_part, probs_part, value_rows,
    key_rows, mixed, keep, wide,
):
    xx, core = idx[2], idx[3]
    part = pl.ds(pl.multiple_of(xx * PART, PART), PART)
    shift = jnp.concatenate([extra[r : r + 1, :] for r in range(PREFIX + 1, PREFIX + 5)], axis=1)
    states = states_own[...] + states_other[...] + shift
    states = jnp.where(rows(states.shape) < PREFIX, states, 0.0).astype(BF16)
    left = lanes((PRE, 128)) < HEAD_DIM
    by_heads(key_rows, states[:, 0:D], left)
    by_heads(value_rows, states[:, D:KVW], left)

    seg = segments[...]
    mine = jnp.where(core == 0, seg[:, 0:HALF], seg[:, HALF:LENGTH])
    theirs = jnp.where(core == 0, seg[:, HALF:LENGTH], seg[:, 0:HALF])
    square = (HALF, HALF)
    mine_down = jnp.transpose(jnp.broadcast_to(mine, square))
    sees_own = (mine_down == jnp.broadcast_to(mine, square)) & (lanes(square) <= rows(square))
    sees_other = (mine_down == jnp.broadcast_to(theirs, square)) & (core == 1)
    hide = jnp.concatenate([jnp.where(m, 0.0, MASKED) for m in (sees_own, sees_other)], axis=1)
    hide = jnp.concatenate([hide, hide], axis=0)
    left = lanes(square) < HEAD_DIM
    ahead_scores = nt(query[...], key_rows[...])
    group = lanes(square) // PRE
    live = lanes(square) - group * PRE < PREFIX
    probs = [jnp.zeros(square, F32)] * 2
    for pair in range(HEADS // 2):
        at = slice(pair * 128, pair * 128 + 128)
        at_v = slice(D + pair * 128, D + pair * 128 + 128)
        q = query[:, at]
        zero = jnp.zeros_like(q)
        both = jnp.concatenate([jnp.where(left, q, zero), jnp.where(left, zero, q)], axis=0)
        keys = jnp.concatenate([kv_own[0:HALF, at], kv_other[0:HALF, at]], axis=0)
        values = jnp.concatenate([kv_own[0:HALF, at_v], kv_other[0:HALF, at_v]], axis=0)
        scores = nt(both, keys) + hide
        block = pair // 4
        mine = [live & (group == 2 * (pair % 4) + side) for side in range(2)]
        prefix = ahead_scores[:, block * 128 : (block + 1) * 128]
        prefix = jnp.concatenate([jnp.where(m, prefix, MASKED) for m in mine], axis=0)
        top = jnp.maximum(jnp.maximum(scores[:, 0:HALF], scores[:, HALF:LENGTH]), prefix)
        top = jnp.max(top, axis=1, keepdims=True)
        expo = jnp.exp(scores - top)
        expo_prefix = jnp.exp(prefix - top)
        total = jnp.sum(expo[:, 0:HALF] + expo[:, HALF:LENGTH] + expo_prefix, axis=1, keepdims=True)
        share = 1.0 / total
        out = nn((expo * share).astype(BF16), values)
        mixed[:, at] = jnp.where(left, out[0:HALF], out[HALF:])
        expo_prefix = expo_prefix * share
        probs[block] = probs[block] + (expo_prefix[0:HALF] + expo_prefix[HALF:])
    probs = jnp.concatenate(probs, axis=1)
    mixed[...] = mixed[...] + nn(probs.astype(BF16), value_rows[...])
    mixed_part[...] = mixed[part, :]
    query_part[...] = query[part, :]
    wide[:, 0 : HEADS * PRE] = probs
    probs_part[...] = wide[part, 0 : HEADS * PRE]

    x = x_in[...] + nn(mixed[...].astype(BF16), w_out[0]) + bias[:, 3 * D : 4 * D].astype(F32)
    keep[...] = x
    attended_part[...] = keep[part, :]
    unit, _ = normalised(x)
    normed = (unit * norms[1, 0:1, :] + norms[1, 1:2, :]).astype(BF16)
    x = x + bias[:, 4 * D + FF : 5 * D + FF].astype(F32)
    for j in range(4):
        inner = nn(normed, w_fc[0, :, j * FCH : (j + 1) * FCH]) + bias[:, 4 * D + j * FCH : 4 * D + (j + 1) * FCH].astype(F32)
        wide[...] = inner
        inner_part[:, j * FCH : (j + 1) * FCH] = wide[part, :]
        active = (0.5 * inner * (1.0 + jnp.tanh(GELU_K * (inner + GELU_C * inner * inner * inner)))).astype(BF16)
        x = x + nn(active, w_fc_out[0, j * FCH : (j + 1) * FCH, :])
    keep[...] = x
    last_part[...] = keep[part, :]
    unit, _ = normalised(x)
    result = (unit * norms[2, 0:1, :] + norms[2, 1:2, :]).astype(BF16)
    final[...] = result

    wide[...] = embedded[...].astype(F32)
    keep[...] = result.astype(F32)
    after = jnp.concatenate([wide[1:HALF, :], kv_other[HALF : HALF + 1, 0:D].astype(F32)], axis=0)
    wide[...] = after
    target = wide[part, :]
    target_part[...] = target
    picked = jnp.sum(keep[part, :] * target, axis=1, keepdims=True)
    following = jnp.concatenate([seg[:, 1:], seg[:, :1]], axis=1)
    kept = (valid[...] > 0) & (lanes(seg.shape) < LENGTH - 1) & (following == seg)
    kept = kept.astype(F32)
    counted = jnp.where(core == 0, kept[:, 0:HALF], kept[:, HALF:LENGTH])
    wide[:, 0:HALF] = jnp.transpose(jnp.broadcast_to(counted, square))
    lane = lanes((PART, 128))
    stats_part[...] = jnp.where(lane == 0, picked, jnp.where(lane == 1, wide[part, 0:128], 0.0))


def layer(idx, *inputs):
    return call(
        layer_body,
        (
            shaped((HALF, D), BF16),
            shaped((PART, D)),
            shaped((PART, D)),
            shaped((PART, FF)),
            shaped((PART, D)),
            shaped((PART, D), BF16),
            shaped((PART, D)),
            shaped((PART, 128)),
            shaped((PART, HEADS * PRE)),
            shaped((HEADS * PRE, D), BF16),
        ),
        [SCALARS] + [WHOLE] * len(inputs),
        (
            pltpu.VMEM((HEADS * PRE, D), BF16),
            pltpu.VMEM((HALF, D), F32),
            pltpu.VMEM((HALF, D), F32),
            pltpu.VMEM((HALF, FCH), F32),
        ),
        limit=10,
        name="attention_and_feed_forward",
        flops=2 * HALF * D * 9 * D,
        moved=22000000,
    )(idx, *inputs)


VCH = 1280


def vocab_body(f_own, f_other, table, own, other, final, grad):
    final[0:HALF, :] = f_own[...]
    final[HALF:LENGTH, :] = f_other[...]
    chunks = SHARD // VCH
    logits = nt(final[...], table[0:VCH, :])
    for j in range(chunks):
        if j + 1 < chunks:
            following = nt(final[...], table[(j + 1) * VCH : (j + 2) * VCH, :])
        now = jnp.max(logits, axis=1, keepdims=True)
        if j:
            now = jnp.maximum(top, now)
            shrink = jnp.exp(top - now)
        expo = jnp.exp(logits - now)
        part = jnp.sum(expo, axis=1, keepdims=True)
        total = total * shrink + part if j else part
        part = nn(expo.astype(BF16), table[j * VCH : (j + 1) * VCH, :])
        grad[...] = grad[...] * shrink + part if j else part
        top, logits = now, following
    mean = grad[...] * (1.0 / total)
    log_sum = top + jnp.log(total)
    for out, at in ((own, slice(0, HALF)), (other, slice(HALF, LENGTH))):
        body, tail = with_stat(mean[at, :], log_sum[at, :])
        out[:, 0:D] = body
        out[:, D:EXT] = tail


def vocabulary(f_own, f_other, table):
    return call(
        vocab_body,
        (shaped((HALF, EXT), BF16),) * 2,
        [WHOLE] * 3,
        (pltpu.VMEM((LENGTH, D), BF16), pltpu.VMEM((LENGTH, D), F32)),
        limit=16,
        name="logits_and_gradient",
        flops=4 * LENGTH * D * SHARD,
        moved=SHARD * D * 2,
    )(f_own, f_other, table)


def merged(refs):
    stats = [stat_of(r) for r in refs]
    top = stats[0]
    for s in stats[1:]:
        top = jnp.maximum(top, s)
    weights = [jnp.exp(s - top) for s in stats]
    total = sum(weights[1:], weights[0])
    mean = sum((w * r[:, 0:D].astype(F32) for w, r in zip(weights[1:], refs[1:])), weights[0] * refs[0][:, 0:D].astype(F32))
    return mean * (1.0 / total), top + jnp.log(total)


def merge_body(idx, own, other, o0, o1, o2, o3, held):
    mean, log_total = merged((own, other))
    body, tail = with_stat(mean, log_total)
    held[:, 0:D] = body
    held[:, D:EXT] = tail
    for k, out in enumerate((o0, o1, o2, o3)):
        out[...] = held[pl.ds(pl.multiple_of(lax.rem(idx[2] + k, 4) * PART, PART), PART), :]


def merge(idx, own, other):
    return call(
        merge_body,
        (shaped((PART, EXT), BF16),) * 4,
        [SCALARS] + [WHOLE] * 2,
        (pltpu.VMEM((HALF, EXT), BF16),),
        limit=8,
        name="merge_two_cores",
        moved=900000,
    )(idx, own, other)


def finely(left, right):
    size = left.shape[0]
    both = nt(jnp.concatenate(two_way(left), axis=0), right)
    return both[0:size] + both[size : 2 * size]


def backward_body(
    idx, extra, p0, p1, p2, p3, attended, last, inner, mixed, query, target, stats, probs_in, value_rows, norms, w_out, w_fc, w_fc_out,
    own, other, result, ones_rows,
):
    mean, log_total = merged((p0, p1, p2, p3))
    counted = stats[:, 1:2]
    loss = jnp.sum((log_total - stats[:, 0:1]) * counted, axis=0, keepdims=True)
    scale = counted * (1.0 / jnp.sum(extra[15:16, :], axis=1, keepdims=True))
    exact = (jnp.exp(stats[:, 0:1] - log_total) - 1.0) * scale
    grad = mean * scale - target[...] * (scale + exact - exact.astype(BF16).astype(F32))
    grad_x = norm_back(last[...], norms[2, 0:1, :], grad)
    grad_normed = jnp.zeros((PART, D), F32)
    for j in range(4):
        u = inner[:, j * FCH : (j + 1) * FCH]
        bend = jnp.tanh(GELU_K * (u + GELU_C * u * u * u))
        slope = 0.5 * (1.0 + bend) + 0.5 * u * (1.0 - bend * bend) * (GELU_K * (1.0 + 3.0 * GELU_C * u * u))
        grad_u = finely(grad_x, w_fc_out[0, j * FCH : (j + 1) * FCH, :]) * slope
        grad_normed = grad_normed + finely(grad_u, w_fc[0, :, j * FCH : (j + 1) * FCH])
    grad_h = grad_x + norm_back(attended[...], norms[1, 0:1, :], grad_normed)
    grad_mixed = finely(grad_h, w_out[0])

    left = lanes((PRE, 128)) < HEAD_DIM
    by_heads(ones_rows, jnp.ones((PRE, D), BF16), left)
    q = query[...]
    probs = probs_in[...]
    grad_probs = finely(grad_mixed, value_rows[...])
    inner_sum = finely(grad_mixed * mixed[...], ones_rows[...])
    grad_scores = jnp.concatenate(two_way(probs * (grad_probs - inner_sum)), axis=0)
    grad_keys = tn(grad_scores, jnp.concatenate([q, q], axis=0))
    probs = probs.astype(BF16)
    grad_values = tn(jnp.concatenate([probs, probs], axis=0), jnp.concatenate(two_way(grad_mixed), axis=0))
    for side, value in enumerate((grad_keys, grad_values)):
        parts = []
        for pair in range(HEADS // 2):
            at = slice(pair * 128, (pair + 1) * 128)
            up = value[2 * pair * PRE : (2 * pair + 1) * PRE, at]
            parts.append(jnp.where(left, up, value[(2 * pair + 1) * PRE : (2 * pair + 2) * PRE, at]))
        folded = jnp.concatenate(parts, axis=1)
        result[:, side * D : (side + 1) * D] = folded[0:8, :]
        for r in range(2):
            for k in range(2):
                result[4 * r + 2 * side + k : 4 * r + 2 * side + k + 1, KVW : KVW + 512] = folded[
                    8 + r : 9 + r, k * 512 : (k + 1) * 512
                ]
    lane = lanes((8, 256))
    result[:, KVW + 512 : FLAT] = jnp.where((lane == 0) & (rows((8, 256)) == 0), loss, 0.0)
    left, right = result[:, 0:SIDE], result[:, SIDE:FLAT]
    own[...] = jnp.where(idx[3] == 0, left, right)
    other[...] = jnp.where(idx[3] == 0, right, left)


def backward(idx, *inputs):
    return call(
        backward_body,
        (shaped((8, SIDE)), shaped((8, SIDE))),
        [SCALARS] + [WHOLE] * len(inputs),
        (pltpu.VMEM((8, FLAT), F32), pltpu.VMEM((HEADS * PRE, D), BF16)),
        limit=10,
        name="backward_to_prefix",
        flops=2 * PART * D * 9 * D,
        moved=20000000,
    )(idx, *inputs)


def send_body(idx, a, b, c, d, out):
    total = (a[...] + c[...]) + (b[...] + d[...])
    tail = total[:, SIDE - 256 : SIDE]
    high, middle, low = three_way(tail[:, 0:1])
    lane = lanes((8, 256))
    pieces = jnp.where(lane == 0, high, jnp.where(lane == 1, middle, jnp.where(lane == 2, low, 0.0)))
    tail = jnp.where(idx[3] == 1, pieces, tail)
    total = jnp.concatenate([total[:, 0 : SIDE - 256], tail], axis=1).astype(BF16)
    out[...] = jnp.broadcast_to(total[None], out.shape)


def copies_to_send(idx, pieces):
    return call(
        send_body,
        shaped((16, 8, SIDE), BF16),
        [SCALARS] + [WHOLE] * 4,
        limit=8,
        name="sum_to_send",
        moved=600000,
    )(idx, *pieces)


def adam(weight, grad, first, second):
    first = BETA_ONE * first + (1.0 - BETA_ONE) * grad
    second = BETA_TWO * second + (1.0 - BETA_TWO) * grad * grad
    move = first / (1.0 - BETA_ONE**STEP) / (jnp.sqrt(second / (1.0 - BETA_TWO**STEP)) + ADAM_EPS)
    return weight - RATE * (move + DECAY * weight), first, second


def total_of(value):
    return jnp.sum(jnp.sum(value, axis=1, keepdims=True), axis=0, keepdims=True)


def received_body(pieces, out):
    total = pieces[0].astype(F32)
    for k in range(1, 16):
        total = total + pieces[k].astype(F32)
    out[...] = total


def received(pieces):
    return call(received_body, shaped((8, SIDE)), [WHOLE], limit=8, name="sum_received", moved=400000)(pieces)


def update_body(idx, side_own, side_other, net_own, net_other, prefix, extra, *refs):
    away, refs = refs[:12], refs[12:]
    (loss, count, norm), outs, refs = refs[:3], refs[3:15], refs[15:]
    held, (columns, sems) = refs[:12], refs[12:]
    copies = [pltpu.make_async_copy(a, b, sems.at[k]) for k, (a, b) in enumerate(zip(away, held))]
    for c in copies:
        c.start()
    place = idx[0] * 4 + idx[1]
    core = idx[3]

    def in_order(mine, theirs):
        return jnp.where(core == 0, mine, theirs), jnp.where(core == 0, theirs, mine)

    flat = jnp.concatenate(in_order(side_own[...], side_other[...]), axis=1)
    loss[...] = jnp.sum(flat[0:1, KVW + 512 : FLAT], axis=1, keepdims=True)
    last = flat[:, KVW : KVW + 512]
    ends = [jnp.concatenate([last[4 * r + k : 4 * r + k + 1, :] for k in range(4)], axis=1) for r in range(2)]
    states = jnp.concatenate([flat[:, 0:KVW], *ends, jnp.zeros((6, KVW), F32)], axis=0)
    columns[...] = states
    pre_weight = prefix[...]

    def back(net):
        hid = net[NET_HID : NET_HID + PRE, :].astype(F32) + net[NET_HID + PRE : NET, :].astype(F32)
        grad = three_products(nn, states, net[0:KVW, :], net[KVW : 2 * KVW, :]) * (1.0 - hid * hid)
        sides = []
        for side in range(2):
            at = NET_IN + side * HALF_HID
            sides.append(
                three_products(nn, grad, net[at : at + HALF_HID, :], net[at + 2 * HALF_HID : at + 3 * HALF_HID, :])
            )
        return hid, grad, jnp.concatenate(sides, axis=1)

    hid_own, grad_own, first = back(net_own)
    hid_other, grad_other, second = back(net_other)
    grad_prefix = first + second
    grad_pre = jnp.concatenate(in_order(grad_own, grad_other), axis=1)
    hid = jnp.concatenate(in_order(hid_own, hid_other), axis=1)
    biases = jnp.sum(grad_pre, axis=0, keepdims=True)
    biases = jnp.concatenate(
        [by_units(biases[:, 0:HALF_HID], biases[:, HALF_HID:PHID]), jnp.sum(states, axis=0, keepdims=True)], axis=1
    )
    squares = (
        total_of(grad_prefix * grad_prefix)
        + total_of(gram(pre_weight) * gram(grad_pre))
        + total_of(gram(hid) * gram(states))
        + total_of(biases * biases)
    )
    size = jnp.sqrt(squares)
    factor = jnp.minimum(1.0, CLIP / (size + 1e-06))
    count[...] = jnp.sum(extra[15:16, :], axis=1, keepdims=True)
    norm[...] = size

    own = pltpu.roll(grad_prefix, lax.rem(PHID - place * 32, PHID), 1)[0:PREFIX, 0:32]
    back_by = lax.rem(HALF_HID - place * UNITS, HALF_HID)
    sides = [pltpu.roll(grad_pre[:, at : at + HALF_HID], back_by, 1)[:, 0:UNITS] for at in (0, HALF_HID)]
    grad_in = outer(jnp.concatenate(sides, axis=1), pre_weight)
    grad_out = outer(hid, columns[:, pl.ds(pl.multiple_of(place * 128, 128), 128)])
    parts = []
    for d in range(16):
        parts += [grad_out[at + d * UNITS : at + (d + 1) * UNITS, :] for at in (0, HALF_HID)]
    grad_out = jnp.concatenate(parts, axis=0)
    turned = jnp.broadcast_to(biases, (8, 5 * PHID))
    turned = pltpu.roll(turned, lax.rem(5 * PHID - place * 160, 5 * PHID), 1)[0:1, 0:160]
    for c in copies:
        c.wait()
    for k, grad in enumerate((own, grad_in, grad_out, turned)):
        new = adam(held[k][...], grad * factor, held[4 + k][...], held[8 + k][...])
        for j in range(3):
            outs[4 * j + k][...] = new[j]


def update(idx, network, weights, firsts, seconds):
    sizes = [shaped(w.shape) for w in weights]
    one = shaped((1, 1))
    away = (*weights, *firsts, *seconds)
    return call(
        update_body,
        (one, one, one, *sizes, *sizes, *sizes),
        [SCALARS] + [WHOLE] * len(network) + [REMAIN] * 12,
        (*(pltpu.VMEM(w.shape, F32) for w in away), pltpu.VMEM((PRE, KVW), F32), pltpu.SemaphoreType.DMA((12,))),
        limit=16,
        name="clip_and_update",
        moved=6000000,
    )(idx, *network, *(in_hbm(w) for w in away))


def from_behind(value, axis, k):
    return lax.ppermute(value, axis, [(i, (i + k) % 4) for i in range(4)])


def around(value, axis):
    return (value, *(from_behind(value, axis, k) for k in (1, 2, 3)))


def scattered(values, axis):
    return (values[0], *(from_behind(values[k], axis, k) for k in (1, 2, 3)))


def ahead(value, k, late):
    pairs = []
    for z in range(4):
        for y in range(4):
            for core in range(2):
                to = (z, (y + k) % 4) if (core == 0) != late else ((z + k) % 4, y)
                pairs.append(((z * 4 + y) * 2 + core, (to[0] * 4 + to[1]) * 2 + core))
    return lax.ppermute(value, ("z", "y", "core"), pairs)


def after(value, *others):
    return lax.optimization_barrier((value, *others))[0]


def met_on_x(value, late):
    pairs = [(2 * i + core, 2 * (i ^ (3 if core ^ late else 1)) + core) for i in range(4) for core in range(2)]
    return lax.ppermute(value, ("x", "core"), pairs)


def swapped(value):
    return lax.ppermute(value, "core", [(0, 1), (1, 0)])


def on_device(
    tokens,
    segments,
    valid,
    embedding,
    positions_table,
    w_qkv,
    w_attn_out,
    w_fc,
    w_fc_out,
    layer_bias,
    norm_params,
    prefix,
    prefix_in,
    prefix_out,
    prefix_bias,
    moment_prefix,
    moment_in,
    moment_out,
    moment_bias,
    square_prefix,
    square_in,
    square_out,
    square_bias,
):
    idx = jnp.stack([lax.axis_index(a) for a in ("z", "y", "x", "core")]).astype(jnp.int32)
    bias_row = prefix_bias.reshape(1, -1)

    packed, own, other = token_rows(
        idx, tokens, embedding, prefix_in.T, prefix_out, prefix, bias_row, segments, valid
    )
    packed = packed.astype(jnp.float16)
    pieces = [packed, *(ahead(packed, k, False) for k in (1, 2, 3))]
    embedded = own + swapped(other)
    first = embedded + met_on_x(embedded, 0)
    stacked = stack([after(p, embedded) for p in pieces])
    packed = [stacked, *(ahead(stacked, k, True) for k in (1, 2, 3))]
    embedded = first + met_on_x(first, 1)
    x, query, keyval = projections(idx, embedded, *bring(positions_table, norm_params, layer_bias, w_qkv))
    keyval, packed = lax.optimization_barrier((keyval, packed))
    packed = [p.astype(F32) for p in packed]
    net, prefix_all, extra, states = prefix_states(idx, packed)
    final, *kept = layer(
        idx, query, keyval, swapped(keyval), embedded, x, states, swapped(states), extra, segments, valid,
        norm_params, layer_bias, w_attn_out, w_fc, w_fc_out,
    )
    final_other, net = lax.optimization_barrier((swapped(final), net))
    own, other = vocabulary(final, final_other, embedding)
    own, net_other = lax.optimization_barrier((own, swapped(net)))
    pieces = scattered(merge(idx, own, swapped(other)), "x")
    own, other = backward(idx, extra, *pieces, *kept, norm_params, w_attn_out, w_fc, w_fc_out)
    grad = copies_to_send(idx, around(own + swapped(other), "x"))
    grad = lax.all_to_all(grad, ("z", "y"), 0, 0, tiled=True)
    grad = received(grad)
    outs = update(
        idx, (grad, swapped(grad), net, net_other, prefix_all, extra),
        (prefix, prefix_in.T, prefix_out, bias_row),
        (moment_prefix, moment_in.T, moment_out, moment_bias.reshape(1, -1)),
        (square_prefix, square_in.T, square_out, square_bias.reshape(1, -1)),
    )
    outs = list(outs)
    for k in range(3):
        outs[k] = outs[k].reshape(())
        outs[4 + 4 * k] = outs[4 + 4 * k].T
        outs[6 + 4 * k] = outs[6 + 4 * k].reshape(-1)
    return tuple(outs)


def solution(mesh):
    split = Mesh(mesh.devices.reshape(4, 4, 4, 2), ("z", "y", "x", "core"))
    dp = ("z", "y")
    sharded = (P(None, dp), P(None, dp), P(None, dp), P(dp))
    placed = (
        P(dp, None),
        P(dp, None),
        P(dp, None),
        P(("x", "core"), None),
        *([P()] * 7),
        *sharded,
        *sharded,
        *sharded,
    )
    return jax.shard_map(
        on_device,
        mesh=split,
        in_specs=placed,
        out_specs=(P(), P(), P(), *sharded, *sharded, *sharded),
        check_vma=False,
    )
```
